128 devices in a mesh: seq: 32 (over y, z_lo, x), ffn: 4 (over z_hi, core).
Axes of the slice: x: 4, y: 4, z: 4 (z_hi: 2, z_lo: 2; z = z_hi * 2 + z_lo), core: 2. Of those that a mesh axis runs over, the one named last changes fastest.
Arguments:
- tokens: bfloat16 [8192, 1024], P('seq'), may hold values from -6 to 6
- segment_kind: int32 [8192], P('seq'), may hold values from 0 to 2
- document: int32 [8192], replicated, may hold values from 0 to 3, as said below
- type_table: bfloat16 [3, 1024], replicated, may hold values from -3 to 3
- attend_gain: bfloat16 [1024], replicated, may hold values from 0.25 to 1.75
- attend_bias: bfloat16 [1024], replicated, may hold values from -1.75 to 1.75
- input_weight: bfloat16 [3, 1024, 1024], P(None, None, 'ffn')
- input_bias: bfloat16 [3, 1024], P(None, 'ffn'), may hold values from -1.75 to 1.75
- inner_gain: bfloat16 [1024], P('ffn'), may hold values from 0.25 to 1.75
- inner_bias: bfloat16 [1024], P('ffn'), may hold values from -1.75 to 1.75
- output_weight: bfloat16 [1024, 1024], P('ffn'), may hold values from -0.1875 to 0.1875
- output_bias: bfloat16 [1024], replicated, may hold values from -1.75 to 1.75
- feed_gain: bfloat16 [1024], replicated, may hold values from 0.25 to 1.75
- feed_bias: bfloat16 [1024], replicated, may hold values from -1.75 to 1.75
- up_weight: bfloat16 [1024, 4096], P(None, 'ffn')
- up_bias: bfloat16 [4096], P('ffn'), may hold values from -1.75 to 1.75
- hidden_gain: bfloat16 [4096], P('ffn'), may hold values from 0.25 to 1.75
- hidden_bias: bfloat16 [4096], P('ffn'), may hold values from -1.75 to 1.75
- down_weight: bfloat16 [4096, 1024], P('ffn'), may hold values from -0.09375 to 0.09375
- down_bias: bfloat16 [1024], replicated, may hold values from -1.75 to 1.75
- cotangent: bfloat16 [8192, 1024], P('seq'), may hold values from -6 to 6
Outputs:
- result: bfloat16 [8192, 1024], P('seq')
- grad_tokens: float32 [8192, 1024], P('seq')
- grad_type_table: float32 [3, 1024], replicated
- grad_attend_gain: float32 [1024], replicated
- grad_attend_bias: float32 [1024], replicated
- grad_input_weight: float32 [3, 1024, 1024], P(None, None, 'ffn')
- grad_input_bias: float32 [3, 1024], P(None, 'ffn')
- grad_inner_gain: float32 [1024], P('ffn')
- grad_inner_bias: float32 [1024], P('ffn')
- grad_output_weight: float32 [1024, 1024], P('ffn')
- grad_output_bias: float32 [1024], replicated
- grad_feed_gain: float32 [1024], replicated
- grad_feed_bias: float32 [1024], replicated
- grad_up_weight: float32 [1024, 4096], P(None, 'ffn')
- grad_up_bias: float32 [4096], P('ffn')
- grad_hidden_gain: float32 [4096], P('ffn')
- grad_hidden_bias: float32 [4096], P('ffn')
- grad_down_weight: float32 [4096, 1024], P('ffn')
- grad_down_bias: float32 [1024], replicated
The draws below stay inside these ranges and needn't reach their ends.
Inputs may be any that keep to these rules, and one draw needn't show every extreme that they name: `document`: document numbers start at 0 and rise by 0 or 1 from one token to the next.
All inputs are finite; a program needn't handle non-finite values.
Results may differ from the reference program's by a relative error of at most 0.0095.
Values may be sent and summed in bfloat16 or wider, within the bound.
No kernel may reach another device: no remote copies, remote signals or barrier semaphores. Data moves between devices by JAX's collectives and lax.ppermute only.
A program may use at most 128 MiB of HBM per device.

```python
import jax
import jax.numpy as jnp
from jax import lax

D = 1024
HEADS = 16
FF = 4096
TOK_DEV = 256
TOKENS = 8192


def draw_document(key, part):
    key = jax.random.fold_in(key, 11)
    first_key, second_key, third_key = jax.random.split(key, 3)
    start_long = jax.random.randint(first_key, (), 1, TOK_DEV // 2 + 1)
    tail_rows = jax.random.randint(second_key, (), 2, TOK_DEV // 2 + 2)
    end_long = TOKENS - tail_rows
    last_cut = end_long + jax.random.randint(third_key, (), 1, tail_rows)
    positions = jnp.arange(TOKENS, dtype=jnp.int32)
    return (positions >= start_long).astype(jnp.int32) + (positions >= end_long).astype(jnp.int32) + (positions >= last_cut).astype(jnp.int32)


def draw_input_weight(key, part):
    key = jax.random.fold_in(key, 5)
    column = jnp.arange(D, dtype=jnp.float32) / D
    column_scale = 0.55 * 3.0 ** column
    random_part = jax.random.normal(key, (3, D, D), jnp.float32)
    factor = jnp.stack([jnp.ones_like(column), jnp.ones_like(column), column_scale])
    return (random_part * factor[:, None, :] * D ** (-0.5)).astype(jnp.bfloat16)


def draw_up_weight(key, part):
    key = jax.random.fold_in(key, 7)
    column = jnp.arange(FF, dtype=jnp.float32) / FF
    column_scale = 0.55 * 3.0 ** column
    random_part = jax.random.normal(key, (D, FF), jnp.float32)
    return (random_part * column_scale[None, :] * D ** (-0.5)).astype(jnp.bfloat16)


def touch_ends(array, own_key, smallest, largest):
    longest = array.shape.index(max(array.shape))
    spots = []
    for shift in (0, 1):
        where = [jax.random.randint(jax.random.fold_in(own_key, axis), (), 0, length) for axis, length in enumerate(array.shape)]
        where[longest] = (where[longest] + shift) % array.shape[longest]
        spots.append(tuple(where))
    return array.at[spots[0]].set(smallest).at[spots[1]].set(largest)


def block_scale(own_key, shape, cuts, least, largest):
    def one(axis_at, blocks):
        draws = jax.random.uniform(jax.random.fold_in(jax.random.fold_in(own_key, 6), axis_at), (blocks,), jnp.float32, least / len(cuts), largest / len(cuts))
        return jnp.repeat(jnp.exp(draws), shape[axis_at] // blocks).reshape((-1,) + (1,) * (len(shape) - axis_at - 1))

    gain = one(*cuts[0])
    for cut in cuts[1:]:
        gain = gain * one(*cut)
    return gain


def scatter_about(own_key, shape, scale, bound, shards=(), kind=jnp.bfloat16):
    entries = scale * jax.random.normal(own_key, shape, jnp.float32)
    if shards:
        entries = entries * block_scale(own_key, shape, shards, -0.22, 0.18)
    return jnp.clip(entries, -bound, bound).astype(kind)


def setup_inputs(seed: int = 0) -> dict:
    key_of = jax.random.split(jax.random.key(seed), 22)
    tokens = scatter_about(key_of[0], (TOKENS, D), 1.0, 6.0, ((0, 32),))
    segment_kind = touch_ends(jax.random.randint(key_of[1], (TOKENS,), 0, 3), jax.random.fold_in(key_of[1], 1), 0, 2).astype(jnp.int32)
    document = draw_document(jax.random.fold_in(key_of[21], 71), 0)
    type_table = scatter_about(key_of[3], (3, D), 0.5, 3.0)
    attend_gain = jnp.clip(1.0 + 0.15 * jax.random.normal(key_of[4], (D,), jnp.float32), 0.25, 1.75).astype(jnp.bfloat16)
    attend_bias = scatter_about(key_of[5], (D,), 0.3, 1.75)
    input_weight = draw_input_weight(jax.random.fold_in(key_of[21], 71), 0)
    input_bias = scatter_about(key_of[7], (3, D), 0.3, 1.75, ((1, 4),))
    inner_gain = jnp.clip(1.0 + 0.15 * jax.random.normal(key_of[8], (D,), jnp.float32), 0.25, 1.75).astype(jnp.bfloat16)
    inner_bias = scatter_about(key_of[9], (D,), 0.3, 1.75, ((0, 4),))
    output_weight = scatter_about(key_of[10], (D, D), D ** -0.5, 0.1875, ((0, 4),))
    output_bias = scatter_about(key_of[11], (D,), 0.3, 1.75)
    feed_gain = jnp.clip(1.0 + 0.15 * jax.random.normal(key_of[12], (D,), jnp.float32), 0.25, 1.75).astype(jnp.bfloat16)
    feed_bias = scatter_about(key_of[13], (D,), 0.3, 1.75)
    up_weight = draw_up_weight(jax.random.fold_in(key_of[21], 71), 0)
    up_bias = scatter_about(key_of[15], (FF,), 0.3, 1.75, ((0, 4),))
    hidden_gain = jnp.clip(1.0 + 0.15 * jax.random.normal(key_of[16], (FF,), jnp.float32), 0.25, 1.75).astype(jnp.bfloat16)
    hidden_bias = scatter_about(key_of[17], (FF,), 0.3, 1.75, ((0, 4),))
    down_weight = scatter_about(key_of[18], (FF, D), FF ** -0.5, 0.09375, ((0, 4),))
    down_bias = scatter_about(key_of[19], (D,), 0.3, 1.75)
    cotangent = scatter_about(key_of[20], (TOKENS, D), 1.0, 6.0, ((0, 32),))
    return {"tokens": tokens, "segment_kind": segment_kind, "document": document, "type_table": type_table, "attend_gain": attend_gain, "attend_bias": attend_bias, "input_weight": input_weight, "input_bias": input_bias, "inner_gain": inner_gain, "inner_bias": inner_bias, "output_weight": output_weight, "output_bias": output_bias, "feed_gain": feed_gain, "feed_bias": feed_bias, "up_weight": up_weight, "up_bias": up_bias, "hidden_gain": hidden_gain, "hidden_bias": hidden_bias, "down_weight": down_weight, "down_bias": down_bias, "cotangent": cotangent}


epsilon = 1e-05
scale_base = 512.0
masked_score = -1e+30
highest = lax.Precision.HIGHEST

@jax.custom_vjp
def low(v):
    return lax.optimization_barrier(v.astype(jnp.bfloat16)).astype(jnp.float32)

@jax.custom_vjp
def low_back(v):
    return v

def low_keep(v):
    return (low(v), None)

def low_pass(kept, grad):
    return (grad,)

def back_keep(v):
    return (v, None)

def back_low(kept, grad):
    return (low(grad),)
low.defvjp(low_keep, low_pass)
low_back.defvjp(back_keep, back_low)

def layer_norm(values, gain_vec, offset_vec):
    center = values - lax.optimization_barrier(jnp.mean(values, axis=-1, keepdims=True))
    spread = lax.optimization_barrier(jnp.mean(center * center, axis=-1, keepdims=True))
    return center * lax.rsqrt(spread + epsilon) * gain_vec + offset_vec

def xpos_tables(positions, head_width, total_rows):
    half_width = head_width // 2
    pair_index = jnp.arange(half_width, dtype=jnp.float32)
    frequency = 1.0 / 10000.0 ** (pair_index / half_width)
    angles = positions.astype(jnp.float32)[:, None] * frequency[None, :]
    ratios = (2.0 * pair_index + 0.4 * head_width) / (1.4 * head_width)
    exponent = (positions - total_rows // 2).astype(jnp.float32)[:, None] / scale_base
    growth = ratios[None, :] ** exponent
    return (jnp.cos(angles)[:, None, :], jnp.sin(angles)[:, None, :], growth[:, None, :])

def rotate(vectors, cosine, sine_table, factor):
    half_width = vectors.shape[-1] // 2
    first_half = vectors[..., :half_width]
    second_half = vectors[..., half_width:]
    return jnp.concatenate([(first_half * cosine - second_half * sine_table) * factor, (second_half * cosine + first_half * sine_table) * factor], axis=-1)

def attend(queries, keys_rot, values_low, document):
    total_rows = queries.shape[0]
    block_rows = min(512, total_rows)
    block_count = total_rows // block_rows
    positions = jnp.arange(total_rows, dtype=jnp.int32)
    score_scale = queries.shape[-1] ** (-0.5)

    def one_block(pieces):
        query_block, query_pos, query_doc = pieces
        scores = jnp.einsum('qhd,khd->hqk', query_block, keys_rot, precision=highest) * score_scale
        scores = low_back(scores)
        allowed = (query_doc[:, None] == document[None, :]) & (positions[None, :] <= query_pos[:, None])
        scores = jnp.where(allowed[None], scores, masked_score)
        soft_weights = low(jax.nn.softmax(scores, axis=-1))
        return jnp.einsum('hqk,khd->qhd', soft_weights, values_low, precision=highest)
    blocks = (queries.reshape((block_count, block_rows) + queries.shape[1:]), positions.reshape(block_count, block_rows), document.reshape(block_count, block_rows))
    mixed = lax.map(jax.checkpoint(one_block), blocks)
    return mixed.reshape(queries.shape)

def reference(tokens, segment_kind, document, type_table, attend_gain, attend_bias, input_weight, input_bias, inner_gain, inner_bias, output_weight, output_bias, feed_gain, feed_bias, up_weight, up_bias, hidden_gain, hidden_bias, down_weight, down_bias, cotangent):
    total_rows = tokens.shape[0]
    head_width = D // HEADS

    def forward(tokens_f, table_f, attend_gain_f, attend_bias_f, input_weight_f, input_bias_f, inner_gain_f, inner_bias_f, output_weight_f, output_bias_f, feed_gain_f, feed_bias_f, up_weight_f, up_bias_f, hidden_gain_f, hidden_bias_f, down_weight_f, down_bias_f):
        one_hot = (segment_kind[:, None] == jnp.arange(3, dtype=jnp.int32)[None, :]).astype(jnp.float32)
        stream = tokens_f + jnp.dot(one_hot, table_f, precision=highest)
        normed = low(layer_norm(stream, attend_gain_f, attend_bias_f))
        projected = low_back(jnp.einsum('td,sdf->tsf', normed, input_weight_f, precision=highest) + input_bias_f[None])
        positions = jnp.arange(total_rows, dtype=jnp.int32)
        cosine, sine_table, growth = xpos_tables(positions, head_width, total_rows)
        head_shape = (total_rows, HEADS, head_width)
        queries = low(rotate(projected[:, 0].reshape(head_shape), cosine, sine_table, growth))
        keys_rot = low(rotate(projected[:, 1].reshape(head_shape), cosine, sine_table, 1.0 / growth))
        values_low = low(projected[:, 2].reshape(head_shape))
        mixed = low_back(attend(queries, keys_rot, values_low, document).reshape(total_rows, D))
        inner = low(layer_norm(mixed, inner_gain_f, inner_bias_f))
        branch = low_back(jnp.dot(inner, output_weight_f, precision=highest) + output_bias_f)
        middle = stream + branch
        feed_in = low(layer_norm(middle, feed_gain_f, feed_bias_f))
        pre_act = low_back(jnp.dot(feed_in, up_weight_f, precision=highest) + up_bias_f)
        hidden = low(layer_norm(jax.nn.gelu(pre_act, approximate=False), hidden_gain_f, hidden_bias_f))
        feed_out = low_back(jnp.dot(hidden, down_weight_f, precision=highest) + down_bias_f)
        return middle + feed_out
    floats = tuple((array_item.astype(jnp.float32) for array_item in (tokens, type_table, attend_gain, attend_bias, input_weight, input_bias, inner_gain, inner_bias, output_weight, output_bias, feed_gain, feed_bias, up_weight, up_bias, hidden_gain, hidden_bias, down_weight, down_bias)))
    result, pullback = jax.vjp(forward, *floats)
    grads = pullback(cotangent.astype(jnp.float32))
    return (result.astype(jnp.bfloat16), grads[0], grads[1], grads[2], grads[3], grads[4], grads[5], grads[6], grads[7], grads[8], grads[9], grads[10], grads[11], grads[12], grads[13], grads[14], grads[15], grads[16], grads[17])
```

```python
from functools import partial
import math

import jax
import jax.numpy as jnp
from jax import lax
from jax.experimental import pallas as pl
from jax.experimental.pallas import tpu as pltpu
from jax.sharding import PartitionSpec as P

D = 1024
FF = 4096
HEAD_DIM = 64
ROW = 1024
PACK = ROW // 2
PLANE = 4

epsilon = 1e-05
scale_base = 512.0
masked_score = -1e30
log2_e = 1.4426950408889634
score_factor = HEAD_DIM ** (-0.5) * log2_e
highest = lax.Precision.HIGHEST
f32 = jnp.float32
bf16 = jnp.bfloat16


def seq_index(y, z, x):
    return (y % 4) * 8 + (z % 2) * 4 + x % 4


def seq_pairs(move):
    pairs = []
    for y in range(4):
        for z in range(2):
            for x in range(4):
                pairs.append((seq_index(y, z, x), seq_index(*move(y, z, x))))
    return pairs


def shift_pairs(dy, dz, dx):
    return seq_pairs(lambda y, z, x: (y + dy, z + dz, x + dx))


def group_of(row):
    return min(row, 7 - row)


TO_SAME = seq_pairs(lambda y, z, x: (group_of(2 * y + z), z, x))
TO_OTHER = seq_pairs(lambda y, z, x: (group_of(2 * y + z), 1 - z, x))
FROM_SAME = [(b, a) for a, b in TO_SAME]
FROM_OTHER = [(b, a) for a, b in TO_OTHER]
X_SHIFTS = [shift_pairs(0, 0, d) for d in (1, 2, 3)]
Y_SHIFTS = [shift_pairs(d, 0, 0) for d in (1, 2, 3)]
Z_SWAP = shift_pairs(0, 1, 0)
CORE_SWAP = [(f, f ^ 1) for f in range(4)]
FAR_SWAP = [(f, f ^ 2) for f in range(4)]
Y_GROUPS = [[seq_index(y, z, x) for y in range(4)] for z in range(2) for x in range(4)]
X_GROUPS = [[seq_index(y, z, x) for x in range(4)] for y in range(4) for z in range(2)]
Z_GROUPS = [[seq_index(y, z, x) for z in range(2)] for y in range(4) for x in range(4)]
YX_GROUPS = [[seq_index(y, z, x) for y in range(4) for x in range(4)] for z in range(2)]


def shift_x(pieces):
    return [lax.ppermute(piece, "seq", pairs) for piece, pairs in zip(pieces[1:], X_SHIFTS)]


def shift_y(pieces):
    return [lax.ppermute(piece, "seq", pairs) for piece, pairs in zip(pieces[1:], Y_SHIFTS)]


def core_swap(values):
    return lax.ppermute(values, "ffn", CORE_SWAP)


def far_swap(values):
    return lax.ppermute(values, "ffn", FAR_SWAP)


def gather_x(values):
    return lax.all_gather(values, "seq", axis_index_groups=X_GROUPS, tiled=True)


def share_yx(values):
    values = lax.all_gather(values, "seq", axis_index_groups=YX_GROUPS)
    return values.reshape((4, 4) + values.shape[1:])


def sum_z(values):
    other = lax.ppermute(values, "seq", Z_SWAP)
    return (values.astype(f32) + other.astype(f32)).astype(bf16)


def after(value, *others):
    return lax.optimization_barrier((value,) + others)[0]


X, Y, Z, CORE, PART = range(5)


def run(kernel, name, here, operands, outs, scratch=(), megabytes=8, far=()):
    first = 1 + len(operands)

    def body(*refs):
        refs = list(refs)
        semaphores = refs.pop() if far else None
        kept = refs[len(refs) - len(far) :]
        refs = refs[: len(refs) - len(far)]
        targets = [refs[first + k] for k in far]
        for k, ref in zip(far, kept):
            refs[first + k] = ref
        kernel(*refs)
        copies = [
            pltpu.make_async_copy(ref, target, semaphores.at[k])
            for k, (ref, target) in enumerate(zip(kept, targets))
        ]
        for copy in copies:
            copy.start()
        for copy in copies:
            copy.wait()

    extra = [pltpu.VMEM(*outs[k]) for k in far]
    if far:
        extra.append(pltpu.SemaphoreType.DMA((len(far),)))
    return pl.pallas_call(
        body,
        in_specs=[pl.BlockSpec(memory_space=pltpu.SMEM)]
        + [pl.BlockSpec(memory_space=pltpu.VMEM)] * len(operands),
        out_specs=[
            pl.BlockSpec(memory_space=pltpu.HBM if k in far else pltpu.VMEM) for k in range(len(outs))
        ],
        out_shape=[jax.ShapeDtypeStruct(shape, kind) for shape, kind in outs],
        scratch_shapes=list(scratch) + extra,
        compiler_params=pltpu.CompilerParams(vmem_limit_bytes=megabytes * 2**20),
        cost_estimate=pl.CostEstimate(
            flops=2**20,
            bytes_accessed=sum(v.size * v.dtype.itemsize for v in operands)
            + sum(math.prod(shape) * jnp.dtype(kind).itemsize for shape, kind in outs),
            transcendentals=0,
        ),
        name=name,
    )(here, *operands)


def dot_nn(a, b):
    return lax.dot_general(a, b, (((1,), (0,)), ((), ())), preferred_element_type=f32)


def dot_nt(a, b):
    return lax.dot_general(a, b, (((1,), (1,)), ((), ())), preferred_element_type=f32)


def dot_tn(a, b):
    return lax.dot_general(a, b, (((0,), (0,)), ((), ())), preferred_element_type=f32)


def before(place, d):
    return lax.rem(place + (4 - d), 4)


def store_at(refs, place, index, value):
    for d, ref in enumerate(refs):

        @pl.when(lax.rem(place + d, 4) == index)
        def _(ref=ref):
            ref[...] = value


def store_half(mine, theirs, core, half, value):
    @pl.when(core == half)
    def _():
        mine[...] = value

    @pl.when(core != half)
    def _():
        theirs[...] = value


def row_of(column):
    return jnp.broadcast_to(column, (column.shape[0], 128)).T[0:1]


def split_three(values):
    high = values.astype(bf16).astype(f32)
    middle = (values - high).astype(bf16).astype(f32)
    return high, middle, values - high - middle


def norm_parts(values):
    center = values - jnp.mean(values, axis=-1, keepdims=True)
    inv_std = lax.rsqrt(jnp.mean(center * center, axis=-1, keepdims=True) + epsilon)
    return center * inv_std, inv_std


def norm_back(grad_out, unit, inv_std, gain):
    scaled = grad_out * gain
    return inv_std * (
        scaled
        - jnp.mean(scaled, axis=-1, keepdims=True)
        - unit * jnp.mean(scaled * unit, axis=-1, keepdims=True)
    )


def pair_pack(values, side):
    left = lax.broadcasted_iota(jnp.int32, (128, 128), 1) < 64
    if side == 0:
        return jnp.where(left, values[:128], pltpu.roll(values[128:], 64, 1))
    return jnp.where(left, pltpu.roll(values[:128], 64, 1), values[128:])


def pair_unpack(even, odd):
    left = lax.broadcasted_iota(jnp.int32, (128, 128), 1) < 64
    low = jnp.where(left, even, pltpu.roll(odd, 64, 1))
    high = jnp.where(left, pltpu.roll(even, 64, 1), odd)
    return jnp.concatenate([low, high], axis=0)


def half_swapped(values):
    lane = lax.broadcasted_iota(jnp.int32, values.shape, 1)
    return jnp.where(lane % 64 < 32, pltpu.roll(values, 96, 1), pltpu.roll(values, 32, 1))


def enter_kernel(
    here, tokens, kind, table, gain, offset, weight, shift, cosine, sine, growth, stream_ref, normed_ref, *out
):
    stream = tokens[...].astype(f32)
    for c in range(3):
        stream = stream + jnp.where(kind[...] == c, table[c : c + 1, :].astype(f32), 0.0)
    stream_ref[...] = stream
    unit, _ = norm_parts(stream)
    normed = (unit * gain[...].astype(f32) + offset[...].astype(f32)).astype(bf16)
    normed_ref[...] = normed
    projected = [dot_nn(normed, weight[s]) + shift[s : s + 1, :].astype(f32) for s in range(3)]
    lane = lax.broadcasted_iota(jnp.int32, (256, 128), 1)
    left = lane < 64
    signed = jnp.where(lane % 64 < 32, -sine[...], sine[...])
    for group in range(2):
        lanes = slice(128 * group, 128 * group + 128)
        query, key, value = [p[:, lanes] for p in projected]
        query = (query * cosine[...] + half_swapped(query) * signed) * growth[...]
        key = (key * cosine[...] + half_swapped(key) * signed) / growth[...]
        for side in range(2):
            if side == 0:
                both = jnp.where(left, key, pltpu.roll(value, 64, 1))
            else:
                both = jnp.where(left, pltpu.roll(key, 64, 1), value)
            message = jnp.concatenate([both, pair_pack(query, side)], axis=0).astype(bf16)
            store_at(out, here[X], 2 * group + side, message)


def enter(here, *operands):
    return run(
        enter_kernel,
        "enter",
        here,
        operands,
        [((256, D), f32), ((256, D), bf16)] + [((384, 128), bf16)] * 4,
        megabytes=5, far=(0, 1),
    )


def rows_kernel(here, p0, p1, p2, p3, kv_ref, q_ref):
    for d, ref in enumerate((p0, p1, p2, p3)):
        source = before(here[X], d)
        kv_ref[pl.ds(pl.multiple_of(source * 256, 256), 256), :] = ref[:256, :]
        q_ref[pl.ds(pl.multiple_of(source * 128, 128), 128), :] = ref[256:, :]


def rows(here, *pieces):
    return run(rows_kernel, "rows", here, pieces, [((ROW, 128), bf16), ((PACK, 128), bf16)], megabytes=1)


def lane_rows(row):
    return jnp.concatenate([row[:, 128 * j : 128 * j + 128] for j in range(8)], axis=0)


def unpack_transposed(source, target, offset):
    for b in range(4):
        piece = source[128 * b : 128 * b + 128, :].T
        target[offset : offset + 64, 256 * b : 256 * b + 128] = piece[:64]
        target[offset : offset + 64, 256 * b + 128 : 256 * b + 256] = piece[64:]


def pack_transposed(columns, target):
    for b in range(4):
        piece = jnp.concatenate(
            [columns[:, 256 * b : 256 * b + 128], columns[:, 256 * b + 128 : 256 * b + 256]], axis=0
        )
        target[128 * b : 128 * b + 128, :] = piece.T.astype(target.dtype)


def chunk_bounds(info, tile):
    z = info[0]
    row = info[1 + tile]
    lowest = info[3 + tile]
    first = jnp.int32(0)
    last = jnp.int32(0)
    for c in range(PLANE):
        start = (2 * c + z) * ROW
        first = first + (start + ROW - 1 < lowest).astype(jnp.int32)
        last = last + (2 * c + z <= row).astype(jnp.int32)
    return first, last


def visible(info, tile, c, begin_ref, shape):
    key = (2 * c + info[0]) * ROW + lax.broadcasted_iota(jnp.int32, shape, 0)
    query = info[1 + tile] * ROW + lax.broadcasted_iota(jnp.int32, shape, 1)
    return (key <= query) & (key >= begin_ref[...])


def needs_mask(info, tile, c):
    key_row = 2 * c + info[0]
    return (key_row == info[1 + tile]) | (key_row * ROW < info[5 + tile])


def plane_copies(info, pieces, kv_ref):
    return [
        (piece, kv_ref.at[pl.ds(pl.multiple_of(before(info[7], d) * ROW, ROW), ROW)])
        for d, piece in enumerate(pieces)
    ]


def forward_kernel(
    info,
    qa,
    qb,
    kv0,
    kv1,
    kv2,
    kv3,
    begin_ref,
    outa_ref,
    outb_ref,
    qt_ref,
    q_in,
    kv_ref,
    vt_ref,
    acc_ref,
    top_ref,
    semaphores,
):
    tile = pl.program_id(0)

    @pl.when(tile == 0)
    def _():
        copies = [
            pltpu.make_async_copy(source, target, semaphores.at[k])
            for k, (source, target) in enumerate(
                [(qa, q_in.at[0]), (qb, q_in.at[1])] + plane_copies(info, (kv0, kv1, kv2, kv3), kv_ref)
            )
        ]
        for copy in copies:
            copy.start()
        for copy in copies:
            copy.wait()
        for c in range(PLANE):
            block = kv_ref[c * ROW : c * ROW + ROW, :].T
            index = lax.broadcasted_iota(jnp.int32, block.shape, 0)
            vt_ref[:, c * ROW : c * ROW + ROW] = jnp.where(index < 64, jnp.ones_like(block), block)
        qt_ref[64:, :] = jnp.zeros((64, ROW), bf16)

    unpack_transposed(q_in.at[tile], qt_ref, 0)

    top_ref[...] = jnp.full(top_ref.shape, masked_score, f32)
    acc_ref[...] = jnp.zeros(acc_ref.shape, f32)

    def step(c, masked):
        start = pl.multiple_of(c * ROW, ROW)
        scores = dot_nn(kv_ref[pl.ds(start, ROW), :], qt_ref[...]) * score_factor
        if masked:
            scores = jnp.where(visible(info, tile, c, begin_ref, scores.shape), scores, 2 * masked_score)
        old = top_ref[...]
        top = jnp.maximum(old, jnp.max(scores, axis=0, keepdims=True))
        weights = jnp.exp2(scores - top)
        top_ref[...] = top
        acc_ref[...] = acc_ref[...] * jnp.exp2(old - top) + dot_nn(
            vt_ref[:, pl.ds(start, ROW)], weights.astype(bf16)
        )

    def body(c, carry):
        masked = needs_mask(info, tile, c)

        @pl.when(masked)
        def _():
            step(c, True)

        @pl.when(jnp.logical_not(masked))
        def _():
            step(c, False)

        return carry

    first, last = chunk_bounds(info, tile)
    lax.fori_loop(first, last, body, 0)
    total = acc_ref[0:1, :]
    some = total > 0
    safe = jnp.where(some, total, 1.0)
    log_total = jnp.where(some, top_ref[...] + jnp.log2(safe), masked_score)
    for index, out_ref in enumerate((outa_ref, outb_ref)):

        @pl.when(tile == index)
        def _(out_ref=out_ref):
            pack_transposed(acc_ref[64:, :] / safe, out_ref)
            parts = [lane_rows(part) for part in split_three(log_total)]
            out_ref[PACK:, :] = jnp.concatenate(parts + [jnp.zeros((8, 128), f32)], axis=0).astype(bf16)


def attend_forward(info, queries_a, queries_b, keys_values, begin):
    hbm = pl.BlockSpec(memory_space=pltpu.HBM)
    return pl.pallas_call(
        forward_kernel,
        grid_spec=pltpu.PrefetchScalarGridSpec(
            num_scalar_prefetch=1,
            grid=(2,),
            in_specs=[hbm] * 6 + [pl.BlockSpec((1, ROW), lambda i, s: (0, i))],
            out_specs=[pl.BlockSpec((PACK + 32, 128), lambda i, s: (0, 0))] * 2,
            scratch_shapes=[
                pltpu.VMEM((128, ROW), bf16),
                pltpu.VMEM((2, PACK, 128), bf16),
                pltpu.VMEM((PLANE * ROW, 128), bf16),
                pltpu.VMEM((128, PLANE * ROW), bf16),
                pltpu.VMEM((128, ROW), f32),
                pltpu.VMEM((1, ROW), f32),
                pltpu.SemaphoreType.DMA((6,)),
            ],
        ),
        out_shape=[jax.ShapeDtypeStruct((PACK + 32, 128), bf16)] * 2,
        compiler_params=pltpu.CompilerParams(vmem_limit_bytes=9 * 2**20),
        cost_estimate=pl.CostEstimate(flops=10 * 10**9, bytes_accessed=2**21, transcendentals=0),
        name="attend_forward",
    )(info, queries_a, queries_b, *keys_values, begin)


def combine_kernel(here, a_ref, b_ref, full_ref, log_ref, *out):
    logs = []
    for ref in (a_ref, b_ref):
        rows = ref[PACK:, :].astype(f32)
        logs.append(rows[:8] + rows[8:16] + rows[16:24])
    top = jnp.maximum(logs[0], logs[1])
    shares = [jnp.exp2(part - top) for part in logs]
    total = shares[0] + shares[1]
    log_ref[...] = top + jnp.log2(total)
    columns = [(share / total).T for share in shares]
    left = lax.broadcasted_iota(jnp.int32, (128, 128), 1) < 64
    for b in range(4):
        mixed = jnp.zeros((128, 128), f32)
        for ref, column in zip((a_ref, b_ref), columns):
            weight = jnp.where(left, column[:, 2 * b : 2 * b + 1], column[:, 2 * b + 1 : 2 * b + 2])
            mixed = mixed + weight * ref[128 * b : 128 * b + 128, :].astype(f32)
        full_ref[128 * b : 128 * b + 128, :] = mixed
        store_at(out, here[X], b, mixed.astype(bf16))


def combine(here, part_a, part_b):
    return run(
        combine_kernel,
        "combine",
        here,
        (part_a, part_b),
        [((PACK, 128), f32), ((8, 128), f32)] + [((128, 128), bf16)] * 4,
        megabytes=1, far=(0, 1),
    )


def grad_message_kernel(here, p0, p1, p2, p3, mixed_ref, log_ref, out_ref):
    for d, ref in enumerate((p0, p1, p2, p3)):
        out_ref[pl.ds(pl.multiple_of(before(here[X], d) * 128, 128), 128), :] = ref[...]
    deltas = []
    for b in range(4):
        rows = slice(128 * b, 128 * b + 128)
        each = (out_ref[rows, :].astype(f32) * mixed_ref[rows, :]).T
        deltas.append(jnp.sum(each[:64], axis=0, keepdims=True))
        deltas.append(jnp.sum(each[64:], axis=0, keepdims=True))
    parts = list(split_three(log_ref[...])) + list(split_three(jnp.concatenate(deltas, axis=0)))
    out_ref[PACK:, :] = jnp.concatenate(parts, axis=0).astype(bf16)


def grad_message(here, *operands):
    return run(grad_message_kernel, "grad_message", here, operands, [((PACK + 48, 128), bf16)], megabytes=1)[0]


def backward_kernel(
    info,
    qa,
    qb,
    ma,
    mb,
    kv0,
    kv1,
    kv2,
    kv3,
    begin_ref,
    dqa_ref,
    dqb_ref,
    own_ref,
    one_ref,
    two_ref,
    three_ref,
    qt_ref,
    gt_ref,
    q_ref,
    g_ref,
    kv_ref,
    kt_ref,
    row_ref,
    acc_ref,
    dq_acc,
    q_in,
    m_in,
    semaphores,
):
    tile = pl.program_id(0)

    def load(query_ref, message_ref):
        unpack_transposed(query_ref, qt_ref, 0)
        unpack_transposed(message_ref, gt_ref, 64)
        q_ref[...] = qt_ref[...].T
        g_ref[...] = gt_ref[...].T
        rows = message_ref[PACK:, :].astype(f32)
        for k in range(2):
            part = rows[24 * k : 24 * k + 8] + rows[24 * k + 8 : 24 * k + 16] + rows[24 * k + 16 : 24 * k + 24]
            for j in range(8):
                row_ref[k : k + 1, 128 * j : 128 * j + 128] = part[j : j + 1, :]

    @pl.when(tile == 0)
    def _():
        copies = [
            pltpu.make_async_copy(source, target, semaphores.at[k])
            for k, (source, target) in enumerate(
                [(qa, q_in.at[0]), (qb, q_in.at[1]), (ma, m_in.at[0]), (mb, m_in.at[1])]
                + plane_copies(info, (kv0, kv1, kv2, kv3), kv_ref)
            )
        ]
        for copy in copies:
            copy.start()
        acc_ref[...] = jnp.zeros(acc_ref.shape, f32)
        qt_ref[64:, :] = jnp.zeros((64, ROW), bf16)
        gt_ref[:64, :] = jnp.zeros((64, ROW), bf16)
        for copy in copies:
            copy.wait()
        for c in range(PLANE):
            kt_ref[:, c * ROW : c * ROW + ROW] = kv_ref[c * ROW : c * ROW + ROW, :].T

    load(q_in.at[tile], m_in.at[tile])
    dq_acc[...] = jnp.zeros(dq_acc.shape, f32)

    def step(c, masked):
        start = pl.multiple_of(c * ROW, ROW)
        block = kv_ref[pl.ds(start, ROW), :]
        scores = dot_nn(block, qt_ref[...]) * score_factor
        if masked:
            scores = jnp.where(visible(info, tile, c, begin_ref, scores.shape), scores, 2 * masked_score)
        weights = jnp.exp2(scores - row_ref[0:1, :])
        grad_weights = dot_nn(block, gt_ref[...])
        grad_scores = (weights * (grad_weights - row_ref[1:2, :])).astype(bf16)
        acc_ref[pl.ds(start, ROW), :] += dot_nn(grad_scores, q_ref[...]) + dot_nn(
            weights.astype(bf16), g_ref[...]
        )
        dq_acc[...] += dot_nn(kt_ref[:, pl.ds(start, ROW)], grad_scores)

    def body(c, carry):
        masked = needs_mask(info, tile, c)

        @pl.when(masked)
        def _():
            step(c, True)

        @pl.when(jnp.logical_not(masked))
        def _():
            step(c, False)

        return carry

    first, last = chunk_bounds(info, tile)
    lax.fori_loop(first, last, body, 0)

    @pl.when(tile == 0)
    def _():
        pack_transposed(dq_acc[:64, :], dqa_ref)

    @pl.when(tile == 1)
    def _():
        pack_transposed(dq_acc[:64, :], dqb_ref)
        for d, ref in enumerate((own_ref, one_ref, two_ref, three_ref)):
            start = pl.multiple_of(lax.rem(info[7] + d, 4) * ROW, ROW)
            ref[...] = acc_ref[pl.ds(start, ROW), :].astype(bf16)


def attend_backward(info, queries_a, queries_b, message_a, message_b, keys_values, begin):
    packed = pl.BlockSpec((PACK, 128), lambda i, s: (0, 0))
    hbm = pl.BlockSpec(memory_space=pltpu.HBM)
    block = pl.BlockSpec((ROW, 128), lambda i, s: (0, 0))
    return pl.pallas_call(
        backward_kernel,
        grid_spec=pltpu.PrefetchScalarGridSpec(
            num_scalar_prefetch=1,
            grid=(2,),
            in_specs=[hbm] * 8 + [pl.BlockSpec((1, ROW), lambda i, s: (0, i))],
            out_specs=[packed] * 2 + [block] * 4,
            scratch_shapes=[
                pltpu.VMEM((128, ROW), bf16),
                pltpu.VMEM((128, ROW), bf16),
                pltpu.VMEM((ROW, 128), bf16),
                pltpu.VMEM((ROW, 128), bf16),
                pltpu.VMEM((PLANE * ROW, 128), bf16),
                pltpu.VMEM((128, PLANE * ROW), bf16),
                pltpu.VMEM((8, ROW), f32),
                pltpu.VMEM((PLANE * ROW, 128), f32),
                pltpu.VMEM((128, ROW), f32),
                pltpu.VMEM((2, PACK, 128), bf16),
                pltpu.VMEM((2, PACK + 48, 128), bf16),
                pltpu.SemaphoreType.DMA((8,)),
            ],
        ),
        out_shape=[jax.ShapeDtypeStruct((PACK, 128), bf16)] * 2
        + [jax.ShapeDtypeStruct((ROW, 128), bf16)] * 4,
        compiler_params=pltpu.CompilerParams(vmem_limit_bytes=17 * 2**20),
        cost_estimate=pl.CostEstimate(flops=18 * 10**9, bytes_accessed=2**22, transcendentals=0),
        name="attend_backward",
    )(info, queries_a, queries_b, message_a, message_b, *keys_values, begin)


def inner_kernel(here, p0, p1, p2, p3, gain, weight, mixed_ref, mine, theirs, heads):
    for d, ref in enumerate((p0, p1, p2, p3)):
        heads[before(here[X], d)] = ref[...].astype(f32)
    mixed = jnp.concatenate([pair_unpack(heads[0], heads[1]), pair_unpack(heads[2], heads[3])], axis=1)
    mixed_ref[...] = mixed
    mean = jnp.mean(mixed, axis=-1, keepdims=True)
    centred = mixed - mean
    spread = jnp.sum(centred * centred, axis=-1, keepdims=True)
    projected = dot_nn((centred * gain[...]).astype(bf16), weight[...])
    for half in range(2):
        tokens = slice(128 * half, 128 * half + 128)
        stats = [row_of(mean[tokens]), row_of(spread[tokens])]
        slots = [jnp.where(here[PART] == j // 2, stats[j % 2], 0.0) for j in range(8)]
        row = jnp.broadcast_to(jnp.concatenate(slots, axis=1), (8, D))
        store_half(mine, theirs, here[CORE], half, jnp.concatenate([projected[tokens], row], axis=0))


def inner(here, *operands):
    return run(
        inner_kernel,
        "inner",
        here,
        operands,
        [((256, 256), f32), ((136, D), f32), ((136, D), f32)],
        [pltpu.VMEM((4, 128, 128), f32)],
        megabytes=3,
    )


def chip_stats_kernel(here, mine, other, out):
    total = mine[...] + other[...]
    high, middle, low = split_three(total[128:])
    index = lax.broadcasted_iota(jnp.int32, (8, D), 0)
    out[...] = jnp.concatenate([total[:128], jnp.where(index < 4, high, middle), low], axis=0).astype(bf16)


def join_stats_kernel(here, chip, far, out):
    total = chip[...].astype(f32) + far[...].astype(f32)
    row = total[128:129] + total[132:133] + total[136:137]
    out[...] = jnp.concatenate([total[:128], jnp.broadcast_to(row, (8, D))], axis=0)


def add_chip_kernel(here, mine, other, out):
    out[...] = (mine[...] + other[...]).astype(bf16)


def add_far_kernel(here, chip, far, out):
    out[...] = chip[...].astype(f32) + far[...].astype(f32)


def chip_stats(here, mine, other):
    return run(chip_stats_kernel, "chip_stats", here, (mine, other), [((144, D), bf16)], megabytes=1)[0]


def join_stats(here, chip, far):
    return run(join_stats_kernel, "join_stats", here, (chip, far), [((136, D), f32)], megabytes=1)[0]


def add_chip(here, mine, other):
    return run(add_chip_kernel, "add_chip", here, (mine, other), [((128, D), bf16)], megabytes=1)[0]


def add_far(here, chip, far):
    return run(add_far_kernel, "add_far", here, (chip, far), [((128, D), f32)], megabytes=1)[0]


def sum_ffn(here, mine, theirs):
    chip = add_chip(here, mine, core_swap(theirs))
    total = add_far(here, chip, far_swap(chip))
    return total, core_swap(total)


def gauss_share(values):
    return 0.5 + 0.5 * lax.erf(values * math.sqrt(0.5))


def feed_kernel(
    here,
    total,
    other,
    vectors,
    stream,
    vec,
    mixed_ref,
    weight,
    grad_hidden,
    both_ref,
    middle_ref,
    before_ref,
    unit_ref,
    inv_ref,
    sums_ref,
    halves,
):
    halves[here[CORE]] = total[...]
    halves[1 - here[CORE]] = other[...]
    ending = vectors[4:5, :] + vec[OUTPUT_BIAS : OUTPUT_BIAS + 1, :]
    inner_gain = vec[INNER : INNER + 1, :256]
    inner_bias = vec[INNER : INNER + 1, 256:512]
    for half in range(2):
        tokens = slice(128 * half, 128 * half + 128)
        stats = jnp.concatenate([halves[half, 128:129, 128 * j : 128 * j + 128] for j in range(8)], axis=0).T
        means = [stats[:, 2 * k : 2 * k + 1] for k in range(4)]
        mean = (means[0] + means[1] + means[2] + means[3]) * 0.25
        spread = stats[:, 1:2] + stats[:, 3:4] + stats[:, 5:6] + stats[:, 7:8]
        projected = halves[half, :128, :]
        for k in range(4):
            move = means[k] - mean
            spread = spread + 256.0 * move * move
            projected = projected + move * vectors[k : k + 1, :]
        inv = lax.rsqrt(spread / D + epsilon)
        middle_ref[tokens, :] = stream[tokens, :] + projected * inv + ending
        unit = (mixed_ref[tokens, :] - mean) * inv
        unit_ref[tokens, :] = unit
        inv_ref[tokens, :] = jnp.broadcast_to(inv, (128, 128))
        both_ref[tokens, D:] = (unit * inner_gain + inner_bias).astype(bf16)
    unit, _ = norm_parts(middle_ref[...])
    both_ref[:, :D] = (
        unit * vec[FEED_GAIN : FEED_GAIN + 1, :] + vec[FEED_BIAS : FEED_BIAS + 1, :]
    ).astype(bf16)
    before_act = dot_nn(both_ref[:, :D], weight[...]) + vec[UP_BIAS : UP_BIAS + 1, :]
    before_ref[...] = before_act
    active = before_act * gauss_share(before_act)
    scaled = grad_hidden[...] * vec[HIDDEN_GAIN : HIDDEN_GAIN + 1, :]
    columns = [
        jnp.sum(part, axis=-1, keepdims=True) for part in (active, active * active, scaled, scaled * active)
    ]
    lane = lax.broadcasted_iota(jnp.int32, (256, 128), 1)
    spread = jnp.zeros((256, 128), f32)
    for k, column in enumerate(columns):
        spread = jnp.where(lane == k, column, spread)
    sums_ref[...] = spread.T[:8]


def feed(here, *operands):
    return run(
        feed_kernel,
        "feed",
        here,
        operands,
        [
            ((256, D + 256), bf16),
            ((256, D), f32),
            ((256, D), f32),
            ((256, 256), f32),
            ((256, 128), f32),
            ((8, 256), f32),
        ],
        [pltpu.VMEM((2, 136, D), f32)],
        megabytes=10, far=(0, 1, 2, 3, 4),
    )


def hidden_kernel(
    here, sums, before_ref, grad_hidden, vec, weight, low_ref, small_ref, mine, theirs, o0, o1, o2, o3
):
    before_act = before_ref[...]
    share = gauss_share(before_act)
    slope = share + before_act * jnp.exp(-0.5 * before_act * before_act) * (1.0 / math.sqrt(2.0 * math.pi))
    columns = sums[...].T
    mean = columns[:, 0:1] / FF
    inv = lax.rsqrt(columns[:, 1:2] / FF - mean * mean + epsilon)
    first = columns[:, 2:3]
    cross = inv * (columns[:, 3:4] - mean * first)
    gain = vec[HIDDEN_GAIN : HIDDEN_GAIN + 1, :]
    unit = (before_act * share - mean) * inv
    low_ref[...] = (unit * gain + vec[HIDDEN_BIAS : HIDDEN_BIAS + 1, :]).astype(bf16)
    grad_out = grad_hidden[...]
    grad_pre = (inv * (grad_out * gain - first / FF - unit * (cross / FF)) * slope).astype(bf16)
    small_ref[0:1, :] = jnp.sum(grad_out * unit, axis=0, keepdims=True)
    small_ref[1:2, :] = jnp.sum(grad_out, axis=0, keepdims=True)
    small_ref[2:3, :] = jnp.sum(grad_pre.astype(f32), axis=0, keepdims=True)
    small_ref[3:, :] = jnp.zeros((5, D), f32)
    for k in range(4):
        lanes = slice(256 * k, 256 * k + 256)
        store_at((o0, o1, o2, o3), here[X], k, jnp.concatenate([low_ref[:, lanes], grad_pre[:, lanes]], axis=0))
    back = dot_nt(grad_pre, weight[...])
    for half in range(2):
        store_half(mine, theirs, here[CORE], half, back[128 * half : 128 * half + 128])


def hidden(here, *operands):
    return run(
        hidden_kernel,
        "hidden",
        here,
        operands,
        [((256, D), bf16), ((8, D), f32), ((128, D), f32), ((128, D), f32)] + [((512, 256), bf16)] * 4,
        megabytes=8, far=(1,),
    )


def feed_out_kernel(here, low_ref, weight, mine, theirs):
    for half in range(2):
        tokens = slice(128 * half, 128 * half + 128)
        store_half(mine, theirs, here[CORE], half, dot_nn(low_ref[tokens, :], weight[...]))


def feed_out(here, low, weight):
    return run(
        feed_out_kernel, "feed_out", here, (low, weight), [((128, D), f32), ((128, D), f32)], megabytes=2
    )


def result_kernel(here, total, other, middle, vec, out, halves):
    halves[here[CORE]] = total[...]
    halves[1 - here[CORE]] = other[...]
    for half in range(2):
        tokens = slice(128 * half, 128 * half + 128)
        out[tokens, :] = (
            middle[tokens, :] + halves[half] + vec[DOWN_BIAS : DOWN_BIAS + 1, :]
        ).astype(bf16)


def result_out(here, *operands):
    return run(
        result_kernel,
        "result",
        here,
        operands,
        [((256, D), bf16)],
        [pltpu.VMEM((2, 128, D), f32)],
        megabytes=4,
    )[0]


def feed_quarter_kernel(here, p0, p1, p2, p3, cotangent, both, out):
    down = jnp.zeros((256, D), f32)
    up = jnp.zeros((256, D), f32)
    for d, ref in enumerate((p0, p1, p2, p3)):
        tokens = pl.ds(pl.multiple_of(before(here[X], d) * 256, 256), 256)
        down = down + dot_tn(ref[:256, :], cotangent[tokens, :])
        up = up + dot_tn(ref[256:, :], both[tokens, :D])
    for y in range(4):
        for z in range(2):
            out[y, z, :128, :] = down[128 * z : 128 * z + 128, 256 * y : 256 * y + 256].astype(bf16)
            rows = slice(256 * y + 128 * z, 256 * y + 128 * z + 128)
            out[y, z, 128:, :] = up[:, rows].T.astype(bf16)


def feed_quarter(here, *operands):
    return run(
        feed_quarter_kernel, "feed_quarter", here, operands, [((4, 2, 256, 256), bf16)], megabytes=3
    )[0]


def middle_back_kernel(
    here,
    total,
    other,
    middle,
    stream,
    cotangent,
    vec,
    weight,
    unit_ref,
    inv_ref,
    vectors,
    grad_ref,
    small_ref,
    h0,
    h1,
    h2,
    h3,
    b0,
    b1,
    b2,
    b3,
    halves,
):
    halves[here[CORE]] = total[...]
    halves[1 - here[CORE]] = other[...]
    grad_feed = jnp.concatenate([halves[0], halves[1]], axis=0)
    unit, inv = norm_parts(middle[...])
    grad_result = cotangent[...].astype(f32)
    grad_middle = grad_result + norm_back(grad_feed, unit, inv, vec[FEED_GAIN : FEED_GAIN + 1, :])
    grad_ref[...] = grad_middle
    low = grad_middle.astype(bf16)
    branch = low.astype(f32)
    for k in range(4):
        store_at((b0, b1, b2, b3), here[X], k, low[:, 256 * k : 256 * k + 256])
    grad_inner = dot_nt(low, weight[...])
    through = vectors[0:1, :] + vectors[1:2, :] + vectors[2:3, :] + vectors[3:4, :]
    first = jnp.sum(branch * through, axis=-1, keepdims=True)
    ending = vectors[4:5, :] + vec[OUTPUT_BIAS : OUTPUT_BIAS + 1, :]
    cross = jnp.sum(branch * (middle[...] - stream[...] - ending), axis=-1, keepdims=True)
    inner_unit = unit_ref[...]
    inner_inv = inv_ref[:, 0:1]
    grad_mixed = inner_inv * (
        grad_inner * vec[INNER : INNER + 1, :256] - first / D - inner_unit * (cross / D)
    )
    for group in range(2):
        lanes = grad_mixed[:, 128 * group : 128 * group + 128]
        for side in range(2):
            store_at((h0, h1, h2, h3), here[X], 2 * group + side, pair_pack(lanes, side).astype(bf16))
    small_ref[0:1, :] = jnp.sum(grad_feed * unit, axis=0, keepdims=True)
    small_ref[1:2, :] = jnp.sum(grad_feed, axis=0, keepdims=True)
    small_ref[2:3, :] = jnp.sum(branch, axis=0, keepdims=True)
    small_ref[3:4, :] = jnp.sum(grad_result, axis=0, keepdims=True)
    small_ref[4:5, :256] = jnp.sum(grad_inner * inner_unit, axis=0, keepdims=True)
    small_ref[4:5, 256:512] = jnp.sum(grad_inner, axis=0, keepdims=True)
    small_ref[4:5, 512:] = jnp.zeros((1, 512), f32)
    small_ref[5:, :] = jnp.zeros((3, D), f32)


def middle_back(here, *operands):
    return run(
        middle_back_kernel,
        "middle_back",
        here,
        operands,
        [((256, D), f32), ((8, D), f32)] + [((128, 128), bf16)] * 4 + [((256, 256), bf16)] * 4,
        [pltpu.VMEM((2, 128, D), f32)],
        megabytes=10, far=(0, 1),
    )


def row_grads_kernel(
    here, own, one, two, three, qa, qb, kv_cos, kv_sin, q_cos, q_sin, out_ref, sums_ref, p0, p1, p2, p3
):
    def turned(values, cosine, sine):
        return (values * cosine + half_swapped(values) * sine).astype(bf16)

    for b in range(8):
        rows = slice(128 * b, 128 * b + 128)
        total = own[rows, :].astype(f32)
        for ref in (one, two, three):
            total = total + ref[rows, :].astype(f32)
        out_ref[rows, :128] = turned(total, kv_cos[rows, :], kv_sin[rows, :])
    for b in range(4):
        rows = slice(128 * b, 128 * b + 128)
        total = qa[rows, :].astype(f32) + qb[rows, :].astype(f32)
        for side in range(2):
            tokens = slice(256 * b + 128 * side, 256 * b + 128 * side + 128)
            values = total if side == 0 else pltpu.roll(total, 64, 1)
            out_ref[tokens, 128:] = turned(values, q_cos[tokens, :], q_sin[tokens, :])
    for b in range(4):
        store_at((p0, p1, p2, p3), here[X], b, out_ref[256 * b : 256 * b + 256, :])
    sums_ref[...] = jnp.broadcast_to(jnp.sum(out_ref[...].astype(f32), axis=0, keepdims=True), (8, 256))


def row_grads(here, *operands):
    return run(
        row_grads_kernel,
        "row_grads",
        here,
        operands,
        [((ROW, 256), bf16), ((8, 256), f32)] + [((256, 256), bf16)] * 4,
        megabytes=3,
    )


def head_weights_kernel(here, weight, out):
    left = lax.broadcasted_iota(jnp.int32, (256, 128), 1) < 64
    for r in range(4):
        rows = slice(256 * r, 256 * r + 256)
        for group in range(2):
            lanes = slice(128 * group, 128 * group + 128)
            query, key, value = [weight[s, rows, lanes].astype(f32) for s in range(3)]
            even = [jnp.where(left, key, pltpu.roll(value, 64, 1)), jnp.where(left, query, 0.0)]
            odd = [
                jnp.where(left, pltpu.roll(key, 64, 1), value),
                jnp.where(left, pltpu.roll(query, 64, 1), 0.0),
            ]
            for side, parts in enumerate((even, odd)):
                out[2 * group + side, rows, :] = jnp.concatenate(parts, axis=1).astype(bf16)


def head_weights(here, weight):
    return run(head_weights_kernel, "head_weights", here, (weight,), [((4, D, 256), bf16)], megabytes=2)[0]


def normed_back_kernel(here, p0, p1, p2, p3, weight, mine, theirs):
    for half in range(2):
        total = jnp.zeros((128, D), f32)
        for d, ref in enumerate((p0, p1, p2, p3)):
            total = total + dot_nt(ref[128 * half : 128 * half + 128, :], weight[before(here[X], d)])
        store_half(mine, theirs, here[CORE], half, total)


def normed_back(here, *operands):
    return run(
        normed_back_kernel, "normed_back", here, operands, [((128, D), f32), ((128, D), f32)], megabytes=2
    )


def attend_quarter_kernel(
    here, normed, projected, sums, both, s0, s1, s2, s3, small_a, small_b, q0, q1, q2, q3
):
    grad_input = dot_tn(projected[...], normed[...])
    grad_output = jnp.zeros((256, 256), f32)
    for d, ref in enumerate((s0, s1, s2, s3)):
        tokens = pl.ds(pl.multiple_of(before(here[X], d) * 256, 256), 256)
        grad_output = grad_output + dot_tn(both[tokens, D:], ref[...])
    slots = [jnp.where(here[X] == k, sums[0:1, :], 0.0) for k in range(4)]
    vectors = [small_a[k : k + 1, :] for k in range(3)] + [small_b[k : k + 1, :] for k in range(5)]
    left = lax.broadcasted_iota(jnp.int32, (128, 128), 1) < 64
    nothing = jnp.zeros((4, 256), f32)
    for y in range(4):
        parts = []
        group = grad_output[:, 128 * (y // 2) : 128 * (y // 2) + 128]
        for z in range(2):
            rows = slice(256 * y + 128 * z, 256 * y + 128 * z + 128)
            ours = group[128 * z : 128 * z + 128, :]
            ours = pltpu.roll(ours, 64, 1) if y % 2 == 0 else ours
            tall = grad_input[:, rows].T
            tall = jnp.concatenate([tall[:, :128], jnp.where(left, tall[:, 128:], ours)], axis=1)
            vector = vectors[2 * y + z]
            small = [vector[:, 256 * k : 256 * k + 256] for k in range(4)]
            small = small + (slots if y == 0 and z == 0 else [nothing]) + [nothing, nothing]
            parts.append(jnp.concatenate([tall] + small, axis=0).astype(bf16)[None])
        store_at((q0, q1, q2, q3), here[Y], y, jnp.concatenate(parts, axis=0))


def attend_quarter(here, *operands):
    return run(
        attend_quarter_kernel,
        "attend_quarter",
        here,
        operands,
        [((2, 144, 256), bf16)] * 4,
        megabytes=3,
    )


def add_four_kernel(here, p0, p1, p2, p3, out):
    total = p0[...].astype(f32) + p1[...].astype(f32) + p2[...].astype(f32) + p3[...].astype(f32)
    out[...] = total.astype(bf16)


def add_four(here, *pieces):
    return run(add_four_kernel, "add_four", here, pieces, [((2, 144, 256), bf16)], megabytes=1)[0]


def feed_weights_kernel(in_ref, down_ref, up_ref):
    for x in range(4):
        for z in range(2):
            rows = slice(256 * x + 128 * z, 256 * x + 128 * z + 128)
            down_ref[rows, :] = in_ref[0, x, z, :128, :].astype(f32)
            up_ref[128 * z : 128 * z + 128, 256 * x : 256 * x + 256] = in_ref[0, x, z, 128:, :].astype(f32)


def feed_weights_out(shared):
    return pl.pallas_call(
        feed_weights_kernel,
        grid=(4,),
        in_specs=[pl.BlockSpec((1, 4, 2, 256, 256), lambda y: (y, 0, 0, 0, 0))],
        out_specs=[pl.BlockSpec((D, 256), lambda y: (0, y)), pl.BlockSpec((256, D), lambda y: (y, 0))],
        out_shape=[jax.ShapeDtypeStruct((D, D), f32)] * 2,
        compiler_params=pltpu.CompilerParams(vmem_limit_bytes=6 * 2**20),
        name="feed_weights",
    )(shared)


def attend_weights_kernel(here, in_ref, input_ref, output_ref, *small_refs):
    for y in range(4):
        for z in range(2):
            rows = slice(256 * y + 128 * z, 256 * y + 128 * z + 128)
            blocks = [in_ref[y, x, z, :128, :].astype(f32) for x in range(4)]
            for s, start in enumerate((128, 0, 64)):
                input_ref[s, rows, :] = jnp.concatenate([b[:, start : start + 64] for b in blocks], axis=1)
            for x in range(4):
                output_ref[128 * z : 128 * z + 128, 256 * x + 64 * y : 256 * x + 64 * y + 64] = blocks[x][:, 192:]
            small = jnp.zeros((16, 256), f32)
            for x in range(4):
                small = small + in_ref[y, x, z, 128:, :].astype(f32)
            small_refs[2 * y + z][...] = jnp.concatenate([small[k : k + 1] for k in range(4)], axis=1)
            if y == 0 and z == 0:
                small_refs[8][...] = jnp.concatenate([small[k : k + 1] for k in range(4, 8)], axis=1)


def attend_weights_out(here, shared):
    return run(
        attend_weights_kernel,
        "attend_weights",
        here,
        (shared,),
        [((3, D, 256), f32), ((256, D), f32)] + [((1, D), f32)] * 9,
        megabytes=7,
    )


def leave_kernel(here, total, other, stream, grad_middle, vec, kind, out_ref, last_ref, halves):
    halves[here[CORE]] = total[...]
    halves[1 - here[CORE]] = other[...]
    grad_normed = jnp.concatenate([halves[0], halves[1]], axis=0)
    unit, inv = norm_parts(stream[...])
    grad = grad_middle[...] + norm_back(grad_normed, unit, inv, vec[ATTEND_GAIN : ATTEND_GAIN + 1, :])
    out_ref[...] = grad
    last_ref[0:1, :] = jnp.sum(grad_normed * unit, axis=0, keepdims=True)
    last_ref[1:2, :] = jnp.sum(grad_normed, axis=0, keepdims=True)
    for c in range(3):
        last_ref[2 + c : 3 + c, :] = jnp.sum(jnp.where(kind[...] == c, grad, 0.0), axis=0, keepdims=True)
    last_ref[5:, :] = jnp.zeros((3, D), f32)


def leave(here, *operands):
    return run(
        leave_kernel,
        "leave",
        here,
        operands,
        [((256, D), f32), ((8, D), f32)],
        [pltpu.VMEM((2, 128, D), f32)],
        megabytes=7,
    )


def ring_sum_kernel(axis, here, p0, p1, p2, p3, out, ring):
    for d, ref in enumerate((p0, p1, p2, p3)):
        ring[before(here[axis], d)] = ref[...]
    out[...] = ring[0] + ring[1] + ring[2] + ring[3]


def ring_sum(here, axis, *pieces):
    return run(
        partial(ring_sum_kernel, axis),
        "ring_sum",
        here,
        pieces,
        [((8, D), f32)],
        [pltpu.VMEM((4, 8, D), f32)],
        megabytes=1,
    )[0]


def last_sum_kernel(here, own, other, table_ref, gain_ref, bias_ref):
    total = own[...] + other[...]
    gain_ref[...] = total[0:1]
    bias_ref[...] = total[1:2]
    table_ref[...] = total[2:5]


def last_sum(here, own, other):
    return run(
        last_sum_kernel,
        "last_sum",
        here,
        (own, other),
        [((3, D), f32), ((1, D), f32), ((1, D), f32)],
        megabytes=1,
    )


ATTEND_GAIN, OUTPUT_BIAS, FEED_GAIN, FEED_BIAS, DOWN_BIAS, UP_BIAS, HIDDEN_GAIN, HIDDEN_BIAS, INNER = range(9)


def tables_of(positions, total_rows):
    pair_index = (jnp.arange(128) % 32).astype(f32)
    frequency = 1.0 / 10000.0 ** (pair_index / 32)
    angles = positions.astype(f32)[:, None] * frequency[None, :]
    ratios = (2.0 * pair_index + 0.4 * HEAD_DIM) / (1.4 * HEAD_DIM)
    exponent = (positions - total_rows // 2).astype(f32)[:, None] / scale_base
    return jnp.cos(angles), jnp.sin(angles), ratios[None, :] ** exponent


def back_tables(positions, total_rows, score_scale):
    lane = jnp.arange(128)
    cosine, sine, growth = tables_of(positions, total_rows)
    cosine = cosine * score_scale
    sine = sine * jnp.where(lane < 32, score_scale, -score_scale)[None]
    turned = (lane < 64)[None]
    return (
        jnp.where(turned, cosine / growth, 1.0),
        jnp.where(turned, sine / growth, 0.0),
        jnp.where(turned, cosine * growth, 0.0),
        jnp.where(turned, sine * growth, 0.0),
    )


def per_device(
    tokens,
    segment_kind,
    document,
    type_table,
    attend_gain,
    attend_bias,
    input_weight,
    input_bias,
    inner_gain,
    inner_bias,
    output_weight,
    output_bias,
    feed_gain,
    feed_bias,
    up_weight,
    up_bias,
    hidden_gain,
    hidden_bias,
    down_weight,
    down_bias,
    cotangent,
):
    local_rows = tokens.shape[0]
    total_rows = document.shape[0]
    local_width = input_weight.shape[2]
    score_scale = HEAD_DIM ** (-0.5)
    place = lax.axis_index("seq")
    part = lax.axis_index("ffn")
    y, z, x = place // 8, (place // 4) % 2, place % 4
    here = jnp.stack([x, y, z, part % 2, part, part, part, part]).astype(jnp.int32)
    query_pos = place * local_rows + jnp.arange(local_rows, dtype=jnp.int32)
    kind = segment_kind[:, None]

    stream, normed_low, *pieces = enter(
        here,
        tokens,
        kind,
        type_table,
        attend_gain[None],
        attend_bias[None],
        input_weight,
        input_bias,
        *tables_of(query_pos, total_rows),
    )
    received = shift_x(pieces)

    begins = jnp.zeros((total_rows,), jnp.int32)
    for number in range(1, 4):
        begins = begins + jnp.where(
            document >= number, jnp.sum((document == number - 1).astype(jnp.int32)), 0
        )
    row_a = jnp.where(y % 2 == z, y, 7 - y)
    row_b = 7 - row_a
    begin_a = lax.dynamic_slice_in_dim(begins, row_a * ROW, ROW)
    begin_b = lax.dynamic_slice_in_dim(begins, row_b * ROW, ROW)
    begin = jnp.concatenate([begin_a, begin_b])[None]
    info = jnp.stack([z, row_a, row_b, begin_a[0], begin_b[0], begin_a[-1], begin_b[-1], y]).astype(
        jnp.int32
    )
    row_kv, row_q = rows(here, pieces[0], *received)
    queries_a = lax.ppermute(row_q, "seq", TO_SAME)
    queries_b = lax.ppermute(row_q, "seq", TO_OTHER)
    kv_received = [lax.ppermute(row_kv, "seq", pairs) for pairs in Y_SHIFTS]
    cotangent_row = gather_x(after(cotangent, row_kv))
    normed_row = gather_x(after(normed_low, row_kv))
    output_weight_f = after(output_weight, row_kv).astype(f32)
    inner_gain_f = inner_gain.astype(f32)
    inner_bias_f = inner_bias.astype(f32)
    through = jnp.concatenate(
        [
            jnp.where(
                jnp.arange(4)[:, None] == part,
                jnp.sum(output_weight_f * inner_gain_f[:, None], axis=0)[None],
                0.0,
            ),
            jnp.sum(output_weight_f * inner_bias_f[:, None], axis=0)[None],
            jnp.zeros((3, D), f32),
        ],
        axis=0,
    )
    through = through + core_swap(through)
    through = through + far_swap(through)
    vec = jnp.concatenate(
        [
            v.astype(f32)
            for v in (
                attend_gain,
                output_bias,
                feed_gain,
                feed_bias,
                down_bias,
                up_bias,
                hidden_gain,
                hidden_bias,
                inner_gain,
                inner_bias,
            )
        ]
        + [jnp.zeros((16 * D - 8 * D - 512,), f32)]
    ).reshape(16, D)
    grad_hidden = jnp.einsum(
        "td,fd->tf", after(cotangent, row_kv), down_weight, preferred_element_type=f32
    )
    plane, queries_a, queries_b, through, vec, grad_hidden, begin, info = lax.optimization_barrier(
        ([row_kv] + kv_received, queries_a, queries_b, through, vec, grad_hidden, begin, info)
    )
    out_a, out_b = attend_forward(info, queries_a, queries_b, plane, begin)
    mixed_row, logs_row, *pieces = combine(
        here, lax.ppermute(out_a, "seq", FROM_SAME), lax.ppermute(out_b, "seq", FROM_OTHER)
    )
    mixed, mine, theirs = inner(
        here, pieces[0], *shift_x(pieces), inner_gain_f[None], output_weight
    )
    chip = chip_stats(here, mine, core_swap(theirs))
    total = join_stats(here, chip, far_swap(chip))
    both, middle, before_act, inner_unit, inner_inv, sums = feed(
        here, total, core_swap(total), through, stream, vec, mixed, up_weight, grad_hidden
    )
    both_row = gather_x(both)
    sums = sums + core_swap(sums)
    sums = sums + far_swap(sums)
    hidden_low, small_a, mine, theirs, *pieces = hidden(
        here, sums, before_act, grad_hidden, vec, up_weight
    )
    slices = shift_x(pieces)
    total, other = sum_ffn(here, mine, theirs)
    feed_mine, feed_theirs = feed_out(here, hidden_low, down_weight)
    feed_chip = add_chip(here, feed_mine, core_swap(feed_theirs))
    total, other, feed_chip = lax.optimization_barrier((total, other, feed_chip))
    slices = [pieces[0]] + slices
    grad_middle, small_b, *pieces = middle_back(
        here,
        total,
        other,
        middle,
        stream,
        cotangent,
        vec,
        output_weight,
        inner_unit,
        inner_inv,
        through,
    )
    head_pieces, branch_pieces = pieces[:4], pieces[4:]
    feed_quarters = feed_quarter(here, *slices, cotangent_row, both_row)
    head_received = shift_x(head_pieces)
    feed_far = far_swap(after(feed_chip, grad_middle))
    head_received, feed_quarters, feed_far = lax.optimization_barrier(
        (head_received, feed_quarters, feed_far)
    )
    message = grad_message(here, head_pieces[0], *head_received, mixed_row, logs_row)
    feed_sums = lax.psum_scatter(
        feed_quarters, "seq", scatter_dimension=0, axis_index_groups=Y_GROUPS
    )
    message_a = lax.ppermute(message, "seq", TO_SAME)
    message_b = lax.ppermute(message, "seq", TO_OTHER)
    branch_received = shift_x(branch_pieces)
    grad_qa, grad_qb, *kv_pieces = attend_backward(
        info, queries_a, queries_b, message_a, message_b, plane, begin
    )
    kv_pieces, feed_sums, branch_received = lax.optimization_barrier(
        (kv_pieces, feed_sums, branch_received)
    )
    kv_parts = shift_y(kv_pieces)
    q_parts = [lax.ppermute(grad_qa, "seq", FROM_SAME), lax.ppermute(grad_qb, "seq", FROM_OTHER)]
    feed_pairs = sum_z(feed_sums)
    feed_total = add_far(here, feed_chip, feed_far)
    result = result_out(here, feed_total, core_swap(feed_total), middle, vec)
    row_pos = (2 * y + z) * ROW + jnp.arange(ROW, dtype=jnp.int32)
    tables = back_tables(after(row_pos, kv_pieces[0]), total_rows, score_scale)
    weight_heads = head_weights(here, after(input_weight, kv_pieces[0]))
    kv_parts, q_parts, tables, feed_pairs, weight_heads, result = lax.optimization_barrier(
        (kv_parts, q_parts, tables, feed_pairs, weight_heads, result)
    )
    feed_shared = share_yx(feed_pairs)
    projected_row, projected_sums, *pieces = row_grads(here, kv_pieces[0], *kv_parts, *q_parts, *tables)
    back_received = shift_x(pieces)
    quarter_pieces = attend_quarter(
        here,
        normed_row,
        projected_row,
        projected_sums,
        both_row,
        branch_pieces[0],
        *branch_received,
        small_a,
        small_b,
    )
    back_received, quarter_pieces = lax.optimization_barrier((back_received, quarter_pieces))
    mine, theirs = normed_back(here, pieces[0], *back_received, weight_heads)
    quarter_received = shift_y(quarter_pieces)
    total, other = sum_ffn(here, mine, theirs)
    attend_pairs = sum_z(add_four(here, quarter_pieces[0], *quarter_received))
    total, other, attend_pairs, feed_shared = lax.optimization_barrier(
        (total, other, attend_pairs, feed_shared)
    )
    attend_shared = share_yx(attend_pairs)
    grad_tokens, last = leave(here, total, other, stream, grad_middle, vec, kind)
    last = ring_sum(here, X, last, *[lax.ppermute(last, "seq", pairs) for pairs in X_SHIFTS])
    last = ring_sum(here, Y, last, *[lax.ppermute(last, "seq", pairs) for pairs in Y_SHIFTS])
    grad_type_table, grad_attend_gain, grad_attend_bias = last_sum(
        here, last, lax.ppermute(last, "seq", Z_SWAP)
    )
    grad_down_weight, grad_up_weight = feed_weights_out(feed_shared)
    grad_input_weight, grad_output_weight, *small = attend_weights_out(here, attend_shared)
    small = [v.reshape(D) for v in small]
    input_sums = small[8].reshape(4, 4, HEAD_DIM)
    return (
        result,
        grad_tokens,
        grad_type_table,
        grad_attend_gain.reshape(D),
        grad_attend_bias.reshape(D),
        grad_input_weight,
        jnp.stack([input_sums[:, k].reshape(local_width) for k in (2, 0, 1)]),
        small[7][:local_width],
        small[7][local_width : 2 * local_width],
        grad_output_weight,
        small[5],
        small[3],
        small[4],
        grad_up_weight,
        small[2],
        small[0],
        small[1],
        grad_down_weight,
        small[6],
    )


def solution(mesh):
    in_specs = (
        P("seq", None),
        P("seq"),
        P(),
        P(),
        P(),
        P(),
        P(None, None, "ffn"),
        P(None, "ffn"),
        P("ffn"),
        P("ffn"),
        P("ffn", None),
        P(),
        P(),
        P(),
        P(None, "ffn"),
        P("ffn"),
        P("ffn"),
        P("ffn"),
        P("ffn", None),
        P(),
        P("seq", None),
    )
    out_specs = (
        P("seq", None),
        P("seq", None),
        P(),
        P(),
        P(),
        P(None, None, "ffn"),
        P(None, "ffn"),
        P("ffn"),
        P("ffn"),
        P("ffn", None),
        P(),
        P(),
        P(),
        P(None, "ffn"),
        P("ffn"),
        P("ffn"),
        P("ffn"),
        P("ffn", None),
        P(),
    )
    return jax.shard_map(
        per_device, mesh=mesh, in_specs=in_specs, out_specs=out_specs, check_vma=False
    )
```

```python
from functools import partial
import math

import jax
import jax.numpy as jnp
from jax import lax
from jax.experimental import pallas as pl
from jax.experimental.pallas import tpu as pltpu
from jax.sharding import PartitionSpec as P

D = 1024
FF = 4096
HEAD_DIM = 64
ROW = 1024
PACK = ROW // 2
PLANE = 4

epsilon = 1e-05
scale_base = 512.0
masked_score = -1e30
log2_e = 1.4426950408889634
score_factor = HEAD_DIM ** (-0.5) * log2_e
highest = lax.Precision.HIGHEST
f32 = jnp.float32
bf16 = jnp.bfloat16


def seq_index(y, z, x):
    return (y % 4) * 8 + (z % 2) * 4 + x % 4


def seq_pairs(move):
    pairs = []
    for y in range(4):
        for z in range(2):
            for x in range(4):
                pairs.append((seq_index(y, z, x), seq_index(*move(y, z, x))))
    return pairs


def shift_pairs(dy, dz, dx):
    return seq_pairs(lambda y, z, x: (y + dy, z + dz, x + dx))


def group_of(row):
    return min(row, 7 - row)


TO_SAME = seq_pairs(lambda y, z, x: (group_of(2 * y + z), z, x))
TO_OTHER = seq_pairs(lambda y, z, x: (group_of(2 * y + z), 1 - z, x))
FROM_SAME = [(b, a) for a, b in TO_SAME]
FROM_OTHER = [(b, a) for a, b in TO_OTHER]
X_SHIFTS = [shift_pairs(0, 0, d) for d in (1, 2, 3)]
Y_SHIFTS = [shift_pairs(d, 0, 0) for d in (1, 2, 3)]
Z_SWAP = shift_pairs(0, 1, 0)
CORE_SWAP = [(f, f ^ 1) for f in range(4)]
FAR_SWAP = [(f, f ^ 2) for f in range(4)]
Y_GROUPS = [[seq_index(y, z, x) for y in range(4)] for z in range(2) for x in range(4)]
X_GROUPS = [[seq_index(y, z, x) for x in range(4)] for y in range(4) for z in range(2)]
Z_GROUPS = [[seq_index(y, z, x) for z in range(2)] for y in range(4) for x in range(4)]
YX_GROUPS = [[seq_index(y, z, x) for y in range(4) for x in range(4)] for z in range(2)]


def shift_x(pieces):
    return [lax.ppermute(piece, "seq", pairs) for piece, pairs in zip(pieces[1:], X_SHIFTS)]


def shift_y(pieces):
    return [lax.ppermute(piece, "seq", pairs) for piece, pairs in zip(pieces[1:], Y_SHIFTS)]


def core_swap(values):
    return lax.ppermute(values, "ffn", CORE_SWAP)


def far_swap(values):
    return lax.ppermute(values, "ffn", FAR_SWAP)


def gather_x(values):
    return lax.all_gather(values, "seq", axis_index_groups=X_GROUPS, tiled=True)


def ring(values, shifts):
    return [values] + [lax.ppermute(values, "seq", pairs) for pairs in shifts]


def sum_z(values):
    other = lax.ppermute(values, "seq", Z_SWAP)
    return (values.astype(f32) + other.astype(f32)).astype(bf16)


def after(value, *others):
    return lax.optimization_barrier((value,) + others)[0]


X, Y, Z, CORE, PART = range(5)


def run(kernel, name, here, operands, outs, scratch=(), megabytes=18):
    return pl.pallas_call(
        kernel,
        in_specs=[pl.BlockSpec(memory_space=pltpu.SMEM)]
        + [pl.BlockSpec(memory_space=pltpu.VMEM)] * len(operands),
        out_specs=[pl.BlockSpec(memory_space=pltpu.VMEM)] * len(outs),
        out_shape=[jax.ShapeDtypeStruct(shape, kind) for shape, kind in outs],
        scratch_shapes=list(scratch),
        compiler_params=pltpu.CompilerParams(vmem_limit_bytes=megabytes * 2**20),
        cost_estimate=pl.CostEstimate(
            flops=2**20,
            bytes_accessed=sum(v.size * v.dtype.itemsize for v in operands)
            + sum(math.prod(shape) * jnp.dtype(kind).itemsize for shape, kind in outs),
            transcendentals=0,
        ),
        name=name,
    )(here, *operands)


def dot_nn(a, b):
    return lax.dot_general(a, b, (((1,), (0,)), ((), ())), preferred_element_type=f32)


def dot_nt(a, b):
    return lax.dot_general(a, b, (((1,), (1,)), ((), ())), preferred_element_type=f32)


def dot_tn(a, b):
    return lax.dot_general(a, b, (((0,), (0,)), ((), ())), preferred_element_type=f32)


def before(place, d):
    return lax.rem(place + (4 - d), 4)


def store_at(refs, place, index, value):
    for d, ref in enumerate(refs):

        @pl.when(lax.rem(place + d, 4) == index)
        def _(ref=ref):
            ref[...] = value


def store_half(mine, theirs, core, half, value):
    @pl.when(core == half)
    def _():
        mine[...] = value

    @pl.when(core != half)
    def _():
        theirs[...] = value


def row_of(column):
    return jnp.broadcast_to(column, (column.shape[0], 128)).T[0:1]


def split_three(values):
    high = values.astype(bf16).astype(f32)
    middle = (values - high).astype(bf16).astype(f32)
    return high, middle, values - high - middle


def norm_parts(values):
    center = values - jnp.mean(values, axis=-1, keepdims=True)
    inv_std = lax.rsqrt(jnp.mean(center * center, axis=-1, keepdims=True) + epsilon)
    return center * inv_std, inv_std


def norm_back(grad_out, unit, inv_std, gain):
    scaled = grad_out * gain
    return inv_std * (
        scaled
        - jnp.mean(scaled, axis=-1, keepdims=True)
        - unit * jnp.mean(scaled * unit, axis=-1, keepdims=True)
    )


def pair_pack(values, side):
    left = lax.broadcasted_iota(jnp.int32, (128, 128), 1) < 64
    if side == 0:
        return jnp.where(left, values[:128], pltpu.roll(values[128:], 64, 1))
    return jnp.where(left, pltpu.roll(values[:128], 64, 1), values[128:])


def pair_unpack(even, odd):
    left = lax.broadcasted_iota(jnp.int32, (128, 128), 1) < 64
    low = jnp.where(left, even, pltpu.roll(odd, 64, 1))
    high = jnp.where(left, pltpu.roll(even, 64, 1), odd)
    return jnp.concatenate([low, high], axis=0)


def half_swapped(values):
    lane = lax.broadcasted_iota(jnp.int32, values.shape, 1)
    return jnp.where(lane % 64 < 32, pltpu.roll(values, 96, 1), pltpu.roll(values, 32, 1))


def enter_kernel(
    here, tokens, kind, table, gain, offset, weight, shift, cosine, sine, growth, stream_ref, normed_ref, *out
):
    stream = tokens[...].astype(f32)
    for c in range(3):
        stream = stream + jnp.where(kind[...] == c, table[c : c + 1, :].astype(f32), 0.0)
    stream_ref[...] = stream
    unit, _ = norm_parts(stream)
    normed = (unit * gain[...].astype(f32) + offset[...].astype(f32)).astype(bf16)
    normed_ref[...] = normed
    projected = [dot_nn(normed, weight[s]) + shift[s : s + 1, :].astype(f32) for s in range(3)]
    lane = lax.broadcasted_iota(jnp.int32, (256, 128), 1)
    left = lane < 64
    signed = jnp.where(lane % 64 < 32, -sine[...], sine[...])
    for group in range(2):
        lanes = slice(128 * group, 128 * group + 128)
        query, key, value = [p[:, lanes] for p in projected]
        query = (query * cosine[...] + half_swapped(query) * signed) * growth[...]
        key = (key * cosine[...] + half_swapped(key) * signed) / growth[...]
        for side in range(2):
            if side == 0:
                both = jnp.where(left, key, pltpu.roll(value, 64, 1))
            else:
                both = jnp.where(left, pltpu.roll(key, 64, 1), value)
            message = jnp.concatenate([both, pair_pack(query, side)], axis=0).astype(bf16)
            store_at(out, here[X], 2 * group + side, message)


def enter(here, *operands):
    return run(
        enter_kernel,
        "enter",
        here,
        operands,
        [((256, D), f32), ((256, D), bf16)] + [((384, 128), bf16)] * 4,
        megabytes=3,
    )


def rows_kernel(here, p0, p1, p2, p3, kv_ref, q_ref):
    for d, ref in enumerate((p0, p1, p2, p3)):
        source = before(here[X], d)
        kv_ref[pl.ds(pl.multiple_of(source * 256, 256), 256), :] = ref[:256, :]
        q_ref[pl.ds(pl.multiple_of(source * 128, 128), 128), :] = ref[256:, :]


def rows(here, *pieces):
    return run(rows_kernel, "rows", here, pieces, [((ROW, 128), bf16), ((PACK, 128), bf16)], megabytes=1)


def lane_rows(row):
    return jnp.concatenate([row[:, 128 * j : 128 * j + 128] for j in range(8)], axis=0)


def unpack_transposed(source, target, offset):
    for b in range(4):
        piece = source[128 * b : 128 * b + 128, :].T
        target[offset : offset + 64, 256 * b : 256 * b + 128] = piece[:64]
        target[offset : offset + 64, 256 * b + 128 : 256 * b + 256] = piece[64:]


def pack_transposed(columns, target):
    for b in range(4):
        piece = jnp.concatenate(
            [columns[:, 256 * b : 256 * b + 128], columns[:, 256 * b + 128 : 256 * b + 256]], axis=0
        )
        target[128 * b : 128 * b + 128, :] = piece.T.astype(target.dtype)


def chunk_bounds(info, tile):
    z = info[0]
    row = info[1 + tile]
    lowest = info[3 + tile]
    first = jnp.int32(0)
    last = jnp.int32(0)
    for c in range(PLANE):
        start = (2 * c + z) * ROW
        first = first + (start + ROW - 1 < lowest).astype(jnp.int32)
        last = last + (2 * c + z <= row).astype(jnp.int32)
    return first, last


def visible(info, tile, c, begin_ref, shape):
    key = (2 * c + info[0]) * ROW + lax.broadcasted_iota(jnp.int32, shape, 0)
    query = info[1 + tile] * ROW + lax.broadcasted_iota(jnp.int32, shape, 1)
    return (key <= query) & (key >= begin_ref[...])


def needs_mask(info, tile, c):
    key_row = 2 * c + info[0]
    return (key_row == info[1 + tile]) | (key_row * ROW < info[5 + tile])


def plane_copies(info, pieces, kv_ref):
    return [
        (piece, kv_ref.at[pl.ds(pl.multiple_of(before(info[7], d) * ROW, ROW), ROW)])
        for d, piece in enumerate(pieces)
    ]


def forward_kernel(
    info,
    qa,
    qb,
    kv0,
    kv1,
    kv2,
    kv3,
    begin_ref,
    outa_ref,
    outb_ref,
    qt_ref,
    q_in,
    kv_ref,
    vt_ref,
    acc_ref,
    top_ref,
    semaphores,
):
    tile = pl.program_id(0)

    @pl.when(tile == 0)
    def _():
        copies = [
            pltpu.make_async_copy(source, target, semaphores.at[k])
            for k, (source, target) in enumerate(
                [(qa, q_in.at[0]), (qb, q_in.at[1])] + plane_copies(info, (kv0, kv1, kv2, kv3), kv_ref)
            )
        ]
        for copy in copies:
            copy.start()
        for copy in copies:
            copy.wait()
        for c in range(PLANE):
            block = kv_ref[c * ROW : c * ROW + ROW, :].T
            index = lax.broadcasted_iota(jnp.int32, block.shape, 0)
            vt_ref[:, c * ROW : c * ROW + ROW] = jnp.where(index < 64, jnp.ones_like(block), block)
        qt_ref[64:, :] = jnp.zeros((64, ROW), bf16)

    unpack_transposed(q_in.at[tile], qt_ref, 0)

    top_ref[...] = jnp.full(top_ref.shape, masked_score, f32)
    acc_ref[...] = jnp.zeros(acc_ref.shape, f32)

    def step(c, masked):
        start = pl.multiple_of(c * ROW, ROW)
        scores = dot_nn(kv_ref[pl.ds(start, ROW), :], qt_ref[...]) * score_factor
        if masked:
            scores = jnp.where(visible(info, tile, c, begin_ref, scores.shape), scores, 2 * masked_score)
        old = top_ref[...]
        top = jnp.maximum(old, jnp.max(scores, axis=0, keepdims=True))
        weights = jnp.exp2(scores - top)
        top_ref[...] = top
        acc_ref[...] = acc_ref[...] * jnp.exp2(old - top) + dot_nn(
            vt_ref[:, pl.ds(start, ROW)], weights.astype(bf16)
        )

    def body(c, carry):
        masked = needs_mask(info, tile, c)

        @pl.when(masked)
        def _():
            step(c, True)

        @pl.when(jnp.logical_not(masked))
        def _():
            step(c, False)

        return carry

    first, last = chunk_bounds(info, tile)
    lax.fori_loop(first, last, body, 0)
    total = acc_ref[0:1, :]
    some = total > 0
    safe = jnp.where(some, total, 1.0)
    log_total = jnp.where(some, top_ref[...] + jnp.log2(safe), masked_score)
    for index, out_ref in enumerate((outa_ref, outb_ref)):

        @pl.when(tile == index)
        def _(out_ref=out_ref):
            pack_transposed(acc_ref[64:, :] / safe, out_ref)
            parts = [lane_rows(part) for part in split_three(log_total)]
            out_ref[PACK:, :] = jnp.concatenate(parts + [jnp.zeros((8, 128), f32)], axis=0).astype(bf16)


def attend_forward(info, queries_a, queries_b, keys_values, begin):
    hbm = pl.BlockSpec(memory_space=pltpu.HBM)
    return pl.pallas_call(
        forward_kernel,
        grid_spec=pltpu.PrefetchScalarGridSpec(
            num_scalar_prefetch=1,
            grid=(2,),
            in_specs=[hbm] * 6 + [pl.BlockSpec((1, ROW), lambda i, s: (0, i))],
            out_specs=[pl.BlockSpec((PACK + 32, 128), lambda i, s: (0, 0))] * 2,
            scratch_shapes=[
                pltpu.VMEM((128, ROW), bf16),
                pltpu.VMEM((2, PACK, 128), bf16),
                pltpu.VMEM((PLANE * ROW, 128), bf16),
                pltpu.VMEM((128, PLANE * ROW), bf16),
                pltpu.VMEM((128, ROW), f32),
                pltpu.VMEM((1, ROW), f32),
                pltpu.SemaphoreType.DMA((6,)),
            ],
        ),
        out_shape=[jax.ShapeDtypeStruct((PACK + 32, 128), bf16)] * 2,
        compiler_params=pltpu.CompilerParams(vmem_limit_bytes=9 * 2**20),
        cost_estimate=pl.CostEstimate(flops=10 * 10**9, bytes_accessed=2**21, transcendentals=0),
        name="attend_forward",
    )(info, queries_a, queries_b, *keys_values, begin)


def combine_kernel(here, a_ref, b_ref, full_ref, log_ref, *out):
    logs = []
    for ref in (a_ref, b_ref):
        rows = ref[PACK:, :].astype(f32)
        logs.append(rows[:8] + rows[8:16] + rows[16:24])
    top = jnp.maximum(logs[0], logs[1])
    shares = [jnp.exp2(part - top) for part in logs]
    total = shares[0] + shares[1]
    log_ref[...] = top + jnp.log2(total)
    columns = [(share / total).T for share in shares]
    left = lax.broadcasted_iota(jnp.int32, (128, 128), 1) < 64
    for b in range(4):
        mixed = jnp.zeros((128, 128), f32)
        for ref, column in zip((a_ref, b_ref), columns):
            weight = jnp.where(left, column[:, 2 * b : 2 * b + 1], column[:, 2 * b + 1 : 2 * b + 2])
            mixed = mixed + weight * ref[128 * b : 128 * b + 128, :].astype(f32)
        full_ref[128 * b : 128 * b + 128, :] = mixed
        store_at(out, here[X], b, mixed.astype(bf16))


def combine(here, part_a, part_b):
    return run(
        combine_kernel,
        "combine",
        here,
        (part_a, part_b),
        [((PACK, 128), f32), ((8, 128), f32)] + [((128, 128), bf16)] * 4,
        megabytes=1,
    )


def grad_message_kernel(here, p0, p1, p2, p3, mixed_ref, log_ref, out_ref):
    for d, ref in enumerate((p0, p1, p2, p3)):
        out_ref[pl.ds(pl.multiple_of(before(here[X], d) * 128, 128), 128), :] = ref[...]
    deltas = []
    for b in range(4):
        rows = slice(128 * b, 128 * b + 128)
        each = (out_ref[rows, :].astype(f32) * mixed_ref[rows, :]).T
        deltas.append(jnp.sum(each[:64], axis=0, keepdims=True))
        deltas.append(jnp.sum(each[64:], axis=0, keepdims=True))
    parts = list(split_three(log_ref[...])) + list(split_three(jnp.concatenate(deltas, axis=0)))
    out_ref[PACK:, :] = jnp.concatenate(parts, axis=0).astype(bf16)


def grad_message(here, *operands):
    return run(grad_message_kernel, "grad_message", here, operands, [((PACK + 48, 128), bf16)], megabytes=1)[0]


def backward_kernel(
    info,
    qa,
    qb,
    ma,
    mb,
    kv0,
    kv1,
    kv2,
    kv3,
    begin_ref,
    dqa_ref,
    dqb_ref,
    own_ref,
    one_ref,
    two_ref,
    three_ref,
    qt_ref,
    gt_ref,
    q_ref,
    g_ref,
    kv_ref,
    kt_ref,
    row_ref,
    acc_ref,
    dq_acc,
    q_in,
    m_in,
    semaphores,
):
    tile = pl.program_id(0)

    def load(query_ref, message_ref):
        unpack_transposed(query_ref, qt_ref, 0)
        unpack_transposed(message_ref, gt_ref, 64)
        q_ref[...] = qt_ref[...].T
        g_ref[...] = gt_ref[...].T
        rows = message_ref[PACK:, :].astype(f32)
        for k in range(2):
            part = rows[24 * k : 24 * k + 8] + rows[24 * k + 8 : 24 * k + 16] + rows[24 * k + 16 : 24 * k + 24]
            for j in range(8):
                row_ref[k : k + 1, 128 * j : 128 * j + 128] = part[j : j + 1, :]

    @pl.when(tile == 0)
    def _():
        copies = [
            pltpu.make_async_copy(source, target, semaphores.at[k])
            for k, (source, target) in enumerate(
                [(qa, q_in.at[0]), (qb, q_in.at[1]), (ma, m_in.at[0]), (mb, m_in.at[1])]
                + plane_copies(info, (kv0, kv1, kv2, kv3), kv_ref)
            )
        ]
        for copy in copies:
            copy.start()
        acc_ref[...] = jnp.zeros(acc_ref.shape, f32)
        qt_ref[64:, :] = jnp.zeros((64, ROW), bf16)
        gt_ref[:64, :] = jnp.zeros((64, ROW), bf16)
        for copy in copies:
            copy.wait()
        for c in range(PLANE):
            kt_ref[:, c * ROW : c * ROW + ROW] = kv_ref[c * ROW : c * ROW + ROW, :].T

    load(q_in.at[tile], m_in.at[tile])
    dq_acc[...] = jnp.zeros(dq_acc.shape, f32)

    def step(c, masked):
        start = pl.multiple_of(c * ROW, ROW)
        block = kv_ref[pl.ds(start, ROW), :]
        scores = dot_nn(block, qt_ref[...]) * score_factor
        if masked:
            scores = jnp.where(visible(info, tile, c, begin_ref, scores.shape), scores, 2 * masked_score)
        weights = jnp.exp2(scores - row_ref[0:1, :])
        grad_weights = dot_nn(block, gt_ref[...])
        grad_scores = (weights * (grad_weights - row_ref[1:2, :])).astype(bf16)
        acc_ref[pl.ds(start, ROW), :] += dot_nn(grad_scores, q_ref[...]) + dot_nn(
            weights.astype(bf16), g_ref[...]
        )
        dq_acc[...] += dot_nn(kt_ref[:, pl.ds(start, ROW)], grad_scores)

    def body(c, carry):
        masked = needs_mask(info, tile, c)

        @pl.when(masked)
        def _():
            step(c, True)

        @pl.when(jnp.logical_not(masked))
        def _():
            step(c, False)

        return carry

    first, last = chunk_bounds(info, tile)
    lax.fori_loop(first, last, body, 0)

    @pl.when(tile == 0)
    def _():
        pack_transposed(dq_acc[:64, :], dqa_ref)

    @pl.when(tile == 1)
    def _():
        pack_transposed(dq_acc[:64, :], dqb_ref)
        for d, ref in enumerate((own_ref, one_ref, two_ref, three_ref)):
            start = pl.multiple_of(lax.rem(info[7] + d, 4) * ROW, ROW)
            ref[...] = acc_ref[pl.ds(start, ROW), :].astype(bf16)


def attend_backward(info, queries_a, queries_b, message_a, message_b, keys_values, begin):
    packed = pl.BlockSpec((PACK, 128), lambda i, s: (0, 0))
    hbm = pl.BlockSpec(memory_space=pltpu.HBM)
    block = pl.BlockSpec((ROW, 128), lambda i, s: (0, 0))
    return pl.pallas_call(
        backward_kernel,
        grid_spec=pltpu.PrefetchScalarGridSpec(
            num_scalar_prefetch=1,
            grid=(2,),
            in_specs=[hbm] * 8 + [pl.BlockSpec((1, ROW), lambda i, s: (0, i))],
            out_specs=[packed] * 2 + [block] * 4,
            scratch_shapes=[
                pltpu.VMEM((128, ROW), bf16),
                pltpu.VMEM((128, ROW), bf16),
                pltpu.VMEM((ROW, 128), bf16),
                pltpu.VMEM((ROW, 128), bf16),
                pltpu.VMEM((PLANE * ROW, 128), bf16),
                pltpu.VMEM((128, PLANE * ROW), bf16),
                pltpu.VMEM((8, ROW), f32),
                pltpu.VMEM((PLANE * ROW, 128), f32),
                pltpu.VMEM((128, ROW), f32),
                pltpu.VMEM((2, PACK, 128), bf16),
                pltpu.VMEM((2, PACK + 48, 128), bf16),
                pltpu.SemaphoreType.DMA((8,)),
            ],
        ),
        out_shape=[jax.ShapeDtypeStruct((PACK, 128), bf16)] * 2
        + [jax.ShapeDtypeStruct((ROW, 128), bf16)] * 4,
        compiler_params=pltpu.CompilerParams(vmem_limit_bytes=16 * 2**20),
        cost_estimate=pl.CostEstimate(flops=18 * 10**9, bytes_accessed=2**22, transcendentals=0),
        name="attend_backward",
    )(info, queries_a, queries_b, message_a, message_b, *keys_values, begin)


def inner_kernel(here, p0, p1, p2, p3, gain, shift, weight, mixed_ref, mine, theirs, heads):
    for d, ref in enumerate((p0, p1, p2, p3)):
        heads[before(here[X], d)] = ref[...].astype(f32)
    mixed = jnp.concatenate([pair_unpack(heads[0], heads[1]), pair_unpack(heads[2], heads[3])], axis=1)
    mixed_ref[...] = mixed
    mean = jnp.mean(mixed, axis=-1, keepdims=True)
    centred = mixed - mean
    spread = jnp.sum(centred * centred, axis=-1, keepdims=True)
    gains = gain[...].astype(f32)
    projected = dot_nn((centred * gains).astype(bf16), weight[...])
    full = weight[...].astype(f32)
    gain_column = jnp.broadcast_to(gains, (128, 256)).T[:, 0:1]
    shift_column = jnp.broadcast_to(shift[...].astype(f32), (128, 256)).T[:, 0:1]
    through = jnp.sum(full * gain_column, axis=0, keepdims=True)
    vectors = [jnp.where(here[PART] == k, through, 0.0) for k in range(4)]
    vectors.append(jnp.sum(full * shift_column, axis=0, keepdims=True))
    for half in range(2):
        tokens = slice(128 * half, 128 * half + 128)
        stats = [row_of(mean[tokens]), row_of(spread[tokens])]
        slots = [jnp.where(here[PART] == j // 2, stats[j % 2], 0.0) for j in range(8)]
        rows = vectors + [jnp.concatenate(slots, axis=1), jnp.zeros((2, D), f32)]
        store_half(mine, theirs, here[CORE], half, jnp.concatenate([projected[tokens]] + rows, axis=0))


def inner(here, *operands):
    return run(
        inner_kernel,
        "inner",
        here,
        operands,
        [((256, 256), f32), ((136, D), f32), ((136, D), f32)],
        [pltpu.VMEM((4, 128, 128), f32)],
        megabytes=4,
    )


def chip_stats_kernel(here, mine, other, out):
    total = mine[...] + other[...]
    parts = list(split_three(total[128:])) + [jnp.zeros((8, D), f32)]
    out[...] = jnp.concatenate([total[:128]] + parts, axis=0).astype(bf16)


def join_stats_kernel(here, chip, far, out):
    total = chip[...].astype(f32) + far[...].astype(f32)
    out[...] = jnp.concatenate([total[:128], total[128:136] + total[136:144] + total[144:152]], axis=0)


def add_chip_kernel(here, mine, other, out):
    out[...] = (mine[...] + other[...]).astype(bf16)


def add_far_kernel(here, chip, far, out):
    out[...] = chip[...].astype(f32) + far[...].astype(f32)


def chip_stats(here, mine, other):
    return run(chip_stats_kernel, "chip_stats", here, (mine, other), [((160, D), bf16)], megabytes=1)[0]


def join_stats(here, chip, far):
    return run(join_stats_kernel, "join_stats", here, (chip, far), [((136, D), f32)], megabytes=1)[0]


def add_chip(here, mine, other):
    return run(add_chip_kernel, "add_chip", here, (mine, other), [((128, D), bf16)], megabytes=1)[0]


def add_far(here, chip, far):
    return run(add_far_kernel, "add_far", here, (chip, far), [((128, D), f32)], megabytes=1)[0]


def sum_ffn(here, mine, theirs):
    chip = add_chip(here, mine, core_swap(theirs))
    total = add_far(here, chip, far_swap(chip))
    return total, core_swap(total)


def gauss_share(values):
    return 0.5 + 0.5 * lax.erf(values * math.sqrt(0.5))


def feed_kernel(
    here,
    total,
    other,
    stream,
    vec,
    mixed_ref,
    weight,
    grad_hidden,
    low_ref,
    inner_ref,
    middle_ref,
    before_ref,
    unit_ref,
    inv_ref,
    sums_ref,
    vectors_ref,
    halves,
):
    halves[here[CORE]] = total[...]
    halves[1 - here[CORE]] = other[...]
    vectors = halves[0, 128:, :]
    vectors_ref[...] = vectors
    ending = vectors[4:5, :] + vec[OUTPUT_BIAS : OUTPUT_BIAS + 1, :]
    inner_gain = vec[INNER : INNER + 1, :256]
    inner_bias = vec[INNER : INNER + 1, 256:512]
    for half in range(2):
        tokens = slice(128 * half, 128 * half + 128)
        stats = jnp.concatenate([halves[half, 133:134, 128 * j : 128 * j + 128] for j in range(8)], axis=0).T
        means = [stats[:, 2 * k : 2 * k + 1] for k in range(4)]
        mean = (means[0] + means[1] + means[2] + means[3]) * 0.25
        spread = stats[:, 1:2] + stats[:, 3:4] + stats[:, 5:6] + stats[:, 7:8]
        projected = halves[half, :128, :]
        for k in range(4):
            move = means[k] - mean
            spread = spread + 256.0 * move * move
            projected = projected + move * vectors[k : k + 1, :]
        inv = lax.rsqrt(spread / D + epsilon)
        middle_ref[tokens, :] = stream[tokens, :] + projected * inv + ending
        unit = (mixed_ref[tokens, :] - mean) * inv
        unit_ref[tokens, :] = unit
        inv_ref[tokens, :] = jnp.broadcast_to(inv, (128, 128))
        inner_ref[tokens, :] = (unit * inner_gain + inner_bias).astype(bf16)
    unit, _ = norm_parts(middle_ref[...])
    low_ref[...] = (
        unit * vec[FEED_GAIN : FEED_GAIN + 1, :] + vec[FEED_BIAS : FEED_BIAS + 1, :]
    ).astype(bf16)
    before_act = dot_nn(low_ref[...], weight[...]) + vec[UP_BIAS : UP_BIAS + 1, :]
    before_ref[...] = before_act
    active = before_act * gauss_share(before_act)
    scaled = grad_hidden[...] * vec[HIDDEN_GAIN : HIDDEN_GAIN + 1, :]
    columns = [
        jnp.sum(part, axis=-1, keepdims=True) for part in (active, active * active, scaled, scaled * active)
    ]
    lane = lax.broadcasted_iota(jnp.int32, (256, 128), 1)
    spread = jnp.zeros((256, 128), f32)
    for k, column in enumerate(columns):
        spread = jnp.where(lane == k, column, spread)
    sums_ref[...] = spread.T[:8]


def feed(here, *operands):
    return run(
        feed_kernel,
        "feed",
        here,
        operands,
        [
            ((256, D), bf16),
            ((256, 256), bf16),
            ((256, D), f32),
            ((256, D), f32),
            ((256, 256), f32),
            ((256, 128), f32),
            ((8, 256), f32),
            ((8, D), f32),
        ],
        [pltpu.VMEM((2, 136, D), f32)],
        megabytes=6,
    )


def hidden_kernel(
    here, sums, before_ref, grad_hidden, vec, weight, low_ref, grad_ref, small_ref, mine, theirs
):
    before_act = before_ref[...]
    share = gauss_share(before_act)
    slope = share + before_act * jnp.exp(-0.5 * before_act * before_act) * (1.0 / math.sqrt(2.0 * math.pi))
    columns = sums[...].T
    mean = columns[:, 0:1] / FF
    inv = lax.rsqrt(columns[:, 1:2] / FF - mean * mean + epsilon)
    first = columns[:, 2:3]
    cross = inv * (columns[:, 3:4] - mean * first)
    gain = vec[HIDDEN_GAIN : HIDDEN_GAIN + 1, :]
    unit = (before_act * share - mean) * inv
    low_ref[...] = (unit * gain + vec[HIDDEN_BIAS : HIDDEN_BIAS + 1, :]).astype(bf16)
    grad_out = grad_hidden[...]
    grad_pre = (inv * (grad_out * gain - first / FF - unit * (cross / FF)) * slope).astype(bf16)
    small_ref[0:1, :] = jnp.sum(grad_out * unit, axis=0, keepdims=True)
    small_ref[1:2, :] = jnp.sum(grad_out, axis=0, keepdims=True)
    small_ref[2:3, :] = jnp.sum(grad_pre.astype(f32), axis=0, keepdims=True)
    small_ref[3:, :] = jnp.zeros((5, D), f32)
    grad_ref[...] = grad_pre
    back = dot_nt(grad_pre, weight[...])
    for half in range(2):
        store_half(mine, theirs, here[CORE], half, back[128 * half : 128 * half + 128])


def hidden(here, *operands):
    return run(
        hidden_kernel,
        "hidden",
        here,
        operands,
        [((256, D), bf16), ((256, D), bf16), ((8, D), f32), ((128, D), f32), ((128, D), f32)],
        megabytes=6,
    )


def feed_out_kernel(here, low_ref, weight, mine, theirs):
    for half in range(2):
        tokens = slice(128 * half, 128 * half + 128)
        store_half(mine, theirs, here[CORE], half, dot_nn(low_ref[tokens, :], weight[...]))


def feed_out(here, low, weight):
    return run(
        feed_out_kernel, "feed_out", here, (low, weight), [((128, D), f32), ((128, D), f32)], megabytes=2
    )


def result_kernel(here, total, other, middle, vec, out, halves):
    halves[here[CORE]] = total[...]
    halves[1 - here[CORE]] = other[...]
    for half in range(2):
        tokens = slice(128 * half, 128 * half + 128)
        out[tokens, :] = (
            middle[tokens, :] + halves[half] + vec[DOWN_BIAS : DOWN_BIAS + 1, :]
        ).astype(bf16)


def result_out(here, *operands):
    return run(
        result_kernel,
        "result",
        here,
        operands,
        [((256, D), bf16)],
        [pltpu.VMEM((2, 128, D), f32)],
        megabytes=4,
    )[0]


def feed_grads_kernel(here, low, cotangent, grad_pre, feed_low, inner_low, branch, small_a, small_b, out):
    grads = dot_tn(inner_low[...], branch[...])
    vectors = [small_a[k : k + 1, :] for k in range(3)] + [small_b[k : k + 1, :] for k in range(5)]
    for k in range(4):
        lanes = slice(256 * k, 256 * k + 256)
        parts = [dot_tn(low[:, lanes], cotangent[...]), dot_tn(grad_pre[:, lanes], feed_low[...])]
        parts += [grads[64 * k : 64 * k + 64], vectors[2 * k], vectors[2 * k + 1], jnp.zeros((14, D), f32)]
        out[k] = jnp.concatenate(parts, axis=0).astype(bf16)


def feed_grads(here, *operands):
    return run(feed_grads_kernel, "feed_grads", here, operands, [((4, 592, D), bf16)], megabytes=8)[0]


def blocks_kernel(here, total, *out):
    for k in range(4):
        store_at(out, here[Y], k, total[:, 256 * k : 256 * k + 256])


def blocks(here, total):
    return run(blocks_kernel, "blocks", here, (total,), [((total.shape[0], 256), bf16)] * 4, megabytes=2)


def pair_kernel(here, p0, p1, p2, p3, out):
    total = p0[...].astype(f32) + p1[...].astype(f32) + p2[...].astype(f32) + p3[...].astype(f32)
    out[...] = jnp.concatenate([total[:256], total[256:512].T, total[512:]], axis=0).astype(bf16)


def pair(here, *pieces):
    return run(pair_kernel, "pair", here, pieces, [((592, 256), bf16)], megabytes=3)[0]


def middle_back_kernel(
    here,
    total,
    other,
    middle,
    stream,
    cotangent,
    vec,
    weight,
    unit_ref,
    inv_ref,
    vectors,
    grad_ref,
    small_ref,
    h0,
    h1,
    h2,
    h3,
    low_ref,
    halves,
):
    halves[here[CORE]] = total[...]
    halves[1 - here[CORE]] = other[...]
    grad_feed = jnp.concatenate([halves[0], halves[1]], axis=0)
    unit, inv = norm_parts(middle[...])
    grad_result = cotangent[...].astype(f32)
    grad_middle = grad_result + norm_back(grad_feed, unit, inv, vec[FEED_GAIN : FEED_GAIN + 1, :])
    grad_ref[...] = grad_middle
    low = grad_middle.astype(bf16)
    branch = low.astype(f32)
    low_ref[...] = low
    grad_inner = dot_nt(low, weight[...])
    through = vectors[0:1, :] + vectors[1:2, :] + vectors[2:3, :] + vectors[3:4, :]
    first = jnp.sum(branch * through, axis=-1, keepdims=True)
    ending = vectors[4:5, :] + vec[OUTPUT_BIAS : OUTPUT_BIAS + 1, :]
    cross = jnp.sum(branch * (middle[...] - stream[...] - ending), axis=-1, keepdims=True)
    inner_unit = unit_ref[...]
    inner_inv = inv_ref[:, 0:1]
    grad_mixed = inner_inv * (
        grad_inner * vec[INNER : INNER + 1, :256] - first / D - inner_unit * (cross / D)
    )
    for group in range(2):
        lanes = grad_mixed[:, 128 * group : 128 * group + 128]
        for side in range(2):
            store_at((h0, h1, h2, h3), here[X], 2 * group + side, pair_pack(lanes, side).astype(bf16))
    small_ref[0:1, :] = jnp.sum(grad_feed * unit, axis=0, keepdims=True)
    small_ref[1:2, :] = jnp.sum(grad_feed, axis=0, keepdims=True)
    small_ref[2:3, :] = jnp.sum(branch, axis=0, keepdims=True)
    small_ref[3:4, :] = jnp.sum(grad_result, axis=0, keepdims=True)
    small_ref[4:5, :256] = jnp.sum(grad_inner * inner_unit, axis=0, keepdims=True)
    small_ref[4:5, 256:512] = jnp.sum(grad_inner, axis=0, keepdims=True)
    small_ref[4:5, 512:] = jnp.zeros((1, 512), f32)
    small_ref[5:, :] = jnp.zeros((3, D), f32)


def middle_back(here, *operands):
    return run(
        middle_back_kernel,
        "middle_back",
        here,
        operands,
        [((256, D), f32), ((8, D), f32)] + [((128, 128), bf16)] * 4 + [((256, D), bf16)],
        [pltpu.VMEM((2, 128, D), f32)],
        megabytes=8,
    )


def row_grads_kernel(
    here, own, one, two, three, qa, qb, cos_in, sin_in, out_ref, sums_ref, p0, p1, p2, p3
):
    left = lax.broadcasted_iota(jnp.int32, (128, 128), 1) < 64

    def turned(values, cos_part, sin_part):
        return (values * cos_part + half_swapped(values) * sin_part).astype(bf16)

    for b in range(8):
        rows = slice(128 * b, 128 * b + 128)
        total = own[rows, :].astype(f32)
        for ref in (one, two, three):
            total = total + ref[rows, :].astype(f32)
        out_ref[rows, :128] = turned(
            total, jnp.where(left, cos_in[rows, :], 1.0), jnp.where(left, sin_in[rows, :], 0.0)
        )
    for b in range(4):
        rows = slice(128 * b, 128 * b + 128)
        total = qa[rows, :].astype(f32) + qb[rows, :].astype(f32)
        for side in range(2):
            tokens = slice(256 * b + 128 * side, 256 * b + 128 * side + 128)
            values = total if side == 0 else pltpu.roll(total, 64, 1)
            values = jnp.where(left, values, 0.0)
            out_ref[tokens, 128:] = turned(
                values, pltpu.roll(cos_in[tokens, :], 64, 1), pltpu.roll(sin_in[tokens, :], 64, 1)
            )
    for b in range(4):
        store_at((p0, p1, p2, p3), here[X], b, out_ref[256 * b : 256 * b + 256, :])
    sums_ref[...] = jnp.broadcast_to(jnp.sum(out_ref[...].astype(f32), axis=0, keepdims=True), (8, 256))


def row_grads(here, *operands):
    return run(
        row_grads_kernel,
        "row_grads",
        here,
        operands,
        [((ROW, 256), bf16), ((8, 256), f32)] + [((256, 256), bf16)] * 4,
        megabytes=3,
    )


def head_weights_kernel(here, weight, out):
    left = lax.broadcasted_iota(jnp.int32, (256, 128), 1) < 64
    for r in range(4):
        rows = slice(256 * r, 256 * r + 256)
        for group in range(2):
            lanes = slice(128 * group, 128 * group + 128)
            query, key, value = [weight[s, rows, lanes].astype(f32) for s in range(3)]
            even = [jnp.where(left, key, pltpu.roll(value, 64, 1)), jnp.where(left, query, 0.0)]
            odd = [
                jnp.where(left, pltpu.roll(key, 64, 1), value),
                jnp.where(left, pltpu.roll(query, 64, 1), 0.0),
            ]
            for side, parts in enumerate((even, odd)):
                out[2 * group + side, rows, :] = jnp.concatenate(parts, axis=1).astype(bf16)


def head_weights(here, weight):
    return run(head_weights_kernel, "head_weights", here, (weight,), [((4, D, 256), bf16)], megabytes=2)[0]


def normed_back_kernel(here, p0, p1, p2, p3, weight, mine, theirs):
    for half in range(2):
        total = jnp.zeros((128, D), f32)
        for d, ref in enumerate((p0, p1, p2, p3)):
            total = total + dot_nt(ref[128 * half : 128 * half + 128, :], weight[before(here[X], d)])
        store_half(mine, theirs, here[CORE], half, total)


def normed_back(here, *operands):
    return run(
        normed_back_kernel, "normed_back", here, operands, [((128, D), f32), ((128, D), f32)], megabytes=2
    )


def attend_quarter_kernel(here, normed, projected, sums, *out):
    grad_input = dot_tn(projected[...], normed[...])
    left = lax.broadcasted_iota(jnp.int32, (64, 128), 1) < 64
    for y in range(4):
        parts = []
        for z in range(2):
            tall = grad_input[:, 256 * y + 128 * z : 256 * y + 128 * z + 128].T
            query = jnp.where(left, tall[:64, 128:], pltpu.roll(tall[64:, 128:], 64, 1))
            last = jnp.zeros((16, 128), f32)
            if y == 0 and z == 0:
                last = jnp.concatenate([sums[0:1, :128], sums[0:1, 128:], last[:14]], axis=0)
            parts.append(jnp.concatenate([tall[:, :128], query, last], axis=0).astype(bf16)[None])
        store_at(out, here[Y], y, jnp.concatenate(parts, axis=0))


def attend_quarter(here, *operands):
    return run(attend_quarter_kernel, "attend_quarter", here, operands, [((2, 208, 128), bf16)] * 4, megabytes=5)


def add_four_kernel(here, p0, p1, p2, p3, out):
    total = p0[...].astype(f32) + p1[...].astype(f32) + p2[...].astype(f32) + p3[...].astype(f32)
    out[...] = total.astype(bf16)


def add_four(here, *pieces):
    return run(add_four_kernel, "add_four", here, pieces, [(pieces[0].shape, bf16)], megabytes=1)[0]


def feed_weights_kernel(here, shared, down, up, output_ref, *rest):
    small_refs, (blocks, semaphores) = rest[:8], rest[8:]
    copies = []
    for y in range(4):
        for x in range(4):
            for i in range(2):
                slot = 8 * y + 2 * x + i
                blocks[slot] = shared[y, x, 256 * i : 256 * i + 256, :].astype(f32)
                y_side, x_side = pl.ds(256 * y, 256), pl.ds(256 * x, 256)
                target = up.at[y_side, x_side] if i else down.at[x_side, y_side]
                copy = pltpu.make_async_copy(blocks.at[slot], target, semaphores.at[slot])
                copy.start()
                copies.append(copy)
    for x in range(4):
        tail = jnp.concatenate([shared[y, x, 512:, :].astype(f32) for y in range(4)], axis=1)
        output_ref[64 * x : 64 * x + 64, :] = tail[:64]
        for k in range(2):
            small_refs[2 * x + k][...] = tail[64 + k : 65 + k]
    for copy in copies:
        copy.wait()


def feed_weights_out(here, shared):
    return pl.pallas_call(
        feed_weights_kernel,
        in_specs=[pl.BlockSpec(memory_space=pltpu.SMEM), pl.BlockSpec(memory_space=pltpu.VMEM)],
        out_specs=[pl.BlockSpec(memory_space=pl.ANY)] * 2 + [pl.BlockSpec(memory_space=pltpu.VMEM)] * 9,
        out_shape=[jax.ShapeDtypeStruct((D, D), f32)] * 2
        + [jax.ShapeDtypeStruct((256, D), f32)]
        + [jax.ShapeDtypeStruct((1, D), f32)] * 8,
        scratch_shapes=[pltpu.VMEM((32, 256, 256), f32), pltpu.SemaphoreType.DMA((32,))],
        compiler_params=pltpu.CompilerParams(vmem_limit_bytes=13 * 2**20),
        cost_estimate=pl.CostEstimate(flops=1, bytes_accessed=1, transcendentals=0),
        name="feed_weights",
    )(here, shared)


def attend_weights_kernel(here, *refs):
    parts, (input_ref, bias_ref), shared = refs[:4], refs[4:6], refs[6]
    for dx, ref in enumerate(parts):
        for dy in range(4):
            shared[before(here[Y], dy), before(here[X], dx)] = ref[dy]
    for y in range(4):
        for z in range(2):
            rows = slice(256 * y + 128 * z, 256 * y + 128 * z + 128)
            blocks = [shared[y, x, z].astype(f32) for x in range(4)]
            queries = [jnp.concatenate([b[128:192, :64], b[128:192, 64:]], axis=0) for b in blocks]
            input_ref[0, rows, :] = jnp.concatenate(queries, axis=1)
            input_ref[1, rows, :] = jnp.concatenate([b[:128, :64] for b in blocks], axis=1)
            input_ref[2, rows, :] = jnp.concatenate([b[:128, 64:] for b in blocks], axis=1)
            if y == 0 and z == 0:
                bias_ref[0:1, :] = jnp.concatenate([b[193:194, :64] for b in blocks], axis=1)
                bias_ref[1:2, :] = jnp.concatenate([b[192:193, :64] for b in blocks], axis=1)
                bias_ref[2:3, :] = jnp.concatenate([b[192:193, 64:] for b in blocks], axis=1)


def attend_weights_out(here, *operands):
    return run(
        attend_weights_kernel,
        "attend_weights",
        here,
        operands,
        [((3, D, 256), f32), ((3, 256), f32)],
        [pltpu.VMEM((4, 4, 2, 208, 128), bf16)],
        megabytes=9,
    )


def leave_kernel(here, total, other, stream, grad_middle, vec, kind, out_ref, last_ref, halves):
    halves[here[CORE]] = total[...]
    halves[1 - here[CORE]] = other[...]
    grad_normed = jnp.concatenate([halves[0], halves[1]], axis=0)
    unit, inv = norm_parts(stream[...])
    grad = grad_middle[...] + norm_back(grad_normed, unit, inv, vec[ATTEND_GAIN : ATTEND_GAIN + 1, :])
    out_ref[...] = grad
    last_ref[0:1, :] = jnp.sum(grad_normed * unit, axis=0, keepdims=True)
    last_ref[1:2, :] = jnp.sum(grad_normed, axis=0, keepdims=True)
    for c in range(3):
        last_ref[2 + c : 3 + c, :] = jnp.sum(jnp.where(kind[...] == c, grad, 0.0), axis=0, keepdims=True)
    last_ref[5:, :] = jnp.zeros((3, D), f32)


def leave(here, *operands):
    return run(
        leave_kernel,
        "leave",
        here,
        operands,
        [((256, D), f32), ((8, D), f32)],
        [pltpu.VMEM((2, 128, D), f32)],
        megabytes=7,
    )


def ring_sum_kernel(axis, here, p0, p1, p2, p3, out, ring):
    for d, ref in enumerate((p0, p1, p2, p3)):
        ring[before(here[axis], d)] = ref[...]
    out[...] = ring[0] + ring[1] + ring[2] + ring[3]


def ring_sum(here, axis, *pieces):
    return run(
        partial(ring_sum_kernel, axis),
        "ring_sum",
        here,
        pieces,
        [((8, D), f32)],
        [pltpu.VMEM((4, 8, D), f32)],
        megabytes=1,
    )[0]


def last_sum_kernel(here, own, other, table_ref, gain_ref, bias_ref):
    total = own[...] + other[...]
    gain_ref[...] = total[0:1]
    bias_ref[...] = total[1:2]
    table_ref[...] = total[2:5]


def last_sum(here, own, other):
    return run(
        last_sum_kernel,
        "last_sum",
        here,
        (own, other),
        [((3, D), f32), ((1, D), f32), ((1, D), f32)],
        megabytes=1,
    )


ATTEND_GAIN, OUTPUT_BIAS, FEED_GAIN, FEED_BIAS, DOWN_BIAS, UP_BIAS, HIDDEN_GAIN, HIDDEN_BIAS, INNER = range(9)


def tables_of(positions, total_rows):
    pair_index = (jnp.arange(128) % 32).astype(f32)
    frequency = 1.0 / 10000.0 ** (pair_index / 32)
    angles = positions.astype(f32)[:, None] * frequency[None, :]
    ratios = (2.0 * pair_index + 0.4 * HEAD_DIM) / (1.4 * HEAD_DIM)
    exponent = (positions - total_rows // 2).astype(f32)[:, None] / scale_base
    return jnp.cos(angles), jnp.sin(angles), ratios[None, :] ** exponent


def back_tables(positions, total_rows, score_scale):
    lane = jnp.arange(128)
    cosine, sine, growth = tables_of(positions, total_rows)
    cosine = cosine * score_scale
    sine = sine * jnp.where(lane % 64 < 32, score_scale, -score_scale)[None]
    turned = (lane < 64)[None]
    factor = jnp.where(turned, 1.0 / growth, growth)
    return cosine * factor, sine * factor


def per_device(
    tokens,
    segment_kind,
    document,
    type_table,
    attend_gain,
    attend_bias,
    input_weight,
    input_bias,
    inner_gain,
    inner_bias,
    output_weight,
    output_bias,
    feed_gain,
    feed_bias,
    up_weight,
    up_bias,
    hidden_gain,
    hidden_bias,
    down_weight,
    down_bias,
    cotangent,
):
    local_rows = tokens.shape[0]
    total_rows = document.shape[0]
    local_width = input_weight.shape[2]
    score_scale = HEAD_DIM ** (-0.5)
    place = lax.axis_index("seq")
    part = lax.axis_index("ffn")
    y, z, x = place // 8, (place // 4) % 2, place % 4
    here = jnp.stack([x, y, z, part % 2, part, part, part, part]).astype(jnp.int32)
    query_pos = place * local_rows + jnp.arange(local_rows, dtype=jnp.int32)
    kind = segment_kind[:, None]

    stream, normed_low, *pieces = enter(
        here,
        tokens,
        kind,
        type_table,
        attend_gain[None],
        attend_bias[None],
        input_weight,
        input_bias,
        *tables_of(query_pos, total_rows),
    )
    received = shift_x(pieces)

    row_kv, row_q = rows(here, pieces[0], *received)
    queries_a = lax.ppermute(row_q, "seq", TO_SAME)
    queries_b = lax.ppermute(row_q, "seq", TO_OTHER)
    kv_received = [lax.ppermute(row_kv, "seq", pairs) for pairs in Y_SHIFTS]

    normed_row = gather_x(after(normed_low, row_kv))

    document = after(document, queries_a)
    begins = jnp.zeros((total_rows,), jnp.int32)
    for number in range(1, 4):
        begins = begins + jnp.where(
            document >= number, jnp.sum((document == number - 1).astype(jnp.int32)), 0
        )
    row_a = jnp.where(y % 2 == z, y, 7 - y)
    row_b = 7 - row_a
    begin_a = lax.dynamic_slice_in_dim(begins, row_a * ROW, ROW)
    begin_b = lax.dynamic_slice_in_dim(begins, row_b * ROW, ROW)
    begin = jnp.concatenate([begin_a, begin_b])[None]
    info = jnp.stack([z, row_a, row_b, begin_a[0], begin_b[0], begin_a[-1], begin_b[-1], y]).astype(
        jnp.int32
    )
    vec = jnp.concatenate(
        [
            v.astype(f32)
            for v in (
                attend_gain,
                output_bias,
                feed_gain,
                feed_bias,
                down_bias,
                up_bias,
                hidden_gain,
                hidden_bias,
                inner_gain,
                inner_bias,
            )
        ]
        + [jnp.zeros((16 * D - 8 * D - 512,), f32)]
    ).reshape(16, D)
    plane, queries_a, queries_b, vec, begin, info = lax.optimization_barrier(
        ([row_kv] + kv_received, queries_a, queries_b, vec, begin, info)
    )
    out_a, out_b = attend_forward(info, queries_a, queries_b, plane, begin)
    part_a = lax.ppermute(out_a, "seq", FROM_SAME)
    part_b = lax.ppermute(out_b, "seq", FROM_OTHER)
    mixed_row, logs_row, *pieces = combine(here, part_a, part_b)
    mixed, mine, theirs = inner(
        here, pieces[0], *shift_x(pieces), inner_gain[None], inner_bias[None], output_weight
    )
    chip = chip_stats(here, mine, core_swap(theirs))
    row_pos = (2 * y + z) * ROW + jnp.arange(ROW, dtype=jnp.int32)
    tables = back_tables(after(row_pos, chip), total_rows, score_scale)
    grad_hidden = jnp.einsum("td,fd->tf", after(cotangent, chip), down_weight, preferred_element_type=f32)
    total = join_stats(here, chip, far_swap(chip))
    total, tables, grad_hidden = lax.optimization_barrier((total, tables, grad_hidden))
    feed_low, inner_low, middle, before_act, inner_unit, inner_inv, sums, through = feed(
        here, total, core_swap(total), stream, vec, mixed, up_weight, grad_hidden
    )
    sums = sums + core_swap(sums)
    sums = sums + far_swap(sums)
    hidden_low, grad_pre, small_a, mine, theirs = hidden(
        here, sums, before_act, grad_hidden, vec, up_weight
    )
    chip = add_chip(here, mine, core_swap(theirs))
    total = add_far(here, chip, far_swap(chip))
    other = core_swap(total)
    grad_middle, small_b, *head_pieces, branch = middle_back(
        here,
        total,
        other,
        middle,
        stream,
        cotangent,
        vec,
        output_weight,
        inner_unit,
        inner_inv,
        through,
    )
    grad_pre, head_pieces = lax.optimization_barrier((grad_pre, head_pieces))
    head_received = shift_x(head_pieces)
    feed_parts = feed_grads(here, hidden_low, cotangent, grad_pre, feed_low, inner_low, branch, small_a, small_b)
    head_received, feed_parts = lax.optimization_barrier((head_received, feed_parts))
    feed_sums = lax.psum_scatter(feed_parts, "seq", scatter_dimension=0, axis_index_groups=X_GROUPS)
    message = grad_message(here, head_pieces[0], *head_received, mixed_row, logs_row)
    message_a = lax.ppermute(message, "seq", TO_SAME)
    message_b = lax.ppermute(message, "seq", TO_OTHER)
    weight_heads = head_weights(here, after(input_weight, message))
    message_a, message_b, weight_heads = lax.optimization_barrier((message_a, message_b, weight_heads))
    grad_qa, grad_qb, *kv_pieces = attend_backward(
        info, queries_a, queries_b, message_a, message_b, plane, begin
    )
    kv_parts = shift_y(kv_pieces)
    q_parts = [lax.ppermute(grad_qa, "seq", FROM_SAME), lax.ppermute(grad_qb, "seq", FROM_OTHER)]
    kv_parts, q_parts = lax.optimization_barrier((kv_parts, q_parts))
    projected_row, projected_sums, *pieces = row_grads(here, kv_pieces[0], *kv_parts, *q_parts, *tables)
    back_received = shift_x(pieces)
    quarter_pieces = attend_quarter(here, normed_row, projected_row, projected_sums)
    quarter_received = shift_y(quarter_pieces)
    block_pieces = blocks(here, after(feed_sums, quarter_pieces))
    block_received = shift_y(block_pieces)
    back_received, quarter_received = lax.optimization_barrier((back_received, quarter_received))
    mine, theirs = normed_back(here, pieces[0], *back_received, weight_heads)
    feed_pair = sum_z(pair(here, block_pieces[0], *block_received))
    chip = add_chip(here, mine, core_swap(theirs))
    chip, feed_pair = lax.optimization_barrier((chip, feed_pair))
    feed_shared = lax.all_gather(feed_pair, "seq", axis_index_groups=YX_GROUPS).reshape(4, 4, 592, 256)
    attend_pair = sum_z(add_four(here, quarter_pieces[0], *quarter_received))
    far, attend_pair = lax.optimization_barrier((far_swap(chip), attend_pair))
    total = add_far(here, chip, far)
    other = core_swap(total)
    attend_near = jnp.stack(ring(attend_pair, Y_SHIFTS))
    grad_tokens, last = leave(here, total, other, stream, grad_middle, vec, kind)
    last = ring_sum(here, X, last, *[lax.ppermute(last, "seq", pairs) for pairs in X_SHIFTS])
    attend_near, last, hidden_low = lax.optimization_barrier((attend_near, last, hidden_low))
    attend_parts = ring(attend_near, X_SHIFTS)
    feed_mine, feed_theirs = feed_out(here, hidden_low, down_weight)
    feed_chip = add_chip(here, feed_mine, core_swap(feed_theirs))
    feed_far = far_swap(feed_chip)
    last = ring_sum(here, Y, last, *[lax.ppermute(last, "seq", pairs) for pairs in Y_SHIFTS])
    grad_type_table, grad_attend_gain, grad_attend_bias = last_sum(
        here, last, lax.ppermute(last, "seq", Z_SWAP)
    )
    total = add_far(here, feed_chip, feed_far)
    other = core_swap(total)
    result = result_out(here, total, other, middle, vec)
    grad_down_weight, grad_up_weight, grad_output_weight, *small = feed_weights_out(here, feed_shared)
    grad_input_weight, grad_input_bias = attend_weights_out(here, *attend_parts)
    small = [v.reshape(D) for v in small]
    return (
        result,
        grad_tokens,
        grad_type_table,
        grad_attend_gain.reshape(D),
        grad_attend_bias.reshape(D),
        grad_input_weight,
        grad_input_bias,
        small[7][:local_width],
        small[7][local_width : 2 * local_width],
        grad_output_weight,
        small[5],
        small[3],
        small[4],
        grad_up_weight,
        small[2],
        small[0],
        small[1],
        grad_down_weight,
        small[6],
    )


def solution(mesh):
    in_specs = (
        P("seq", None),
        P("seq"),
        P(),
        P(),
        P(),
        P(),
        P(None, None, "ffn"),
        P(None, "ffn"),
        P("ffn"),
        P("ffn"),
        P("ffn", None),
        P(),
        P(),
        P(),
        P(None, "ffn"),
        P("ffn"),
        P("ffn"),
        P("ffn"),
        P("ffn", None),
        P(),
        P("seq", None),
    )
    out_specs = (
        P("seq", None),
        P("seq", None),
        P(),
        P(),
        P(),
        P(None, None, "ffn"),
        P(None, "ffn"),
        P("ffn"),
        P("ffn"),
        P("ffn", None),
        P(),
        P(),
        P(),
        P(None, "ffn"),
        P("ffn"),
        P("ffn"),
        P("ffn"),
        P("ffn", None),
        P(),
    )
    return jax.shard_map(
        per_device, mesh=mesh, in_specs=in_specs, out_specs=out_specs, check_vma=False
    )
```

```python
from functools import partial
import math

import jax
import jax.numpy as jnp
from jax import lax
from jax.experimental import pallas as pl
from jax.experimental.pallas import tpu as pltpu
from jax.sharding import PartitionSpec as P

D = 1024
FF = 4096
HEAD_DIM = 64
ROW = 1024
PACK = ROW // 2
PLANE = 4

epsilon = 1e-05
scale_base = 512.0
masked_score = -1e30
log2_e = 1.4426950408889634
score_factor = HEAD_DIM ** (-0.5) * log2_e
highest = lax.Precision.HIGHEST
f32 = jnp.float32
bf16 = jnp.bfloat16


def seq_index(y, z, x):
    return (y % 4) * 8 + (z % 2) * 4 + x % 4


def seq_pairs(move):
    pairs = []
    for y in range(4):
        for z in range(2):
            for x in range(4):
                pairs.append((seq_index(y, z, x), seq_index(*move(y, z, x))))
    return pairs


def shift_pairs(dy, dz, dx):
    return seq_pairs(lambda y, z, x: (y + dy, z + dz, x + dx))


def group_of(row):
    return min(row, 7 - row)


TO_SAME = seq_pairs(lambda y, z, x: (group_of(2 * y + z), z, x))
TO_OTHER = seq_pairs(lambda y, z, x: (group_of(2 * y + z), 1 - z, x))
FROM_SAME = [(b, a) for a, b in TO_SAME]
FROM_OTHER = [(b, a) for a, b in TO_OTHER]
X_SHIFTS = [shift_pairs(0, 0, d) for d in (1, 2, 3)]
Y_SHIFTS = [shift_pairs(d, 0, 0) for d in (1, 2, 3)]
Z_SWAP = shift_pairs(0, 1, 0)
X_SWAP = seq_pairs(lambda y, z, x: (y, z, x ^ 1))
Y_SWAP = seq_pairs(lambda y, z, x: (y ^ 1, z, x))
CORE_SWAP = [(f, f ^ 1) for f in range(4)]
FAR_SWAP = [(f, f ^ 2) for f in range(4)]
Y_GROUPS = [[seq_index(y, z, x) for y in range(4)] for z in range(2) for x in range(4)]
X_GROUPS = [[seq_index(y, z, x) for x in range(4)] for y in range(4) for z in range(2)]
Z_GROUPS = [[seq_index(y, z, x) for z in range(2)] for y in range(4) for x in range(4)]
YX_GROUPS = [[seq_index(y, z, x) for y in range(4) for x in range(4)] for z in range(2)]


def shift_x(pieces):
    return [lax.ppermute(piece, "seq", pairs) for piece, pairs in zip(pieces[1:], X_SHIFTS)]


def shift_y(pieces):
    return [lax.ppermute(piece, "seq", pairs) for piece, pairs in zip(pieces[1:], Y_SHIFTS)]


def core_swap(values):
    return lax.ppermute(values, "ffn", CORE_SWAP)


def far_swap(values):
    return lax.ppermute(values, "ffn", FAR_SWAP)


def gather_x(values):
    return lax.all_gather(values, "seq", axis_index_groups=X_GROUPS, tiled=True)


def ring(values, shifts):
    return [values] + [lax.ppermute(values, "seq", pairs) for pairs in shifts]


def sum_z(values):
    other = lax.ppermute(values, "seq", Z_SWAP)
    return (values.astype(f32) + other.astype(f32)).astype(bf16)


def after(value, *others):
    return lax.optimization_barrier((value,) + others)[0]


X, Y, Z, CORE, PART = range(5)


def run(kernel, name, here, operands, outs, scratch=(), megabytes=18):
    return pl.pallas_call(
        kernel,
        in_specs=[pl.BlockSpec(memory_space=pltpu.SMEM)]
        + [pl.BlockSpec(memory_space=pltpu.VMEM)] * len(operands),
        out_specs=[pl.BlockSpec(memory_space=pltpu.VMEM)] * len(outs),
        out_shape=[jax.ShapeDtypeStruct(shape, kind) for shape, kind in outs],
        scratch_shapes=list(scratch),
        compiler_params=pltpu.CompilerParams(vmem_limit_bytes=megabytes * 2**20),
        cost_estimate=pl.CostEstimate(
            flops=2**20,
            bytes_accessed=sum(v.size * v.dtype.itemsize for v in operands)
            + sum(math.prod(shape) * jnp.dtype(kind).itemsize for shape, kind in outs),
            transcendentals=0,
        ),
        name=name,
    )(here, *operands)


def dot_nn(a, b):
    return lax.dot_general(a, b, (((1,), (0,)), ((), ())), preferred_element_type=f32)


def dot_nt(a, b):
    return lax.dot_general(a, b, (((1,), (1,)), ((), ())), preferred_element_type=f32)


def dot_tn(a, b):
    return lax.dot_general(a, b, (((0,), (0,)), ((), ())), preferred_element_type=f32)


def before(place, d):
    return lax.rem(place + (4 - d), 4)


def store_at(refs, place, index, value):
    for d, ref in enumerate(refs):

        @pl.when(lax.rem(place + d, 4) == index)
        def _(ref=ref):
            ref[...] = value


def store_half(mine, theirs, core, half, value):
    @pl.when(core == half)
    def _():
        mine[...] = value

    @pl.when(core != half)
    def _():
        theirs[...] = value


def row_of(column):
    return jnp.broadcast_to(column, (column.shape[0], 128)).T[0:1]


def split_three(values):
    high = values.astype(bf16).astype(f32)
    middle = (values - high).astype(bf16).astype(f32)
    return high, middle, values - high - middle


def norm_parts(values):
    center = values - jnp.mean(values, axis=-1, keepdims=True)
    inv_std = lax.rsqrt(jnp.mean(center * center, axis=-1, keepdims=True) + epsilon)
    return center * inv_std, inv_std


def norm_back(grad_out, unit, inv_std, gain):
    scaled = grad_out * gain
    return inv_std * (
        scaled
        - jnp.mean(scaled, axis=-1, keepdims=True)
        - unit * jnp.mean(scaled * unit, axis=-1, keepdims=True)
    )


def pair_pack(values, side):
    left = lax.broadcasted_iota(jnp.int32, (128, 128), 1) < 64
    if side == 0:
        return jnp.where(left, values[:128], pltpu.roll(values[128:], 64, 1))
    return jnp.where(left, pltpu.roll(values[:128], 64, 1), values[128:])


def pair_unpack(even, odd):
    left = lax.broadcasted_iota(jnp.int32, (128, 128), 1) < 64
    low = jnp.where(left, even, pltpu.roll(odd, 64, 1))
    high = jnp.where(left, pltpu.roll(even, 64, 1), odd)
    return jnp.concatenate([low, high], axis=0)


def half_swapped(values):
    lane = lax.broadcasted_iota(jnp.int32, values.shape, 1)
    return jnp.where(lane % 64 < 32, pltpu.roll(values, 96, 1), pltpu.roll(values, 32, 1))


def enter_kernel(
    here, tokens, kind, table, norm, weight, shift, cosine, sine, growth, stream_ref, normed_ref, *out
):
    stream = tokens[...].astype(f32)
    kinds = jnp.broadcast_to(kind[...].astype(f32), (128, 256)).T[:, 0:1]
    for c in range(3):
        stream = stream + jnp.where(kinds == c, table[c : c + 1, :].astype(f32), 0.0)
    stream_ref[...] = stream
    unit, _ = norm_parts(stream)
    normed = (unit * norm[0:1, :].astype(f32) + norm[1:2, :].astype(f32)).astype(bf16)
    normed_ref[...] = normed
    projected = [dot_nn(normed, weight[s]) + shift[s : s + 1, :].astype(f32) for s in range(3)]
    lane = lax.broadcasted_iota(jnp.int32, (256, 128), 1)
    left = lane < 64
    signed = jnp.where(lane % 64 < 32, -sine[...], sine[...])
    for group in range(2):
        lanes = slice(128 * group, 128 * group + 128)
        query, key, value = [p[:, lanes] for p in projected]
        query = (query * cosine[...] + half_swapped(query) * signed) * growth[...]
        key = (key * cosine[...] + half_swapped(key) * signed) / growth[...]
        for side in range(2):
            if side == 0:
                both = jnp.where(left, key, pltpu.roll(value, 64, 1))
            else:
                both = jnp.where(left, pltpu.roll(key, 64, 1), value)
            message = jnp.concatenate([both, pair_pack(query, side)], axis=0).astype(bf16)
            store_at(out, here[X], 2 * group + side, message)


def enter(here, *operands):
    return run(
        enter_kernel,
        "enter",
        here,
        operands,
        [((256, D), f32), ((256, D), bf16)] + [((384, 128), bf16)] * 4,
        megabytes=3,
    )


def rows_kernel(here, p0, p1, p2, p3, kv_ref, q_ref):
    for d, ref in enumerate((p0, p1, p2, p3)):
        source = before(here[X], d)
        kv_ref[pl.ds(pl.multiple_of(source * 256, 256), 256), :] = ref[:256, :]
        q_ref[pl.ds(pl.multiple_of(source * 128, 128), 128), :] = ref[256:, :]


def rows(here, *pieces):
    return run(rows_kernel, "rows", here, pieces, [((ROW, 128), bf16), ((PACK, 128), bf16)], megabytes=1)


def lane_rows(row):
    return jnp.concatenate([row[:, 128 * j : 128 * j + 128] for j in range(8)], axis=0)


def unpack_transposed(source, target, offset):
    for b in range(4):
        piece = source[128 * b : 128 * b + 128, :].T
        target[offset : offset + 64, 256 * b : 256 * b + 128] = piece[:64]
        target[offset : offset + 64, 256 * b + 128 : 256 * b + 256] = piece[64:]


def pack_transposed(columns, target):
    for b in range(4):
        piece = jnp.concatenate(
            [columns[:, 256 * b : 256 * b + 128], columns[:, 256 * b + 128 : 256 * b + 256]], axis=0
        )
        target[128 * b : 128 * b + 128, :] = piece.T.astype(target.dtype)


def chunk_bounds(info, tile):
    z = info[0]
    row = info[1 + tile]
    lowest = info[3 + tile]
    first = jnp.int32(0)
    last = jnp.int32(0)
    for c in range(PLANE):
        start = (2 * c + z) * ROW
        first = first + (start + ROW - 1 < lowest).astype(jnp.int32)
        last = last + (2 * c + z <= row).astype(jnp.int32)
    return first, last


def visible(info, tile, c, begin_ref, keys, queries):
    shape = (keys.stop - keys.start, queries.stop - queries.start)
    key = (2 * c + info[0]) * ROW + keys.start + lax.broadcasted_iota(jnp.int32, shape, 0)
    query = info[1 + tile] * ROW + queries.start + lax.broadcasted_iota(jnp.int32, shape, 1)
    return (key <= query) & (key >= begin_ref[:, queries])


def each_block(info, tile, step):
    whole, low, high = slice(0, ROW), slice(0, ROW // 2), slice(ROW // 2, ROW)

    def body(c, carry):
        own = 2 * c + info[0] == info[1 + tile]
        masked = jnp.logical_not(own) & needs_mask(info, tile, c)

        @pl.when(own)
        def _():
            step(c, True, low, whole)
            step(c, True, high, high)

        @pl.when(masked)
        def _():
            step(c, True, whole, whole)

        @pl.when(jnp.logical_not(own | masked))
        def _():
            step(c, False, whole, whole)

        return carry

    first, last = chunk_bounds(info, tile)
    lax.fori_loop(first, last, body, 0)


def needs_mask(info, tile, c):
    key_row = 2 * c + info[0]
    return (key_row == info[1 + tile]) | (key_row * ROW < info[5 + tile])


def plane_copies(info, pieces, kv_ref):
    return [
        (piece, kv_ref.at[pl.ds(pl.multiple_of(before(info[7], d) * ROW, ROW), ROW)])
        for d, piece in enumerate(pieces)
    ]


def forward_kernel(
    info,
    qa,
    qb,
    kv0,
    kv1,
    kv2,
    kv3,
    begin_ref,
    outa_ref,
    outb_ref,
    kv_ref,
    q_in,
    qt_ref,
    vt_ref,
    acc_ref,
    top_ref,
    semaphores,
):
    tile = pl.program_id(0)

    @pl.when(tile == 0)
    def _():
        copies = [
            pltpu.make_async_copy(source, target, semaphores.at[k])
            for k, (source, target) in enumerate(
                [(qa, q_in.at[0]), (qb, q_in.at[1])] + plane_copies(info, (kv0, kv1, kv2, kv3), kv_ref)
            )
        ]
        for copy in copies:
            copy.start()
        for copy in copies:
            copy.wait()
        for c in range(PLANE):
            block = kv_ref[c * ROW : c * ROW + ROW, :].T
            index = lax.broadcasted_iota(jnp.int32, block.shape, 0)
            vt_ref[:, c * ROW : c * ROW + ROW] = jnp.where(index < 64, jnp.ones_like(block), block)
        qt_ref[64:, :] = jnp.zeros((64, ROW), bf16)

    unpack_transposed(q_in.at[tile], qt_ref, 0)

    top_ref[...] = jnp.full(top_ref.shape, masked_score, f32)
    acc_ref[...] = jnp.zeros(acc_ref.shape, f32)

    def step(c, masked, keys, queries):
        start = pl.multiple_of(c * ROW + keys.start, ROW // 2)
        count = keys.stop - keys.start
        scores = dot_nn(kv_ref[pl.ds(start, count), :], qt_ref[:, queries]) * score_factor
        if masked:
            seen = visible(info, tile, c, begin_ref, keys, queries)
            scores = jnp.where(seen, scores, 2 * masked_score)
        old = top_ref[:, queries]
        top = jnp.maximum(old, jnp.max(scores, axis=0, keepdims=True))
        weights = jnp.exp2(scores - top)
        top_ref[:, queries] = top
        acc_ref[:, queries] = acc_ref[:, queries] * jnp.exp2(old - top) + dot_nn(
            vt_ref[:, pl.ds(start, count)], weights.astype(bf16)
        )

    each_block(info, tile, step)
    total = acc_ref[0:1, :]
    some = total > 0
    safe = jnp.where(some, total, 1.0)
    log_total = jnp.where(some, top_ref[...] + jnp.log2(safe), masked_score)
    for index, out_ref in enumerate((outa_ref, outb_ref)):

        @pl.when(tile == index)
        def _(out_ref=out_ref):
            pack_transposed(acc_ref[64:, :] / safe, out_ref)
            parts = [lane_rows(part) for part in split_three(log_total)]
            out_ref[PACK:, :] = jnp.concatenate(parts + [jnp.zeros((8, 128), f32)], axis=0).astype(bf16)


def attend_forward(info, queries_a, queries_b, keys_values, begin):
    hbm = pl.BlockSpec(memory_space=pltpu.HBM)
    return pl.pallas_call(
        forward_kernel,
        grid_spec=pltpu.PrefetchScalarGridSpec(
            num_scalar_prefetch=1,
            grid=(2,),
            in_specs=[hbm] * 6 + [pl.BlockSpec((1, ROW), lambda i, s: (0, i))],
            out_specs=[pl.BlockSpec(memory_space=pltpu.VMEM)] * 4,
            scratch_shapes=[
                pltpu.VMEM((128, ROW), bf16),
                pltpu.VMEM((128, PLANE * ROW), bf16),
                pltpu.VMEM((128, ROW), f32),
                pltpu.VMEM((1, ROW), f32),
                pltpu.SemaphoreType.DMA((6,)),
            ],
        ),
        out_shape=[jax.ShapeDtypeStruct((PACK + 32, 128), bf16)] * 2
        + [jax.ShapeDtypeStruct((PLANE * ROW, 128), bf16), jax.ShapeDtypeStruct((2, PACK, 128), bf16)],
        compiler_params=pltpu.CompilerParams(vmem_limit_bytes=9 * 2**20),
        cost_estimate=pl.CostEstimate(flops=10 * 10**9, bytes_accessed=2**21, transcendentals=0),
        name="attend_forward",
    )(info, queries_a, queries_b, *keys_values, begin)


def combine_kernel(here, a_ref, b_ref, full_ref, log_ref, *out):
    logs = []
    for ref in (a_ref, b_ref):
        rows = ref[PACK:, :].astype(f32)
        logs.append(rows[:8] + rows[8:16] + rows[16:24])
    top = jnp.maximum(logs[0], logs[1])
    shares = [jnp.exp2(part - top) for part in logs]
    total = shares[0] + shares[1]
    log_ref[...] = top + jnp.log2(total)
    columns = [(share / total).T for share in shares]
    left = lax.broadcasted_iota(jnp.int32, (128, 128), 1) < 64
    for b in range(4):
        mixed = jnp.zeros((128, 128), f32)
        for ref, column in zip((a_ref, b_ref), columns):
            weight = jnp.where(left, column[:, 2 * b : 2 * b + 1], column[:, 2 * b + 1 : 2 * b + 2])
            mixed = mixed + weight * ref[128 * b : 128 * b + 128, :].astype(f32)
        full_ref[128 * b : 128 * b + 128, :] = mixed
        store_at(out, here[X], b, mixed.astype(bf16))


def combine(here, part_a, part_b):
    return run(
        combine_kernel,
        "combine",
        here,
        (part_a, part_b),
        [((PACK, 128), f32), ((8, 128), f32)] + [((128, 128), bf16)] * 4,
        megabytes=1,
    )


def grad_message_kernel(here, p0, p1, p2, p3, mixed_ref, log_ref, out_ref):
    for d, ref in enumerate((p0, p1, p2, p3)):
        out_ref[pl.ds(pl.multiple_of(before(here[X], d) * 128, 128), 128), :] = ref[...]
    deltas = []
    for b in range(4):
        rows = slice(128 * b, 128 * b + 128)
        each = (out_ref[rows, :].astype(f32) * mixed_ref[rows, :]).T
        deltas.append(jnp.sum(each[:64], axis=0, keepdims=True))
        deltas.append(jnp.sum(each[64:], axis=0, keepdims=True))
    parts = list(split_three(log_ref[...])) + list(split_three(jnp.concatenate(deltas, axis=0)))
    out_ref[PACK:, :] = jnp.concatenate(parts, axis=0).astype(bf16)


def grad_message(here, *operands):
    return run(grad_message_kernel, "grad_message", here, operands, [((PACK + 48, 128), bf16)], megabytes=1)[0]


def backward_kernel(
    info,
    plane,
    queries,
    ma,
    mb,
    begin_ref,
    dqa_ref,
    dqb_ref,
    own_ref,
    one_ref,
    two_ref,
    three_ref,
    qt_ref,
    gt_ref,
    q_ref,
    g_ref,
    kv_ref,
    kt_ref,
    row_ref,
    acc_ref,
    dq_acc,
    q_in,
    m_in,
    semaphores,
):
    tile = pl.program_id(0)

    def load(query_ref, message_ref):
        unpack_transposed(query_ref, qt_ref, 0)
        unpack_transposed(message_ref, gt_ref, 64)
        q_ref[...] = qt_ref[...].T
        g_ref[...] = gt_ref[...].T
        rows = message_ref[PACK:, :].astype(f32)
        for k in range(2):
            part = rows[24 * k : 24 * k + 8] + rows[24 * k + 8 : 24 * k + 16] + rows[24 * k + 16 : 24 * k + 24]
            for j in range(8):
                row_ref[k : k + 1, 128 * j : 128 * j + 128] = part[j : j + 1, :]

    @pl.when(tile == 0)
    def _():
        copies = [
            pltpu.make_async_copy(source, target, semaphores.at[k])
            for k, (source, target) in enumerate(
                [(queries, q_in), (ma, m_in.at[0]), (mb, m_in.at[1]), (plane, kv_ref)]
            )
        ]
        for copy in copies:
            copy.start()
        acc_ref[...] = jnp.zeros(acc_ref.shape, f32)
        qt_ref[64:, :] = jnp.zeros((64, ROW), bf16)
        gt_ref[:64, :] = jnp.zeros((64, ROW), bf16)
        for copy in copies:
            copy.wait()
        for c in range(PLANE):
            kt_ref[:, c * ROW : c * ROW + ROW] = kv_ref[c * ROW : c * ROW + ROW, :].T

    load(q_in.at[tile], m_in.at[tile])
    dq_acc[...] = jnp.zeros(dq_acc.shape, f32)

    def step(c, masked, keys, queries):
        start = pl.multiple_of(c * ROW + keys.start, ROW // 2)
        count = keys.stop - keys.start
        block = kv_ref[pl.ds(start, count), :]
        scores = dot_nn(block, qt_ref[:, queries]) * score_factor
        if masked:
            seen = visible(info, tile, c, begin_ref, keys, queries)
            scores = jnp.where(seen, scores, 2 * masked_score)
        weights = jnp.exp2(scores - row_ref[0:1, queries])
        grad_weights = dot_nn(block, gt_ref[:, queries])
        grad_scores = (weights * (grad_weights - row_ref[1:2, queries])).astype(bf16)
        acc_ref[pl.ds(start, count), :] += dot_nn(grad_scores, q_ref[queries, :]) + dot_nn(
            weights.astype(bf16), g_ref[queries, :]
        )
        dq_acc[:, queries] += dot_nn(kt_ref[:, pl.ds(start, count)], grad_scores)

    each_block(info, tile, step)

    @pl.when(tile == 0)
    def _():
        pack_transposed(dq_acc[:64, :], dqa_ref)

    @pl.when(tile == 1)
    def _():
        pack_transposed(dq_acc[:64, :], dqb_ref)
        for d, ref in enumerate((own_ref, one_ref, two_ref, three_ref)):
            start = pl.multiple_of(lax.rem(info[7] + d, 4) * ROW, ROW)
            ref[...] = acc_ref[pl.ds(start, ROW), :].astype(bf16)


def attend_backward(info, plane, queries, message_a, message_b, begin):
    packed = pl.BlockSpec((PACK, 128), lambda i, s: (0, 0))
    hbm = pl.BlockSpec(memory_space=pltpu.HBM)
    block = pl.BlockSpec((ROW, 128), lambda i, s: (0, 0))
    return pl.pallas_call(
        backward_kernel,
        grid_spec=pltpu.PrefetchScalarGridSpec(
            num_scalar_prefetch=1,
            grid=(2,),
            in_specs=[hbm] * 4 + [pl.BlockSpec((1, ROW), lambda i, s: (0, i))],
            out_specs=[packed] * 2 + [block] * 4,
            scratch_shapes=[
                pltpu.VMEM((128, ROW), bf16),
                pltpu.VMEM((128, ROW), bf16),
                pltpu.VMEM((ROW, 128), bf16),
                pltpu.VMEM((ROW, 128), bf16),
                pltpu.VMEM((PLANE * ROW, 128), bf16),
                pltpu.VMEM((128, PLANE * ROW), bf16),
                pltpu.VMEM((8, ROW), f32),
                pltpu.VMEM((PLANE * ROW, 128), f32),
                pltpu.VMEM((128, ROW), f32),
                pltpu.VMEM((2, PACK, 128), bf16),
                pltpu.VMEM((2, PACK + 48, 128), bf16),
                pltpu.SemaphoreType.DMA((4,)),
            ],
        ),
        out_shape=[jax.ShapeDtypeStruct((PACK, 128), bf16)] * 2
        + [jax.ShapeDtypeStruct((ROW, 128), bf16)] * 4,
        compiler_params=pltpu.CompilerParams(vmem_limit_bytes=16 * 2**20),
        cost_estimate=pl.CostEstimate(flops=18 * 10**9, bytes_accessed=2**22, transcendentals=0),
        name="attend_backward",
    )(info, plane, queries, message_a, message_b, begin)


def inner_kernel(here, p0, p1, p2, p3, gain, shift, weight, mixed_ref, mine, theirs, heads):
    for d, ref in enumerate((p0, p1, p2, p3)):
        heads[before(here[X], d)] = ref[...].astype(f32)
    mixed = jnp.concatenate([pair_unpack(heads[0], heads[1]), pair_unpack(heads[2], heads[3])], axis=1)
    mixed_ref[...] = mixed
    mean = jnp.mean(mixed, axis=-1, keepdims=True)
    centred = mixed - mean
    spread = jnp.sum(centred * centred, axis=-1, keepdims=True)
    gains = gain[...].astype(f32)
    projected = dot_nn((centred * gains).astype(bf16), weight[...])
    full = weight[...].astype(f32)
    gain_column = jnp.broadcast_to(gains, (128, 256)).T[:, 0:1]
    shift_column = jnp.broadcast_to(shift[...].astype(f32), (128, 256)).T[:, 0:1]
    through = jnp.sum(full * gain_column, axis=0, keepdims=True)
    vectors = [jnp.where(here[PART] == k, through, 0.0) for k in range(4)]
    vectors.append(jnp.sum(full * shift_column, axis=0, keepdims=True))
    for half in range(2):
        tokens = slice(128 * half, 128 * half + 128)
        stats = [row_of(mean[tokens]), row_of(spread[tokens])]
        slots = [jnp.where(here[PART] == j // 2, stats[j % 2], 0.0) for j in range(8)]
        rows = vectors + [jnp.concatenate(slots, axis=1), jnp.zeros((2, D), f32)]
        store_half(mine, theirs, here[CORE], half, jnp.concatenate([projected[tokens]] + rows, axis=0))


def inner(here, *operands):
    return run(
        inner_kernel,
        "inner",
        here,
        operands,
        [((256, 256), f32), ((136, D), f32), ((136, D), f32)],
        [pltpu.VMEM((4, 128, 128), f32)],
        megabytes=4,
    )


def chip_stats_kernel(here, mine, other, out):
    total = mine[...] + other[...]
    parts = list(split_three(total[128:])) + [jnp.zeros((8, D), f32)]
    out[...] = jnp.concatenate([total[:128]] + parts, axis=0).astype(bf16)


def join_stats_kernel(here, chip, far, out):
    total = chip[...].astype(f32) + far[...].astype(f32)
    out[...] = jnp.concatenate([total[:128], total[128:136] + total[136:144] + total[144:152]], axis=0)


def add_chip_kernel(here, mine, other, out):
    out[...] = (mine[...] + other[...]).astype(bf16)


def add_far_kernel(here, chip, far, out):
    out[...] = chip[...].astype(f32) + far[...].astype(f32)


def chip_stats(here, mine, other):
    return run(chip_stats_kernel, "chip_stats", here, (mine, other), [((160, D), bf16)], megabytes=1)[0]


def join_stats(here, chip, far):
    return run(join_stats_kernel, "join_stats", here, (chip, far), [((136, D), f32)], megabytes=1)[0]


def add_chip(here, mine, other):
    return run(add_chip_kernel, "add_chip", here, (mine, other), [((128, D), bf16)], megabytes=1)[0]


def add_far(here, chip, far):
    return run(add_far_kernel, "add_far", here, (chip, far), [((128, D), f32)], megabytes=1)[0]


def sum_ffn(here, mine, theirs):
    chip = add_chip(here, mine, core_swap(theirs))
    total = add_far(here, chip, far_swap(chip))
    return total, core_swap(total)


def gauss_share(values):
    return 0.5 + 0.5 * lax.erf(values * math.sqrt(0.5))


def feed_kernel(
    here,
    total,
    other,
    stream,
    vec,
    mixed_ref,
    weight,
    grad_hidden,
    low_ref,
    inner_ref,
    middle_ref,
    before_ref,
    unit_ref,
    inv_ref,
    sums_ref,
    vectors_ref,
    halves,
):
    halves[here[CORE]] = total[...]
    halves[1 - here[CORE]] = other[...]
    vectors = halves[0, 128:, :]
    vectors_ref[...] = vectors
    ending = vectors[4:5, :] + vec[OUTPUT_BIAS : OUTPUT_BIAS + 1, :]
    inner_gain = vec[INNER : INNER + 1, :256]
    inner_bias = vec[INNER : INNER + 1, 256:512]
    for half in range(2):
        tokens = slice(128 * half, 128 * half + 128)
        stats = jnp.concatenate([halves[half, 133:134, 128 * j : 128 * j + 128] for j in range(8)], axis=0).T
        means = [stats[:, 2 * k : 2 * k + 1] for k in range(4)]
        mean = (means[0] + means[1] + means[2] + means[3]) * 0.25
        spread = stats[:, 1:2] + stats[:, 3:4] + stats[:, 5:6] + stats[:, 7:8]
        projected = halves[half, :128, :]
        for k in range(4):
            move = means[k] - mean
            spread = spread + 256.0 * move * move
            projected = projected + move * vectors[k : k + 1, :]
        inv = lax.rsqrt(spread / D + epsilon)
        middle_ref[tokens, :] = stream[tokens, :] + projected * inv + ending
        unit = (mixed_ref[tokens, :] - mean) * inv
        unit_ref[tokens, :] = unit
        inv_ref[tokens, :] = jnp.broadcast_to(inv, (128, 128))
        inner_ref[tokens, :] = (unit * inner_gain + inner_bias).astype(bf16)
    unit, _ = norm_parts(middle_ref[...])
    low_ref[...] = (
        unit * vec[FEED_GAIN : FEED_GAIN + 1, :] + vec[FEED_BIAS : FEED_BIAS + 1, :]
    ).astype(bf16)
    before_act = dot_nn(low_ref[...], weight[...]) + vec[UP_BIAS : UP_BIAS + 1, :]
    before_ref[...] = before_act
    active = before_act * gauss_share(before_act)
    scaled = grad_hidden[...] * vec[HIDDEN_GAIN : HIDDEN_GAIN + 1, :]
    columns = [
        jnp.sum(part, axis=-1, keepdims=True) for part in (active, active * active, scaled, scaled * active)
    ]
    lane = lax.broadcasted_iota(jnp.int32, (256, 128), 1)
    spread = jnp.zeros((256, 128), f32)
    for k, column in enumerate(columns):
        spread = jnp.where(lane == k, column, spread)
    sums_ref[...] = spread.T[:8]


def feed(here, *operands):
    return run(
        feed_kernel,
        "feed",
        here,
        operands,
        [
            ((256, D), bf16),
            ((256, 256), bf16),
            ((256, D), f32),
            ((256, D), f32),
            ((256, 256), f32),
            ((256, 128), f32),
            ((8, 256), f32),
            ((8, D), f32),
        ],
        [pltpu.VMEM((2, 136, D), f32)],
        megabytes=6,
    )


def hidden_kernel(
    here, sums, before_ref, grad_hidden, vec, weight, low_ref, grad_ref, small_ref, mine, theirs
):
    before_act = before_ref[...]
    share = gauss_share(before_act)
    slope = share + before_act * jnp.exp(-0.5 * before_act * before_act) * (1.0 / math.sqrt(2.0 * math.pi))
    columns = sums[...].T
    mean = columns[:, 0:1] / FF
    inv = lax.rsqrt(columns[:, 1:2] / FF - mean * mean + epsilon)
    first = columns[:, 2:3]
    cross = inv * (columns[:, 3:4] - mean * first)
    gain = vec[HIDDEN_GAIN : HIDDEN_GAIN + 1, :]
    unit = (before_act * share - mean) * inv
    low_ref[...] = (unit * gain + vec[HIDDEN_BIAS : HIDDEN_BIAS + 1, :]).astype(bf16)
    grad_out = grad_hidden[...]
    grad_pre = (inv * (grad_out * gain - first / FF - unit * (cross / FF)) * slope).astype(bf16)
    small_ref[0:1, :] = jnp.sum(grad_out * unit, axis=0, keepdims=True)
    small_ref[1:2, :] = jnp.sum(grad_out, axis=0, keepdims=True)
    small_ref[2:3, :] = jnp.sum(grad_pre.astype(f32), axis=0, keepdims=True)
    small_ref[3:, :] = jnp.zeros((5, D), f32)
    grad_ref[...] = grad_pre
    back = dot_nt(grad_pre, weight[...])
    for half in range(2):
        store_half(mine, theirs, here[CORE], half, back[128 * half : 128 * half + 128])


def hidden(here, *operands):
    return run(
        hidden_kernel,
        "hidden",
        here,
        operands,
        [((256, D), bf16), ((256, D), bf16), ((8, D), f32), ((128, D), f32), ((128, D), f32)],
        megabytes=6,
    )


def feed_out_kernel(here, low_ref, weight, mine, theirs):
    for half in range(2):
        tokens = slice(128 * half, 128 * half + 128)
        store_half(mine, theirs, here[CORE], half, dot_nn(low_ref[tokens, :], weight[...]))


def feed_out(here, low, weight):
    return run(
        feed_out_kernel, "feed_out", here, (low, weight), [((128, D), f32), ((128, D), f32)], megabytes=2
    )


def result_kernel(here, total, other, middle, vec, out, halves):
    halves[here[CORE]] = total[...]
    halves[1 - here[CORE]] = other[...]
    for half in range(2):
        tokens = slice(128 * half, 128 * half + 128)
        out[tokens, :] = (
            middle[tokens, :] + halves[half] + vec[DOWN_BIAS : DOWN_BIAS + 1, :]
        ).astype(bf16)


def result_out(here, *operands):
    return run(
        result_kernel,
        "result",
        here,
        operands,
        [((256, D), bf16)],
        [pltpu.VMEM((2, 128, D), f32)],
        megabytes=4,
    )[0]


def feed_grads_kernel(here, low, cotangent, grad_pre, feed_low, inner_low, branch, small_a, small_b, out):
    grads = dot_tn(inner_low[...], branch[...])
    vectors = [small_a[k : k + 1, :] for k in range(3)] + [small_b[k : k + 1, :] for k in range(5)]
    for k in range(4):
        lanes = slice(256 * k, 256 * k + 256)
        parts = [dot_tn(low[:, lanes], cotangent[...]), dot_tn(grad_pre[:, lanes], feed_low[...])]
        parts += [grads[64 * k : 64 * k + 64], vectors[2 * k], vectors[2 * k + 1], jnp.zeros((14, D), f32)]
        out[k] = jnp.concatenate(parts, axis=0).astype(bf16)


def feed_grads(here, *operands):
    return run(feed_grads_kernel, "feed_grads", here, operands, [((4, 592, D), bf16)], megabytes=8)[0]


def blocks_kernel(here, total, *out):
    for k in range(4):
        store_at(out, here[Y], k, total[:, 256 * k : 256 * k + 256])


def blocks(here, total):
    return run(blocks_kernel, "blocks", here, (total,), [((total.shape[0], 256), bf16)] * 4, megabytes=2)


def pair_kernel(here, p0, p1, p2, p3, out):
    total = p0[...].astype(f32) + p1[...].astype(f32) + p2[...].astype(f32) + p3[...].astype(f32)
    out[...] = jnp.concatenate([total[:256], total[256:512].T, total[512:]], axis=0).astype(bf16)


def pair(here, *pieces):
    return run(pair_kernel, "pair", here, pieces, [((592, 256), bf16)], megabytes=3)[0]


def middle_back_kernel(
    here,
    total,
    other,
    middle,
    stream,
    cotangent,
    vec,
    weight,
    unit_ref,
    inv_ref,
    vectors,
    grad_ref,
    small_ref,
    h0,
    h1,
    h2,
    h3,
    low_ref,
    halves,
):
    halves[here[CORE]] = total[...]
    halves[1 - here[CORE]] = other[...]
    grad_feed = jnp.concatenate([halves[0], halves[1]], axis=0)
    unit, inv = norm_parts(middle[...])
    grad_result = cotangent[...].astype(f32)
    grad_middle = grad_result + norm_back(grad_feed, unit, inv, vec[FEED_GAIN : FEED_GAIN + 1, :])
    grad_ref[...] = grad_middle
    low = grad_middle.astype(bf16)
    branch = low.astype(f32)
    low_ref[...] = low
    grad_inner = dot_nt(low, weight[...])
    through = vectors[0:1, :] + vectors[1:2, :] + vectors[2:3, :] + vectors[3:4, :]
    first = jnp.sum(branch * through, axis=-1, keepdims=True)
    ending = vectors[4:5, :] + vec[OUTPUT_BIAS : OUTPUT_BIAS + 1, :]
    cross = jnp.sum(branch * (middle[...] - stream[...] - ending), axis=-1, keepdims=True)
    inner_unit = unit_ref[...]
    inner_inv = inv_ref[:, 0:1]
    grad_mixed = inner_inv * (
        grad_inner * vec[INNER : INNER + 1, :256] - first / D - inner_unit * (cross / D)
    )
    for group in range(2):
        lanes = grad_mixed[:, 128 * group : 128 * group + 128]
        for side in range(2):
            store_at((h0, h1, h2, h3), here[X], 2 * group + side, pair_pack(lanes, side).astype(bf16))
    small_ref[0:1, :] = jnp.sum(grad_feed * unit, axis=0, keepdims=True)
    small_ref[1:2, :] = jnp.sum(grad_feed, axis=0, keepdims=True)
    small_ref[2:3, :] = jnp.sum(branch, axis=0, keepdims=True)
    small_ref[3:4, :] = jnp.sum(grad_result, axis=0, keepdims=True)
    small_ref[4:5, :256] = jnp.sum(grad_inner * inner_unit, axis=0, keepdims=True)
    small_ref[4:5, 256:512] = jnp.sum(grad_inner, axis=0, keepdims=True)
    small_ref[4:5, 512:] = jnp.zeros((1, 512), f32)
    small_ref[5:, :] = jnp.zeros((3, D), f32)


def middle_back(here, *operands):
    return run(
        middle_back_kernel,
        "middle_back",
        here,
        operands,
        [((256, D), f32), ((8, D), f32)] + [((128, 128), bf16)] * 4 + [((256, D), bf16)],
        [pltpu.VMEM((2, 128, D), f32)],
        megabytes=8,
    )


def row_grads_kernel(
    here, own, one, two, three, qa, qb, cos_in, sin_in, out_ref, sums_ref, p0, p1, p2, p3
):
    left = lax.broadcasted_iota(jnp.int32, (128, 128), 1) < 64

    def turned(values, cos_part, sin_part):
        return (values * cos_part + half_swapped(values) * sin_part).astype(bf16)

    for b in range(8):
        rows = slice(128 * b, 128 * b + 128)
        total = own[rows, :].astype(f32)
        for ref in (one, two, three):
            total = total + ref[rows, :].astype(f32)
        out_ref[rows, :128] = turned(
            total, jnp.where(left, cos_in[rows, :], 1.0), jnp.where(left, sin_in[rows, :], 0.0)
        )
    for b in range(4):
        rows = slice(128 * b, 128 * b + 128)
        total = qa[rows, :].astype(f32) + qb[rows, :].astype(f32)
        for side in range(2):
            tokens = slice(256 * b + 128 * side, 256 * b + 128 * side + 128)
            values = total if side == 0 else pltpu.roll(total, 64, 1)
            values = jnp.where(left, values, 0.0)
            out_ref[tokens, 128:] = turned(
                values, pltpu.roll(cos_in[tokens, :], 64, 1), pltpu.roll(sin_in[tokens, :], 64, 1)
            )
    for b in range(4):
        store_at((p0, p1, p2, p3), here[X], b, out_ref[256 * b : 256 * b + 256, :])
    sums_ref[...] = jnp.broadcast_to(jnp.sum(out_ref[...].astype(f32), axis=0, keepdims=True), (8, 256))


def row_grads(here, *operands):
    return run(
        row_grads_kernel,
        "row_grads",
        here,
        operands,
        [((ROW, 256), bf16), ((8, 256), f32)] + [((256, 256), bf16)] * 4,
        megabytes=3,
    )


def head_weights_kernel(here, weight, out):
    left = lax.broadcasted_iota(jnp.int32, (256, 128), 1) < 64
    for r in range(4):
        rows = slice(256 * r, 256 * r + 256)
        for group in range(2):
            lanes = slice(128 * group, 128 * group + 128)
            query, key, value = [weight[s, rows, lanes].astype(f32) for s in range(3)]
            even = [jnp.where(left, key, pltpu.roll(value, 64, 1)), jnp.where(left, query, 0.0)]
            odd = [
                jnp.where(left, pltpu.roll(key, 64, 1), value),
                jnp.where(left, pltpu.roll(query, 64, 1), 0.0),
            ]
            for side, parts in enumerate((even, odd)):
                out[2 * group + side, rows, :] = jnp.concatenate(parts, axis=1).astype(bf16)


def head_weights(here, weight):
    return run(head_weights_kernel, "head_weights", here, (weight,), [((4, D, 256), bf16)], megabytes=2)[0]


def normed_back_kernel(here, p0, p1, p2, p3, weight, mine, theirs):
    for half in range(2):
        total = jnp.zeros((128, D), f32)
        for d, ref in enumerate((p0, p1, p2, p3)):
            total = total + dot_nt(ref[128 * half : 128 * half + 128, :], weight[before(here[X], d)])
        store_half(mine, theirs, here[CORE], half, total)


def normed_back(here, *operands):
    return run(
        normed_back_kernel, "normed_back", here, operands, [((128, D), f32), ((128, D), f32)], megabytes=2
    )


def attend_quarter_kernel(here, normed, projected, sums, *out):
    grad_input = dot_tn(projected[...], normed[...])
    left = lax.broadcasted_iota(jnp.int32, (64, 128), 1) < 64
    for y in range(4):
        parts = []
        for z in range(2):
            tall = grad_input[:, 256 * y + 128 * z : 256 * y + 128 * z + 128].T
            query = jnp.where(left, tall[:64, 128:], pltpu.roll(tall[64:, 128:], 64, 1))
            last = jnp.zeros((16, 128), f32)
            if y == 0 and z == 0:
                last = jnp.concatenate([sums[0:1, :128], sums[0:1, 128:], last[:14]], axis=0)
            parts.append(jnp.concatenate([tall[:, :128], query, last], axis=0).astype(bf16)[None])
        store_at(out, here[Y], y, jnp.concatenate(parts, axis=0))


def attend_quarter(here, *operands):
    return run(attend_quarter_kernel, "attend_quarter", here, operands, [((2, 208, 128), bf16)] * 4, megabytes=5)


def add_four_kernel(here, p0, p1, p2, p3, out):
    total = p0[...].astype(f32) + p1[...].astype(f32) + p2[...].astype(f32) + p3[...].astype(f32)
    out[...] = total.astype(bf16)


def add_four(here, *pieces):
    return run(add_four_kernel, "add_four", here, pieces, [(pieces[0].shape, bf16)], megabytes=1)[0]


def feed_weights_kernel(here, shared, down, up, output_ref, *rest):
    small_refs, (inputs, blocks, arrived, sent) = rest[:8], rest[8:]
    loads = [pltpu.make_async_copy(shared.at[y], inputs.at[y], arrived.at[y]) for y in range(4)]
    for load in loads:
        load.start()
    copies = []
    for y in range(4):
        loads[y].wait()
        for x in range(4):
            blocks[y, :, 256 * x : 256 * x + 256] = inputs[y, x, 256:512, :].astype(f32)
        copies.append(pltpu.make_async_copy(blocks.at[y], up.at[pl.ds(256 * y, 256)], sent.at[y]))
        copies[-1].start()
    for x in range(4):
        for y in range(4):
            blocks[4 + x, :, 256 * y : 256 * y + 256] = inputs[y, x, :256, :].astype(f32)
        copies.append(pltpu.make_async_copy(blocks.at[4 + x], down.at[pl.ds(256 * x, 256)], sent.at[4 + x]))
        copies[-1].start()
    for x in range(4):
        tail = jnp.concatenate([inputs[y, x, 512:, :].astype(f32) for y in range(4)], axis=1)
        output_ref[64 * x : 64 * x + 64, :] = tail[:64]
        for k in range(2):
            small_refs[2 * x + k][...] = tail[64 + k : 65 + k]
    for copy in copies:
        copy.wait()


def feed_weights_out(here, shared):
    return pl.pallas_call(
        feed_weights_kernel,
        in_specs=[pl.BlockSpec(memory_space=pltpu.SMEM), pl.BlockSpec(memory_space=pl.ANY)],
        out_specs=[pl.BlockSpec(memory_space=pl.ANY)] * 2 + [pl.BlockSpec(memory_space=pltpu.VMEM)] * 9,
        out_shape=[jax.ShapeDtypeStruct((D, D), f32)] * 2
        + [jax.ShapeDtypeStruct((256, D), f32)]
        + [jax.ShapeDtypeStruct((1, D), f32)] * 8,
        scratch_shapes=[
            pltpu.VMEM((4, 4, 592, 256), bf16),
            pltpu.VMEM((8, 256, D), f32),
            pltpu.SemaphoreType.DMA((4,)),
            pltpu.SemaphoreType.DMA((8,)),
        ],
        compiler_params=pltpu.CompilerParams(vmem_limit_bytes=56 * 2**20),
        cost_estimate=pl.CostEstimate(flops=8 * 10**9, bytes_accessed=2**24, transcendentals=0),
        name="feed_weights",
    )(here, shared)


def attend_weights_kernel(here, *refs):
    parts, (input_ref, bias_ref), shared = refs[:4], refs[4:6], refs[6]
    for dx, ref in enumerate(parts):
        for dy in range(4):
            shared[before(here[Y], dy), before(here[X], dx)] = ref[dy]
    for y in range(4):
        for z in range(2):
            rows = slice(256 * y + 128 * z, 256 * y + 128 * z + 128)
            blocks = [shared[y, x, z].astype(f32) for x in range(4)]
            queries = [jnp.concatenate([b[128:192, :64], b[128:192, 64:]], axis=0) for b in blocks]
            input_ref[0, rows, :] = jnp.concatenate(queries, axis=1)
            input_ref[1, rows, :] = jnp.concatenate([b[:128, :64] for b in blocks], axis=1)
            input_ref[2, rows, :] = jnp.concatenate([b[:128, 64:] for b in blocks], axis=1)
            if y == 0 and z == 0:
                bias_ref[0:1, :] = jnp.concatenate([b[193:194, :64] for b in blocks], axis=1)
                bias_ref[1:2, :] = jnp.concatenate([b[192:193, :64] for b in blocks], axis=1)
                bias_ref[2:3, :] = jnp.concatenate([b[192:193, 64:] for b in blocks], axis=1)


def attend_weights_out(here, *operands):
    return run(
        attend_weights_kernel,
        "attend_weights",
        here,
        operands,
        [((3, D, 256), f32), ((3, 256), f32)],
        [pltpu.VMEM((4, 4, 2, 208, 128), bf16)],
        megabytes=9,
    )


def leave_kernel(here, total, other, stream, grad_middle, vec, kind, out_ref, last_ref, halves):
    halves[here[CORE]] = total[...]
    halves[1 - here[CORE]] = other[...]
    grad_normed = jnp.concatenate([halves[0], halves[1]], axis=0)
    unit, inv = norm_parts(stream[...])
    grad = grad_middle[...] + norm_back(grad_normed, unit, inv, vec[ATTEND_GAIN : ATTEND_GAIN + 1, :])
    out_ref[...] = grad
    kinds = jnp.broadcast_to(kind[...].astype(f32), (128, 256)).T[:, 0:1]
    last_ref[0:1, :] = jnp.sum(grad_normed * unit, axis=0, keepdims=True)
    last_ref[1:2, :] = jnp.sum(grad_normed, axis=0, keepdims=True)
    for c in range(3):
        last_ref[2 + c : 3 + c, :] = jnp.sum(jnp.where(kinds == c, grad, 0.0), axis=0, keepdims=True)
    last_ref[5:, :] = jnp.zeros((3, D), f32)


def leave(here, *operands):
    return run(
        leave_kernel,
        "leave",
        here,
        operands,
        [((256, D), f32), ((8, D), f32)],
        [pltpu.VMEM((2, 128, D), f32)],
        megabytes=7,
    )


def ring_sum(values, swap, opposite):
    values = values + lax.ppermute(values, "seq", swap)
    return values + lax.ppermute(values, "seq", opposite)


def last_sum_kernel(here, own, other, table_ref, gain_ref, bias_ref):
    total = own[...] + other[...]
    gain_ref[...] = total[0:1]
    bias_ref[...] = total[1:2]
    table_ref[...] = total[2:5]


def last_sum(here, own, other):
    return run(
        last_sum_kernel,
        "last_sum",
        here,
        (own, other),
        [((3, D), f32), ((1, D), f32), ((1, D), f32)],
        megabytes=1,
    )


ATTEND_GAIN, OUTPUT_BIAS, FEED_GAIN, FEED_BIAS, DOWN_BIAS, UP_BIAS, HIDDEN_GAIN, HIDDEN_BIAS, INNER = range(9)


def tables_of(positions, total_rows):
    pair_index = (jnp.arange(128) % 32).astype(f32)
    frequency = 1.0 / 10000.0 ** (pair_index / 32)
    angles = positions.astype(f32)[:, None] * frequency[None, :]
    ratios = (2.0 * pair_index + 0.4 * HEAD_DIM) / (1.4 * HEAD_DIM)
    exponent = (positions - total_rows // 2).astype(f32)[:, None] / scale_base
    return jnp.cos(angles), jnp.sin(angles), ratios[None, :] ** exponent


def back_tables(positions, total_rows, score_scale):
    lane = jnp.arange(128)
    cosine, sine, growth = tables_of(positions, total_rows)
    cosine = cosine * score_scale
    sine = sine * jnp.where(lane % 64 < 32, score_scale, -score_scale)[None]
    turned = (lane < 64)[None]
    factor = jnp.where(turned, 1.0 / growth, growth)
    return cosine * factor, sine * factor


def per_device(
    tokens,
    segment_kind,
    document,
    type_table,
    attend_gain,
    attend_bias,
    input_weight,
    input_bias,
    inner_gain,
    inner_bias,
    output_weight,
    output_bias,
    feed_gain,
    feed_bias,
    up_weight,
    up_bias,
    hidden_gain,
    hidden_bias,
    down_weight,
    down_bias,
    cotangent,
):
    local_rows = tokens.shape[0]
    total_rows = document.shape[0]
    local_width = input_weight.shape[2]
    score_scale = HEAD_DIM ** (-0.5)
    place = lax.axis_index("seq")
    part = lax.axis_index("ffn")
    y, z, x = place // 8, (place // 4) % 2, place % 4
    here = jnp.stack([x, y, z, part % 2, part, part, part, part]).astype(jnp.int32)
    query_pos = place * local_rows + jnp.arange(local_rows, dtype=jnp.int32)
    kind = segment_kind[None]

    stream, normed_low, *pieces = enter(
        here,
        tokens,
        kind,
        type_table,
        jnp.stack([attend_gain, attend_bias]),
        input_weight,
        input_bias,
        *tables_of(query_pos, total_rows),
    )
    received = shift_x(pieces)

    row_kv, row_q = rows(here, pieces[0], *received)
    kv_received = [lax.ppermute(row_kv, "seq", pairs) for pairs in Y_SHIFTS]
    queries_a = lax.ppermute(row_q, "seq", TO_SAME)
    queries_b = lax.ppermute(row_q, "seq", TO_OTHER)

    normed_row = gather_x(after(normed_low, row_kv))

    document = after(document, queries_a)
    begins = jnp.zeros((total_rows,), jnp.int32)
    for number in range(1, 4):
        begins = begins + jnp.where(
            document >= number, jnp.sum((document == number - 1).astype(jnp.int32)), 0
        )
    row_a = jnp.where(y % 2 == z, y, 7 - y)
    row_b = 7 - row_a
    begin_a = lax.dynamic_slice_in_dim(begins, row_a * ROW, ROW)
    begin_b = lax.dynamic_slice_in_dim(begins, row_b * ROW, ROW)
    begin = jnp.concatenate([begin_a, begin_b])[None]
    info = jnp.stack([z, row_a, row_b, begin_a[0], begin_b[0], begin_a[-1], begin_b[-1], y]).astype(
        jnp.int32
    )
    vec = jnp.concatenate(
        [
            v.astype(f32)
            for v in (
                attend_gain,
                output_bias,
                feed_gain,
                feed_bias,
                down_bias,
                up_bias,
                hidden_gain,
                hidden_bias,
                inner_gain,
                inner_bias,
            )
        ]
        + [jnp.zeros((16 * D - 8 * D - 512,), f32)]
    ).reshape(16, D)
    queries_a, queries_b, plane, vec, begin, info = lax.optimization_barrier(
        (queries_a, queries_b, [row_kv] + kv_received, vec, begin, info)
    )
    out_a, out_b, plane, queries = attend_forward(info, queries_a, queries_b, plane, begin)
    part_a = lax.ppermute(out_a, "seq", FROM_SAME)
    part_b = lax.ppermute(out_b, "seq", FROM_OTHER)
    mixed_row, logs_row, *pieces = combine(here, part_a, part_b)
    mixed, mine, theirs = inner(
        here, pieces[0], *shift_x(pieces), inner_gain[None], inner_bias[None], output_weight
    )
    chip = chip_stats(here, mine, core_swap(theirs))
    row_pos = (2 * y + z) * ROW + jnp.arange(ROW, dtype=jnp.int32)
    tables = back_tables(after(row_pos, chip), total_rows, score_scale)
    grad_hidden = jnp.einsum("td,fd->tf", after(cotangent, chip), down_weight, preferred_element_type=f32)
    total = join_stats(here, chip, far_swap(chip))
    total, tables, grad_hidden = lax.optimization_barrier((total, tables, grad_hidden))
    feed_low, inner_low, middle, before_act, inner_unit, inner_inv, sums, through = feed(
        here, total, core_swap(total), stream, vec, mixed, up_weight, grad_hidden
    )
    sums = sums + core_swap(sums)
    sums = sums + far_swap(sums)
    hidden_low, grad_pre, small_a, mine, theirs = hidden(
        here, sums, before_act, grad_hidden, vec, up_weight
    )
    chip = add_chip(here, mine, core_swap(theirs))
    total = add_far(here, chip, far_swap(chip))
    other = core_swap(total)
    grad_middle, small_b, *head_pieces, branch = middle_back(
        here,
        total,
        other,
        middle,
        stream,
        cotangent,
        vec,
        output_weight,
        inner_unit,
        inner_inv,
        through,
    )
    grad_pre, head_pieces = lax.optimization_barrier((grad_pre, head_pieces))
    head_received = shift_x(head_pieces)
    feed_parts = feed_grads(here, hidden_low, cotangent, grad_pre, feed_low, inner_low, branch, small_a, small_b)
    head_received, feed_parts, normed_row = lax.optimization_barrier((head_received, feed_parts, normed_row))
    feed_sums = lax.psum_scatter(feed_parts, "seq", scatter_dimension=0, axis_index_groups=X_GROUPS)
    message = grad_message(here, head_pieces[0], *head_received, mixed_row, logs_row)
    message_a = lax.ppermute(message, "seq", TO_SAME)
    message_b = lax.ppermute(message, "seq", TO_OTHER)
    weight_heads = head_weights(here, after(input_weight, message))
    message_a, message_b, weight_heads = lax.optimization_barrier((message_a, message_b, weight_heads))
    grad_qa, grad_qb, *kv_pieces = attend_backward(
        info, plane, queries, message_a, message_b, begin
    )
    kv_parts = shift_y(kv_pieces)
    q_parts = [lax.ppermute(grad_qa, "seq", FROM_SAME), lax.ppermute(grad_qb, "seq", FROM_OTHER)]
    feed_mine, feed_theirs = feed_out(here, after(hidden_low, kv_pieces[0]), down_weight)
    feed_chip = add_chip(here, feed_mine, core_swap(feed_theirs))
    feed_far = far_swap(feed_chip)
    kv_parts, q_parts, feed_chip = lax.optimization_barrier((kv_parts, q_parts, feed_chip))
    projected_row, projected_sums, *pieces = row_grads(here, kv_pieces[0], *kv_parts, *q_parts, *tables)
    back_received = shift_x(pieces)
    block_pieces = blocks(here, after(feed_sums, projected_row))
    block_received = shift_y(block_pieces)
    quarter_pieces = attend_quarter(here, normed_row, after(projected_row, block_pieces), projected_sums)
    block_received, back_received, quarter_pieces = lax.optimization_barrier(
        (block_received, back_received, quarter_pieces)
    )
    feed_pair = sum_z(pair(here, block_pieces[0], *block_received))
    quarter_received = shift_y(quarter_pieces)
    mine, theirs = normed_back(here, pieces[0], *back_received, weight_heads)
    mine, theirs, feed_pair = lax.optimization_barrier((mine, theirs, feed_pair))
    feed_shared = lax.all_gather(feed_pair, "seq", axis_index_groups=YX_GROUPS).reshape(4, 4, 592, 256)
    chip = add_chip(here, mine, core_swap(theirs))
    far, quarter_received = lax.optimization_barrier((far_swap(chip), quarter_received))
    total = add_far(here, chip, far)
    other = core_swap(total)
    attend_pair = sum_z(add_four(here, quarter_pieces[0], *quarter_received))
    grad_tokens, last = leave(here, total, other, stream, grad_middle, vec, kind)
    last, attend_pair = lax.optimization_barrier((last, attend_pair))
    attend_near = jnp.stack(ring(attend_pair, Y_SHIFTS))
    last = ring_sum(last, X_SWAP, X_SHIFTS[1])
    attend_near, last = lax.optimization_barrier((attend_near, last))
    attend_parts = ring(attend_near, X_SHIFTS)
    last = ring_sum(last, Y_SWAP, Y_SHIFTS[1])
    feed_chip, feed_far, last = lax.optimization_barrier((feed_chip, feed_far, last))
    last_other = lax.ppermute(last, "seq", Z_SWAP)
    total = add_far(here, feed_chip, feed_far)
    result = result_out(here, total, core_swap(total), middle, vec)
    grad_type_table, grad_attend_gain, grad_attend_bias = last_sum(here, last, last_other)
    grad_down_weight, grad_up_weight, grad_output_weight, *small = feed_weights_out(here, feed_shared)
    attend_parts, result, grad_type_table, grad_down_weight = lax.optimization_barrier(
        (attend_parts, result, grad_type_table, grad_down_weight)
    )
    grad_input_weight, grad_input_bias = attend_weights_out(here, *attend_parts)
    small = [v.reshape(D) for v in small]
    return (
        result,
        grad_tokens,
        grad_type_table,
        grad_attend_gain.reshape(D),
        grad_attend_bias.reshape(D),
        grad_input_weight,
        grad_input_bias,
        small[7][:local_width],
        small[7][local_width : 2 * local_width],
        grad_output_weight,
        small[5],
        small[3],
        small[4],
        grad_up_weight,
        small[2],
        small[0],
        small[1],
        grad_down_weight,
        small[6],
    )


def solution(mesh):
    in_specs = (
        P("seq", None),
        P("seq"),
        P(),
        P(),
        P(),
        P(),
        P(None, None, "ffn"),
        P(None, "ffn"),
        P("ffn"),
        P("ffn"),
        P("ffn", None),
        P(),
        P(),
        P(),
        P(None, "ffn"),
        P("ffn"),
        P("ffn"),
        P("ffn"),
        P("ffn", None),
        P(),
        P("seq", None),
    )
    out_specs = (
        P("seq", None),
        P("seq", None),
        P(),
        P(),
        P(),
        P(None, None, "ffn"),
        P(None, "ffn"),
        P("ffn"),
        P("ffn"),
        P("ffn", None),
        P(),
        P(),
        P(),
        P(None, "ffn"),
        P("ffn"),
        P("ffn"),
        P("ffn"),
        P("ffn", None),
        P(),
    )
    return jax.shard_map(
        per_device, mesh=mesh, in_specs=in_specs, out_specs=out_specs, check_vma=False
    )
```

```python
from functools import partial
import math

import jax
import jax.numpy as jnp
from jax import lax
from jax.experimental import pallas as pl
from jax.experimental.pallas import tpu as pltpu
from jax.sharding import PartitionSpec as P

D = 1024
FF = 4096
HEAD_DIM = 64
ROW = 1024
PACK = ROW // 2
PLANE = 4

epsilon = 1e-05
scale_base = 512.0
masked_score = -1e30
log2_e = 1.4426950408889634
score_factor = HEAD_DIM ** (-0.5) * log2_e
highest = lax.Precision.HIGHEST
f32 = jnp.float32
bf16 = jnp.bfloat16


def seq_index(y, z, x):
    return (y % 4) * 8 + (z % 2) * 4 + x % 4


def seq_pairs(move):
    pairs = []
    for y in range(4):
        for z in range(2):
            for x in range(4):
                pairs.append((seq_index(y, z, x), seq_index(*move(y, z, x))))
    return pairs


def shift_pairs(dy, dz, dx):
    return seq_pairs(lambda y, z, x: (y + dy, z + dz, x + dx))


def group_of(row):
    return min(row, 7 - row)


TO_SAME = seq_pairs(lambda y, z, x: (group_of(2 * y + z), z, x))
TO_OTHER = seq_pairs(lambda y, z, x: (group_of(2 * y + z), 1 - z, x))
FROM_SAME = [(b, a) for a, b in TO_SAME]
FROM_OTHER = [(b, a) for a, b in TO_OTHER]
X_SHIFTS = [shift_pairs(0, 0, d) for d in (1, 2, 3)]
Y_SHIFTS = [shift_pairs(d, 0, 0) for d in (1, 2, 3)]
Z_SWAP = shift_pairs(0, 1, 0)
X_SWAP = seq_pairs(lambda y, z, x: (y, z, x ^ 1))
Y_SWAP = seq_pairs(lambda y, z, x: (y ^ 1, z, x))
CORE_SWAP = [(f, f ^ 1) for f in range(4)]
FAR_SWAP = [(f, f ^ 2) for f in range(4)]
Y_GROUPS = [[seq_index(y, z, x) for y in range(4)] for z in range(2) for x in range(4)]
X_GROUPS = [[seq_index(y, z, x) for x in range(4)] for y in range(4) for z in range(2)]
Z_GROUPS = [[seq_index(y, z, x) for z in range(2)] for y in range(4) for x in range(4)]
YX_GROUPS = [[seq_index(y, z, x) for y in range(4) for x in range(4)] for z in range(2)]


def shift_x(pieces):
    return [lax.ppermute(piece, "seq", pairs) for piece, pairs in zip(pieces[1:], X_SHIFTS)]


def shift_y(pieces):
    return [lax.ppermute(piece, "seq", pairs) for piece, pairs in zip(pieces[1:], Y_SHIFTS)]


def core_swap(values):
    return lax.ppermute(values, "ffn", CORE_SWAP)


def far_swap(values):
    return lax.ppermute(values, "ffn", FAR_SWAP)


def gather_x(values):
    return lax.all_gather(values, "seq", axis_index_groups=X_GROUPS, tiled=True)


def ring(values, shifts):
    return [values] + [lax.ppermute(values, "seq", pairs) for pairs in shifts]


def sum_z(values):
    other = lax.ppermute(values, "seq", Z_SWAP)
    return (values.astype(f32) + other.astype(f32)).astype(bf16)


def after(value, *others):
    return lax.optimization_barrier((value,) + others)[0]


X, Y, Z, CORE, PART = range(5)


def run(kernel, name, here, operands, outs, scratch=(), megabytes=18, weight=0):
    return pl.pallas_call(
        kernel,
        in_specs=[pl.BlockSpec(memory_space=pltpu.SMEM)]
        + [pl.BlockSpec(memory_space=pltpu.VMEM)] * len(operands),
        out_specs=[pl.BlockSpec(memory_space=pltpu.VMEM)] * len(outs),
        out_shape=[jax.ShapeDtypeStruct(shape, kind) for shape, kind in outs],
        scratch_shapes=list(scratch),
        compiler_params=pltpu.CompilerParams(vmem_limit_bytes=megabytes * 2**20),
        cost_estimate=pl.CostEstimate(
            flops=2**20 + weight * 10**9,
            bytes_accessed=sum(v.size * v.dtype.itemsize for v in operands)
            + sum(math.prod(shape) * jnp.dtype(kind).itemsize for shape, kind in outs),
            transcendentals=0,
        ),
        name=name,
    )(here, *operands)


def dot_nn(a, b):
    return lax.dot_general(a, b, (((1,), (0,)), ((), ())), preferred_element_type=f32)


def dot_nt(a, b):
    return lax.dot_general(a, b, (((1,), (1,)), ((), ())), preferred_element_type=f32)


def dot_tn(a, b):
    return lax.dot_general(a, b, (((0,), (0,)), ((), ())), preferred_element_type=f32)


def before(place, d):
    return lax.rem(place + (4 - d), 4)


def store_at(refs, place, index, value):
    for d, ref in enumerate(refs):

        @pl.when(lax.rem(place + d, 4) == index)
        def _(ref=ref):
            ref[...] = value


def store_half(mine, theirs, core, half, value):
    @pl.when(core == half)
    def _():
        mine[...] = value

    @pl.when(core != half)
    def _():
        theirs[...] = value


def row_of(column):
    return jnp.broadcast_to(column, (column.shape[0], 128)).T[0:1]


def split_three(values):
    high = values.astype(bf16).astype(f32)
    middle = (values - high).astype(bf16).astype(f32)
    return high, middle, values - high - middle


def norm_parts(values):
    center = values - jnp.mean(values, axis=-1, keepdims=True)
    inv_std = lax.rsqrt(jnp.mean(center * center, axis=-1, keepdims=True) + epsilon)
    return center * inv_std, inv_std


def norm_back(grad_out, unit, inv_std, gain):
    scaled = grad_out * gain
    return inv_std * (
        scaled
        - jnp.mean(scaled, axis=-1, keepdims=True)
        - unit * jnp.mean(scaled * unit, axis=-1, keepdims=True)
    )


def pair_pack(values, side):
    left = lax.broadcasted_iota(jnp.int32, (128, 128), 1) < 64
    if side == 0:
        return jnp.where(left, values[:128], pltpu.roll(values[128:], 64, 1))
    return jnp.where(left, pltpu.roll(values[:128], 64, 1), values[128:])


def pair_unpack(even, odd):
    left = lax.broadcasted_iota(jnp.int32, (128, 128), 1) < 64
    low = jnp.where(left, even, pltpu.roll(odd, 64, 1))
    high = jnp.where(left, pltpu.roll(even, 64, 1), odd)
    return jnp.concatenate([low, high], axis=0)


def half_swapped(values):
    lane = lax.broadcasted_iota(jnp.int32, values.shape, 1)
    return jnp.where(lane % 64 < 32, pltpu.roll(values, 96, 1), pltpu.roll(values, 32, 1))


def enter_kernel(
    here, tokens, kind, table, norm, weight, shift, cosine, sine, growth, stream_ref, normed_ref, *out
):
    stream = tokens[...].astype(f32)
    kinds = jnp.broadcast_to(kind[...].astype(f32), (128, 256)).T[:, 0:1]
    for c in range(3):
        stream = stream + jnp.where(kinds == c, table[c : c + 1, :].astype(f32), 0.0)
    stream_ref[...] = stream
    unit, _ = norm_parts(stream)
    normed = (unit * norm[0:1, :].astype(f32) + norm[1:2, :].astype(f32)).astype(bf16)
    normed_ref[...] = normed
    projected = [dot_nn(normed, weight[s]) + shift[s : s + 1, :].astype(f32) for s in range(3)]
    lane = lax.broadcasted_iota(jnp.int32, (256, 128), 1)
    left = lane < 64
    signed = jnp.where(lane % 64 < 32, -sine[...], sine[...])
    for group in range(2):
        lanes = slice(128 * group, 128 * group + 128)
        query, key, value = [p[:, lanes] for p in projected]
        query = (query * cosine[...] + half_swapped(query) * signed) * growth[...]
        key = (key * cosine[...] + half_swapped(key) * signed) / growth[...]
        for side in range(2):
            if side == 0:
                both = jnp.where(left, key, pltpu.roll(value, 64, 1))
            else:
                both = jnp.where(left, pltpu.roll(key, 64, 1), value)
            message = jnp.concatenate([both, pair_pack(query, side)], axis=0).astype(bf16)
            store_at(out, here[X], 2 * group + side, message)


def enter(here, *operands):
    return run(
        enter_kernel,
        "enter",
        here,
        operands,
        [((256, D), f32), ((256, D), bf16)] + [((384, 128), bf16)] * 4,
        megabytes=3,
    )


def rows_kernel(here, p0, p1, p2, p3, kv_ref, q_ref):
    for d, ref in enumerate((p0, p1, p2, p3)):
        source = before(here[X], d)
        kv_ref[pl.ds(pl.multiple_of(source * 256, 256), 256), :] = ref[:256, :]
        q_ref[pl.ds(pl.multiple_of(source * 128, 128), 128), :] = ref[256:, :]


def rows(here, *pieces):
    return run(rows_kernel, "rows", here, pieces, [((ROW, 128), bf16), ((PACK, 128), bf16)], megabytes=1)


def lane_rows(row):
    return jnp.concatenate([row[:, 128 * j : 128 * j + 128] for j in range(8)], axis=0)


def unpack_transposed(source, target, offset):
    for b in range(4):
        piece = source[128 * b : 128 * b + 128, :].T
        target[offset : offset + 64, 256 * b : 256 * b + 128] = piece[:64]
        target[offset : offset + 64, 256 * b + 128 : 256 * b + 256] = piece[64:]


def pack_transposed(columns, target):
    for b in range(4):
        piece = jnp.concatenate(
            [columns[:, 256 * b : 256 * b + 128], columns[:, 256 * b + 128 : 256 * b + 256]], axis=0
        )
        target[128 * b : 128 * b + 128, :] = piece.T.astype(target.dtype)


def chunk_bounds(info, tile):
    z = info[0]
    row = info[1 + tile]
    lowest = info[3 + tile]
    first = jnp.int32(0)
    last = jnp.int32(0)
    for c in range(PLANE):
        start = (2 * c + z) * ROW
        first = first + (start + ROW - 1 < lowest).astype(jnp.int32)
        last = last + (2 * c + z <= row).astype(jnp.int32)
    return first, last


def visible(info, tile, c, begin_ref, keys, queries):
    shape = (keys.stop - keys.start, queries.stop - queries.start)
    key = (2 * c + info[0]) * ROW + keys.start + lax.broadcasted_iota(jnp.int32, shape, 0)
    query = info[1 + tile] * ROW + queries.start + lax.broadcasted_iota(jnp.int32, shape, 1)
    return (key <= query) & (key >= begin_ref[:, queries])


def each_block(info, tile, step):
    whole, low, high = slice(0, ROW), slice(0, ROW // 2), slice(ROW // 2, ROW)

    def body(c, carry):
        own = 2 * c + info[0] == info[1 + tile]
        masked = jnp.logical_not(own) & needs_mask(info, tile, c)

        @pl.when(own)
        def _():
            step(c, True, low, whole)
            step(c, True, high, high)

        @pl.when(masked)
        def _():
            step(c, True, whole, whole)

        @pl.when(jnp.logical_not(own | masked))
        def _():
            step(c, False, whole, whole)

        return carry

    first, last = chunk_bounds(info, tile)
    lax.fori_loop(first, last, body, 0)


def needs_mask(info, tile, c):
    key_row = 2 * c + info[0]
    return (key_row == info[1 + tile]) | (key_row * ROW < info[5 + tile])


def plane_copies(info, pieces, kv_ref):
    return [
        (piece, kv_ref.at[pl.ds(pl.multiple_of(before(info[7], d) * ROW, ROW), ROW)])
        for d, piece in enumerate(pieces)
    ]


def forward_kernel(
    info,
    qa,
    qb,
    kv0,
    kv1,
    kv2,
    kv3,
    begin_ref,
    outa_ref,
    outb_ref,
    kv_ref,
    q_in,
    qt_ref,
    vt_ref,
    acc_ref,
    top_ref,
    semaphores,
):
    tile = pl.program_id(0)

    @pl.when(tile == 0)
    def _():
        copies = [
            pltpu.make_async_copy(source, target, semaphores.at[k])
            for k, (source, target) in enumerate(
                [(qa, q_in.at[0]), (qb, q_in.at[1])] + plane_copies(info, (kv0, kv1, kv2, kv3), kv_ref)
            )
        ]
        for copy in copies:
            copy.start()
        for copy in copies:
            copy.wait()
        for c in range(PLANE):
            block = kv_ref[c * ROW : c * ROW + ROW, :].T
            index = lax.broadcasted_iota(jnp.int32, block.shape, 0)
            vt_ref[:, c * ROW : c * ROW + ROW] = jnp.where(index < 64, jnp.ones_like(block), block)
        qt_ref[64:, :] = jnp.zeros((64, ROW), bf16)

    unpack_transposed(q_in.at[tile], qt_ref, 0)

    top_ref[...] = jnp.full(top_ref.shape, masked_score, f32)
    acc_ref[...] = jnp.zeros(acc_ref.shape, f32)

    def step(c, masked, keys, queries):
        start = pl.multiple_of(c * ROW + keys.start, ROW // 2)
        count = keys.stop - keys.start
        scores = dot_nn(kv_ref[pl.ds(start, count), :], qt_ref[:, queries]) * score_factor
        if masked:
            seen = visible(info, tile, c, begin_ref, keys, queries)
            scores = jnp.where(seen, scores, 2 * masked_score)
        old = top_ref[:, queries]
        top = jnp.maximum(old, jnp.max(scores, axis=0, keepdims=True))
        weights = jnp.exp2(scores - top)
        top_ref[:, queries] = top
        acc_ref[:, queries] = acc_ref[:, queries] * jnp.exp2(old - top) + dot_nn(
            vt_ref[:, pl.ds(start, count)], weights.astype(bf16)
        )

    each_block(info, tile, step)
    total = acc_ref[0:1, :]
    some = total > 0
    safe = jnp.where(some, total, 1.0)
    log_total = jnp.where(some, top_ref[...] + jnp.log2(safe), masked_score)
    for index, out_ref in enumerate((outa_ref, outb_ref)):

        @pl.when(tile == index)
        def _(out_ref=out_ref):
            pack_transposed(acc_ref[64:, :] / safe, out_ref)
            parts = [lane_rows(part) for part in split_three(log_total)]
            out_ref[PACK:, :] = jnp.concatenate(parts + [jnp.zeros((8, 128), f32)], axis=0).astype(bf16)


def attend_forward(info, queries_a, queries_b, keys_values, begin):
    hbm = pl.BlockSpec(memory_space=pltpu.HBM)
    return pl.pallas_call(
        forward_kernel,
        grid_spec=pltpu.PrefetchScalarGridSpec(
            num_scalar_prefetch=1,
            grid=(2,),
            in_specs=[hbm] * 6 + [pl.BlockSpec((1, ROW), lambda i, s: (0, i))],
            out_specs=[pl.BlockSpec(memory_space=pltpu.VMEM)] * 4,
            scratch_shapes=[
                pltpu.VMEM((128, ROW), bf16),
                pltpu.VMEM((128, PLANE * ROW), bf16),
                pltpu.VMEM((128, ROW), f32),
                pltpu.VMEM((1, ROW), f32),
                pltpu.SemaphoreType.DMA((6,)),
            ],
        ),
        out_shape=[jax.ShapeDtypeStruct((PACK + 32, 128), bf16)] * 2
        + [jax.ShapeDtypeStruct((PLANE * ROW, 128), bf16), jax.ShapeDtypeStruct((2, PACK, 128), bf16)],
        compiler_params=pltpu.CompilerParams(vmem_limit_bytes=9 * 2**20),
        cost_estimate=pl.CostEstimate(flops=10 * 10**9, bytes_accessed=2**21, transcendentals=0),
        name="attend_forward",
    )(info, queries_a, queries_b, *keys_values, begin)


def combine_kernel(here, a_ref, b_ref, full_ref, log_ref, *out):
    logs = []
    for ref in (a_ref, b_ref):
        rows = ref[PACK:, :].astype(f32)
        logs.append(rows[:8] + rows[8:16] + rows[16:24])
    top = jnp.maximum(logs[0], logs[1])
    shares = [jnp.exp2(part - top) for part in logs]
    total = shares[0] + shares[1]
    log_ref[...] = top + jnp.log2(total)
    columns = [(share / total).T for share in shares]
    left = lax.broadcasted_iota(jnp.int32, (128, 128), 1) < 64
    for b in range(4):
        mixed = jnp.zeros((128, 128), f32)
        for ref, column in zip((a_ref, b_ref), columns):
            weight = jnp.where(left, column[:, 2 * b : 2 * b + 1], column[:, 2 * b + 1 : 2 * b + 2])
            mixed = mixed + weight * ref[128 * b : 128 * b + 128, :].astype(f32)
        full_ref[128 * b : 128 * b + 128, :] = mixed
        store_at(out, here[X], b, mixed.astype(bf16))


def combine(here, part_a, part_b):
    return run(
        combine_kernel,
        "combine",
        here,
        (part_a, part_b),
        [((PACK, 128), f32), ((8, 128), f32)] + [((128, 128), bf16)] * 4,
        megabytes=1,
    )


def grad_message_kernel(here, p0, p1, p2, p3, mixed_ref, log_ref, out_ref):
    for d, ref in enumerate((p0, p1, p2, p3)):
        out_ref[pl.ds(pl.multiple_of(before(here[X], d) * 128, 128), 128), :] = ref[...]
    deltas = []
    for b in range(4):
        rows = slice(128 * b, 128 * b + 128)
        each = (out_ref[rows, :].astype(f32) * mixed_ref[rows, :]).T
        deltas.append(jnp.sum(each[:64], axis=0, keepdims=True))
        deltas.append(jnp.sum(each[64:], axis=0, keepdims=True))
    parts = list(split_three(log_ref[...])) + list(split_three(jnp.concatenate(deltas, axis=0)))
    out_ref[PACK:, :] = jnp.concatenate(parts, axis=0).astype(bf16)


def grad_message(here, *operands):
    return run(grad_message_kernel, "grad_message", here, operands, [((PACK + 48, 128), bf16)], megabytes=1)[0]


def backward_kernel(
    info,
    plane,
    queries,
    ma,
    mb,
    begin_ref,
    dqa_ref,
    dqb_ref,
    own_ref,
    one_ref,
    two_ref,
    three_ref,
    qt_ref,
    gt_ref,
    q_ref,
    g_ref,
    kv_ref,
    kt_ref,
    row_ref,
    acc_ref,
    dq_acc,
    q_in,
    m_in,
    semaphores,
):
    tile = pl.program_id(0)

    def load(query_ref, message_ref):
        unpack_transposed(query_ref, qt_ref, 0)
        unpack_transposed(message_ref, gt_ref, 64)
        q_ref[...] = qt_ref[...].T
        g_ref[...] = gt_ref[...].T
        rows = message_ref[PACK:, :].astype(f32)
        for k in range(2):
            part = rows[24 * k : 24 * k + 8] + rows[24 * k + 8 : 24 * k + 16] + rows[24 * k + 16 : 24 * k + 24]
            for j in range(8):
                row_ref[k : k + 1, 128 * j : 128 * j + 128] = part[j : j + 1, :]

    @pl.when(tile == 0)
    def _():
        copies = [
            pltpu.make_async_copy(source, target, semaphores.at[k])
            for k, (source, target) in enumerate(
                [(queries, q_in), (ma, m_in.at[0]), (mb, m_in.at[1]), (plane, kv_ref)]
            )
        ]
        for copy in copies:
            copy.start()
        acc_ref[...] = jnp.zeros(acc_ref.shape, f32)
        qt_ref[64:, :] = jnp.zeros((64, ROW), bf16)
        gt_ref[:64, :] = jnp.zeros((64, ROW), bf16)
        for copy in copies:
            copy.wait()
        for c in range(PLANE):
            kt_ref[:, c * ROW : c * ROW + ROW] = kv_ref[c * ROW : c * ROW + ROW, :].T

    load(q_in.at[tile], m_in.at[tile])
    dq_acc[...] = jnp.zeros(dq_acc.shape, f32)

    def step(c, masked, keys, queries):
        start = pl.multiple_of(c * ROW + keys.start, ROW // 2)
        count = keys.stop - keys.start
        block = kv_ref[pl.ds(start, count), :]
        scores = dot_nn(block, qt_ref[:, queries]) * score_factor
        if masked:
            seen = visible(info, tile, c, begin_ref, keys, queries)
            scores = jnp.where(seen, scores, 2 * masked_score)
        weights = jnp.exp2(scores - row_ref[0:1, queries])
        grad_weights = dot_nn(block, gt_ref[:, queries])
        grad_scores = (weights * (grad_weights - row_ref[1:2, queries])).astype(bf16)
        acc_ref[pl.ds(start, count), :] += dot_nn(grad_scores, q_ref[queries, :]) + dot_nn(
            weights.astype(bf16), g_ref[queries, :]
        )
        dq_acc[:, queries] += dot_nn(kt_ref[:, pl.ds(start, count)], grad_scores)

    each_block(info, tile, step)

    @pl.when(tile == 0)
    def _():
        pack_transposed(dq_acc[:64, :], dqa_ref)

    @pl.when(tile == 1)
    def _():
        pack_transposed(dq_acc[:64, :], dqb_ref)
        for d, ref in enumerate((own_ref, one_ref, two_ref, three_ref)):
            start = pl.multiple_of(lax.rem(info[7] + d, 4) * ROW, ROW)
            ref[...] = acc_ref[pl.ds(start, ROW), :].astype(bf16)


def attend_backward(info, plane, queries, message_a, message_b, begin):
    packed = pl.BlockSpec((PACK, 128), lambda i, s: (0, 0))
    hbm = pl.BlockSpec(memory_space=pltpu.HBM)
    block = pl.BlockSpec((ROW, 128), lambda i, s: (0, 0))
    return pl.pallas_call(
        backward_kernel,
        grid_spec=pltpu.PrefetchScalarGridSpec(
            num_scalar_prefetch=1,
            grid=(2,),
            in_specs=[hbm] * 4 + [pl.BlockSpec((1, ROW), lambda i, s: (0, i))],
            out_specs=[packed] * 2 + [block] * 4,
            scratch_shapes=[
                pltpu.VMEM((128, ROW), bf16),
                pltpu.VMEM((128, ROW), bf16),
                pltpu.VMEM((ROW, 128), bf16),
                pltpu.VMEM((ROW, 128), bf16),
                pltpu.VMEM((PLANE * ROW, 128), bf16),
                pltpu.VMEM((128, PLANE * ROW), bf16),
                pltpu.VMEM((8, ROW), f32),
                pltpu.VMEM((PLANE * ROW, 128), f32),
                pltpu.VMEM((128, ROW), f32),
                pltpu.VMEM((2, PACK, 128), bf16),
                pltpu.VMEM((2, PACK + 48, 128), bf16),
                pltpu.SemaphoreType.DMA((4,)),
            ],
        ),
        out_shape=[jax.ShapeDtypeStruct((PACK, 128), bf16)] * 2
        + [jax.ShapeDtypeStruct((ROW, 128), bf16)] * 4,
        compiler_params=pltpu.CompilerParams(vmem_limit_bytes=16 * 2**20),
        cost_estimate=pl.CostEstimate(flops=18 * 10**9, bytes_accessed=2**22, transcendentals=0),
        name="attend_backward",
    )(info, plane, queries, message_a, message_b, begin)


def inner_kernel(here, p0, p1, p2, p3, gain, shift, weight, mixed_ref, mine, theirs, heads):
    for d, ref in enumerate((p0, p1, p2, p3)):
        heads[before(here[X], d)] = ref[...].astype(f32)
    mixed = jnp.concatenate([pair_unpack(heads[0], heads[1]), pair_unpack(heads[2], heads[3])], axis=1)
    mixed_ref[...] = mixed
    mean = jnp.mean(mixed, axis=-1, keepdims=True)
    centred = mixed - mean
    spread = jnp.sum(centred * centred, axis=-1, keepdims=True)
    gains = gain[...].astype(f32)
    projected = dot_nn((centred * gains).astype(bf16), weight[...])
    full = weight[...].astype(f32)
    gain_column = jnp.broadcast_to(gains, (128, 256)).T[:, 0:1]
    shift_column = jnp.broadcast_to(shift[...].astype(f32), (128, 256)).T[:, 0:1]
    through = jnp.sum(full * gain_column, axis=0, keepdims=True)
    vectors = [jnp.where(here[PART] == k, through, 0.0) for k in range(4)]
    vectors.append(jnp.sum(full * shift_column, axis=0, keepdims=True))
    for half in range(2):
        tokens = slice(128 * half, 128 * half + 128)
        stats = [row_of(mean[tokens]), row_of(spread[tokens])]
        slots = [jnp.where(here[PART] == j // 2, stats[j % 2], 0.0) for j in range(8)]
        rows = vectors + [jnp.concatenate(slots, axis=1), jnp.zeros((2, D), f32)]
        store_half(mine, theirs, here[CORE], half, jnp.concatenate([projected[tokens]] + rows, axis=0))


def inner(here, *operands):
    return run(
        inner_kernel,
        "inner",
        here,
        operands,
        [((256, 256), f32), ((136, D), f32), ((136, D), f32)],
        [pltpu.VMEM((4, 128, 128), f32)],
        megabytes=4,
    )


def chip_stats_kernel(here, mine, other, out):
    total = mine[...] + other[...]
    parts = list(split_three(total[128:])) + [jnp.zeros((8, D), f32)]
    out[...] = jnp.concatenate([total[:128]] + parts, axis=0).astype(bf16)


def join_stats_kernel(here, chip, far, out):
    total = chip[...].astype(f32) + far[...].astype(f32)
    out[...] = jnp.concatenate([total[:128], total[128:136] + total[136:144] + total[144:152]], axis=0)


def add_chip_kernel(here, mine, other, out):
    out[...] = (mine[...] + other[...]).astype(bf16)


def add_far_kernel(here, chip, far, out):
    out[...] = chip[...].astype(f32) + far[...].astype(f32)


def chip_stats(here, mine, other):
    return run(chip_stats_kernel, "chip_stats", here, (mine, other), [((160, D), bf16)], megabytes=1)[0]


def join_stats(here, chip, far):
    return run(join_stats_kernel, "join_stats", here, (chip, far), [((136, D), f32)], megabytes=1)[0]


def add_chip(here, mine, other):
    return run(add_chip_kernel, "add_chip", here, (mine, other), [((128, D), bf16)], megabytes=1)[0]


def add_far(here, chip, far):
    return run(add_far_kernel, "add_far", here, (chip, far), [((128, D), f32)], megabytes=1)[0]


def sum_ffn(here, mine, theirs):
    chip = add_chip(here, mine, core_swap(theirs))
    total = add_far(here, chip, far_swap(chip))
    return total, core_swap(total)


def gauss_share(values):
    return 0.5 + 0.5 * lax.erf(values * math.sqrt(0.5))


def feed_kernel(
    here,
    total,
    other,
    stream,
    vec,
    mixed_ref,
    weight,
    grad_hidden,
    low_ref,
    inner_ref,
    middle_ref,
    before_ref,
    unit_ref,
    inv_ref,
    sums_ref,
    vectors_ref,
    halves,
):
    halves[here[CORE]] = total[...]
    halves[1 - here[CORE]] = other[...]
    vectors = halves[0, 128:, :]
    vectors_ref[...] = vectors
    ending = vectors[4:5, :] + vec[OUTPUT_BIAS : OUTPUT_BIAS + 1, :]
    inner_gain = vec[INNER : INNER + 1, :256]
    inner_bias = vec[INNER : INNER + 1, 256:512]
    for half in range(2):
        tokens = slice(128 * half, 128 * half + 128)
        stats = jnp.concatenate([halves[half, 133:134, 128 * j : 128 * j + 128] for j in range(8)], axis=0).T
        means = [stats[:, 2 * k : 2 * k + 1] for k in range(4)]
        mean = (means[0] + means[1] + means[2] + means[3]) * 0.25
        spread = stats[:, 1:2] + stats[:, 3:4] + stats[:, 5:6] + stats[:, 7:8]
        projected = halves[half, :128, :]
        for k in range(4):
            move = means[k] - mean
            spread = spread + 256.0 * move * move
            projected = projected + move * vectors[k : k + 1, :]
        inv = lax.rsqrt(spread / D + epsilon)
        middle_ref[tokens, :] = stream[tokens, :] + projected * inv + ending
        unit = (mixed_ref[tokens, :] - mean) * inv
        unit_ref[tokens, :] = unit
        inv_ref[tokens, :] = jnp.broadcast_to(inv, (128, 128))
        inner_ref[tokens, :] = (unit * inner_gain + inner_bias).astype(bf16)
    unit, _ = norm_parts(middle_ref[...])
    low_ref[...] = (
        unit * vec[FEED_GAIN : FEED_GAIN + 1, :] + vec[FEED_BIAS : FEED_BIAS + 1, :]
    ).astype(bf16)
    before_act = dot_nn(low_ref[...], weight[...]) + vec[UP_BIAS : UP_BIAS + 1, :]
    before_ref[...] = before_act
    active = before_act * gauss_share(before_act)
    scaled = grad_hidden[...] * vec[HIDDEN_GAIN : HIDDEN_GAIN + 1, :]
    columns = [
        jnp.sum(part, axis=-1, keepdims=True) for part in (active, active * active, scaled, scaled * active)
    ]
    lane = lax.broadcasted_iota(jnp.int32, (256, 128), 1)
    spread = jnp.zeros((256, 128), f32)
    for k, column in enumerate(columns):
        spread = jnp.where(lane == k, column, spread)
    sums_ref[...] = spread.T[:8]


def feed(here, *operands):
    return run(
        feed_kernel,
        "feed",
        here,
        operands,
        [
            ((256, D), bf16),
            ((256, 256), bf16),
            ((256, D), f32),
            ((256, D), f32),
            ((256, 256), f32),
            ((256, 128), f32),
            ((8, 256), f32),
            ((8, D), f32),
        ],
        [pltpu.VMEM((2, 136, D), f32)],
        megabytes=6,
    )


def hidden_kernel(
    here, sums, before_ref, grad_hidden, vec, weight, low_ref, grad_ref, small_ref, mine, theirs
):
    before_act = before_ref[...]
    share = gauss_share(before_act)
    slope = share + before_act * jnp.exp(-0.5 * before_act * before_act) * (1.0 / math.sqrt(2.0 * math.pi))
    columns = sums[...].T
    mean = columns[:, 0:1] / FF
    inv = lax.rsqrt(columns[:, 1:2] / FF - mean * mean + epsilon)
    first = columns[:, 2:3]
    cross = inv * (columns[:, 3:4] - mean * first)
    gain = vec[HIDDEN_GAIN : HIDDEN_GAIN + 1, :]
    unit = (before_act * share - mean) * inv
    low_ref[...] = (unit * gain + vec[HIDDEN_BIAS : HIDDEN_BIAS + 1, :]).astype(bf16)
    grad_out = grad_hidden[...]
    grad_pre = (inv * (grad_out * gain - first / FF - unit * (cross / FF)) * slope).astype(bf16)
    small_ref[0:1, :] = jnp.sum(grad_out * unit, axis=0, keepdims=True)
    small_ref[1:2, :] = jnp.sum(grad_out, axis=0, keepdims=True)
    small_ref[2:3, :] = jnp.sum(grad_pre.astype(f32), axis=0, keepdims=True)
    small_ref[3:, :] = jnp.zeros((5, D), f32)
    grad_ref[...] = grad_pre
    back = dot_nt(grad_pre, weight[...])
    for half in range(2):
        store_half(mine, theirs, here[CORE], half, back[128 * half : 128 * half + 128])


def hidden(here, *operands):
    return run(
        hidden_kernel,
        "hidden",
        here,
        operands,
        [((256, D), bf16), ((256, D), bf16), ((8, D), f32), ((128, D), f32), ((128, D), f32)],
        megabytes=6,
    )


def feed_out_kernel(here, low_ref, weight, mine, theirs):
    for half in range(2):
        tokens = slice(128 * half, 128 * half + 128)
        store_half(mine, theirs, here[CORE], half, dot_nn(low_ref[tokens, :], weight[...]))


def feed_out(here, low, weight):
    return run(
        feed_out_kernel, "feed_out", here, (low, weight), [((128, D), f32), ((128, D), f32)], megabytes=2
    )


def result_kernel(here, total, other, middle, vec, out, halves):
    halves[here[CORE]] = total[...]
    halves[1 - here[CORE]] = other[...]
    for half in range(2):
        tokens = slice(128 * half, 128 * half + 128)
        out[tokens, :] = (
            middle[tokens, :] + halves[half] + vec[DOWN_BIAS : DOWN_BIAS + 1, :]
        ).astype(bf16)


def result_out(here, *operands):
    return run(
        result_kernel,
        "result",
        here,
        operands,
        [((256, D), bf16)],
        [pltpu.VMEM((2, 128, D), f32)],
        megabytes=4,
    )[0]


def feed_grads_kernel(here, low, cotangent, grad_pre, feed_low, inner_low, branch, small_a, small_b, out):
    grads = dot_tn(inner_low[...], branch[...])
    vectors = [small_a[k : k + 1, :] for k in range(3)] + [small_b[k : k + 1, :] for k in range(5)]
    for k in range(4):
        lanes = slice(256 * k, 256 * k + 256)
        parts = [dot_tn(low[:, lanes], cotangent[...]), dot_tn(grad_pre[:, lanes], feed_low[...])]
        parts += [grads[64 * k : 64 * k + 64], vectors[2 * k], vectors[2 * k + 1], jnp.zeros((14, D), f32)]
        out[k] = jnp.concatenate(parts, axis=0).astype(bf16)


def feed_grads(here, *operands):
    return run(feed_grads_kernel, "feed_grads", here, operands, [((4, 592, D), bf16)], megabytes=8)[0]


def blocks_kernel(here, total, *out):
    for k in range(4):
        store_at(out, here[Y], k, total[:, 256 * k : 256 * k + 256])


def blocks(here, total):
    return run(blocks_kernel, "blocks", here, (total,), [((total.shape[0], 256), bf16)] * 4, megabytes=2)


def pair_kernel(here, p0, p1, p2, p3, out):
    total = p0[...].astype(f32) + p1[...].astype(f32) + p2[...].astype(f32) + p3[...].astype(f32)
    out[...] = jnp.concatenate([total[:256], total[256:512].T, total[512:]], axis=0).astype(bf16)


def pair(here, *pieces):
    return run(pair_kernel, "pair", here, pieces, [((592, 256), bf16)], megabytes=3)[0]


def middle_back_kernel(
    here,
    total,
    other,
    middle,
    stream,
    cotangent,
    vec,
    weight,
    unit_ref,
    inv_ref,
    vectors,
    grad_ref,
    small_ref,
    h0,
    h1,
    h2,
    h3,
    low_ref,
    halves,
):
    halves[here[CORE]] = total[...]
    halves[1 - here[CORE]] = other[...]
    grad_feed = jnp.concatenate([halves[0], halves[1]], axis=0)
    unit, inv = norm_parts(middle[...])
    grad_result = cotangent[...].astype(f32)
    grad_middle = grad_result + norm_back(grad_feed, unit, inv, vec[FEED_GAIN : FEED_GAIN + 1, :])
    grad_ref[...] = grad_middle
    low = grad_middle.astype(bf16)
    branch = low.astype(f32)
    low_ref[...] = low
    grad_inner = dot_nt(low, weight[...])
    through = vectors[0:1, :] + vectors[1:2, :] + vectors[2:3, :] + vectors[3:4, :]
    first = jnp.sum(branch * through, axis=-1, keepdims=True)
    ending = vectors[4:5, :] + vec[OUTPUT_BIAS : OUTPUT_BIAS + 1, :]
    cross = jnp.sum(branch * (middle[...] - stream[...] - ending), axis=-1, keepdims=True)
    inner_unit = unit_ref[...]
    inner_inv = inv_ref[:, 0:1]
    grad_mixed = inner_inv * (
        grad_inner * vec[INNER : INNER + 1, :256] - first / D - inner_unit * (cross / D)
    )
    for group in range(2):
        lanes = grad_mixed[:, 128 * group : 128 * group + 128]
        for side in range(2):
            store_at((h0, h1, h2, h3), here[X], 2 * group + side, pair_pack(lanes, side).astype(bf16))
    small_ref[0:1, :] = jnp.sum(grad_feed * unit, axis=0, keepdims=True)
    small_ref[1:2, :] = jnp.sum(grad_feed, axis=0, keepdims=True)
    small_ref[2:3, :] = jnp.sum(branch, axis=0, keepdims=True)
    small_ref[3:4, :] = jnp.sum(grad_result, axis=0, keepdims=True)
    small_ref[4:5, :256] = jnp.sum(grad_inner * inner_unit, axis=0, keepdims=True)
    small_ref[4:5, 256:512] = jnp.sum(grad_inner, axis=0, keepdims=True)
    small_ref[4:5, 512:] = jnp.zeros((1, 512), f32)
    small_ref[5:, :] = jnp.zeros((3, D), f32)


def middle_back(here, *operands):
    return run(
        middle_back_kernel,
        "middle_back",
        here,
        operands,
        [((256, D), f32), ((8, D), f32)] + [((128, 128), bf16)] * 4 + [((256, D), bf16)],
        [pltpu.VMEM((2, 128, D), f32)],
        megabytes=8,
    )


def row_grads_kernel(
    here, own, one, two, three, qa, qb, cos_in, sin_in, out_ref, sums_ref, p0, p1, p2, p3
):
    left = lax.broadcasted_iota(jnp.int32, (128, 128), 1) < 64

    def turned(values, cos_part, sin_part):
        return (values * cos_part + half_swapped(values) * sin_part).astype(bf16)

    for b in range(8):
        rows = slice(128 * b, 128 * b + 128)
        total = own[rows, :].astype(f32)
        for ref in (one, two, three):
            total = total + ref[rows, :].astype(f32)
        out_ref[rows, :128] = turned(
            total, jnp.where(left, cos_in[rows, :], 1.0), jnp.where(left, sin_in[rows, :], 0.0)
        )
    for b in range(4):
        rows = slice(128 * b, 128 * b + 128)
        total = qa[rows, :].astype(f32) + qb[rows, :].astype(f32)
        for side in range(2):
            tokens = slice(256 * b + 128 * side, 256 * b + 128 * side + 128)
            values = total if side == 0 else pltpu.roll(total, 64, 1)
            values = jnp.where(left, values, 0.0)
            out_ref[tokens, 128:] = turned(
                values, pltpu.roll(cos_in[tokens, :], 64, 1), pltpu.roll(sin_in[tokens, :], 64, 1)
            )
    for b in range(4):
        store_at((p0, p1, p2, p3), here[X], b, out_ref[256 * b : 256 * b + 256, :])
    sums_ref[...] = jnp.broadcast_to(jnp.sum(out_ref[...].astype(f32), axis=0, keepdims=True), (8, 256))


def row_grads(here, *operands):
    return run(
        row_grads_kernel,
        "row_grads",
        here,
        operands,
        [((ROW, 256), bf16), ((8, 256), f32)] + [((256, 256), bf16)] * 4,
        megabytes=3,
    )


def head_weights_kernel(here, weight, out):
    left = lax.broadcasted_iota(jnp.int32, (256, 128), 1) < 64
    for r in range(4):
        rows = slice(256 * r, 256 * r + 256)
        for group in range(2):
            lanes = slice(128 * group, 128 * group + 128)
            query, key, value = [weight[s, rows, lanes].astype(f32) for s in range(3)]
            even = [jnp.where(left, key, pltpu.roll(value, 64, 1)), jnp.where(left, query, 0.0)]
            odd = [
                jnp.where(left, pltpu.roll(key, 64, 1), value),
                jnp.where(left, pltpu.roll(query, 64, 1), 0.0),
            ]
            for side, parts in enumerate((even, odd)):
                out[2 * group + side, rows, :] = jnp.concatenate(parts, axis=1).astype(bf16)


def head_weights(here, weight):
    return run(head_weights_kernel, "head_weights", here, (weight,), [((4, D, 256), bf16)], megabytes=2)[0]


def normed_back_kernel(here, p0, p1, p2, p3, weight, mine, theirs):
    for half in range(2):
        total = jnp.zeros((128, D), f32)
        for d, ref in enumerate((p0, p1, p2, p3)):
            total = total + dot_nt(ref[128 * half : 128 * half + 128, :], weight[before(here[X], d)])
        store_half(mine, theirs, here[CORE], half, total)


def normed_back(here, *operands):
    return run(
        normed_back_kernel, "normed_back", here, operands, [((128, D), f32), ((128, D), f32)], megabytes=2
    )


def attend_quarter_kernel(here, normed, projected, sums, *out):
    grad_input = dot_tn(projected[...], normed[...])
    left = lax.broadcasted_iota(jnp.int32, (64, 128), 1) < 64
    for y in range(4):
        parts = []
        for z in range(2):
            tall = grad_input[:, 256 * y + 128 * z : 256 * y + 128 * z + 128].T
            query = jnp.where(left, tall[:64, 128:], pltpu.roll(tall[64:, 128:], 64, 1))
            last = jnp.zeros((16, 128), f32)
            if y == 0 and z == 0:
                last = jnp.concatenate([sums[0:1, :128], sums[0:1, 128:], last[:14]], axis=0)
            parts.append(jnp.concatenate([tall[:, :128], query, last], axis=0).astype(bf16)[None])
        store_at(out, here[Y], y, jnp.concatenate(parts, axis=0))


def attend_quarter(here, *operands):
    return run(attend_quarter_kernel, "attend_quarter", here, operands, [((2, 208, 128), bf16)] * 4, megabytes=5)


def add_four_kernel(here, p0, p1, p2, p3, out):
    total = p0[...].astype(f32) + p1[...].astype(f32) + p2[...].astype(f32) + p3[...].astype(f32)
    out[...] = total.astype(bf16)


def add_four(here, *pieces):
    return run(add_four_kernel, "add_four", here, pieces, [(pieces[0].shape, bf16)], megabytes=1)[0]


def feed_weights_kernel(here, shared, down, up, output_ref, *rest):
    small_refs, (inputs, blocks, arrived, sent) = rest[:8], rest[8:]
    loads = [pltpu.make_async_copy(shared.at[y], inputs.at[y], arrived.at[y]) for y in range(4)]
    for load in loads:
        load.start()
    copies = []
    for y in range(4):
        loads[y].wait()
        for x in range(4):
            blocks[y, :, 256 * x : 256 * x + 256] = inputs[y, x, 256:512, :].astype(f32)
        copies.append(pltpu.make_async_copy(blocks.at[y], up.at[pl.ds(256 * y, 256)], sent.at[y]))
        copies[-1].start()
    for x in range(4):
        for y in range(4):
            blocks[4 + x, :, 256 * y : 256 * y + 256] = inputs[y, x, :256, :].astype(f32)
        copies.append(pltpu.make_async_copy(blocks.at[4 + x], down.at[pl.ds(256 * x, 256)], sent.at[4 + x]))
        copies[-1].start()
    for x in range(4):
        tail = jnp.concatenate([inputs[y, x, 512:, :].astype(f32) for y in range(4)], axis=1)
        output_ref[64 * x : 64 * x + 64, :] = tail[:64]
        for k in range(2):
            small_refs[2 * x + k][...] = tail[64 + k : 65 + k]
    for copy in copies:
        copy.wait()


def feed_weights_out(here, shared):
    return pl.pallas_call(
        feed_weights_kernel,
        in_specs=[pl.BlockSpec(memory_space=pltpu.SMEM), pl.BlockSpec(memory_space=pl.ANY)],
        out_specs=[pl.BlockSpec(memory_space=pl.ANY)] * 2 + [pl.BlockSpec(memory_space=pltpu.VMEM)] * 9,
        out_shape=[jax.ShapeDtypeStruct((D, D), f32)] * 2
        + [jax.ShapeDtypeStruct((256, D), f32)]
        + [jax.ShapeDtypeStruct((1, D), f32)] * 8,
        scratch_shapes=[
            pltpu.VMEM((4, 4, 592, 256), bf16),
            pltpu.VMEM((8, 256, D), f32),
            pltpu.SemaphoreType.DMA((4,)),
            pltpu.SemaphoreType.DMA((8,)),
        ],
        compiler_params=pltpu.CompilerParams(vmem_limit_bytes=56 * 2**20),
        cost_estimate=pl.CostEstimate(flops=1, bytes_accessed=1, transcendentals=0),
        name="feed_weights",
    )(here, shared)


def attend_weights_kernel(here, *refs):
    parts, (input_ref, bias_ref), shared = refs[:4], refs[4:6], refs[6]
    for dx, ref in enumerate(parts):
        for dy in range(4):
            shared[before(here[Y], dy), before(here[X], dx)] = ref[dy]
    for y in range(4):
        for z in range(2):
            rows = slice(256 * y + 128 * z, 256 * y + 128 * z + 128)
            blocks = [shared[y, x, z].astype(f32) for x in range(4)]
            queries = [jnp.concatenate([b[128:192, :64], b[128:192, 64:]], axis=0) for b in blocks]
            input_ref[0, rows, :] = jnp.concatenate(queries, axis=1)
            input_ref[1, rows, :] = jnp.concatenate([b[:128, :64] for b in blocks], axis=1)
            input_ref[2, rows, :] = jnp.concatenate([b[:128, 64:] for b in blocks], axis=1)
            if y == 0 and z == 0:
                bias_ref[0:1, :] = jnp.concatenate([b[193:194, :64] for b in blocks], axis=1)
                bias_ref[1:2, :] = jnp.concatenate([b[192:193, :64] for b in blocks], axis=1)
                bias_ref[2:3, :] = jnp.concatenate([b[192:193, 64:] for b in blocks], axis=1)


def attend_weights_out(here, *operands):
    return run(
        attend_weights_kernel,
        "attend_weights",
        here,
        operands,
        [((3, D, 256), f32), ((3, 256), f32)],
        [pltpu.VMEM((4, 4, 2, 208, 128), bf16)],
        megabytes=9,
    )


def leave_kernel(here, total, other, stream, grad_middle, vec, kind, out_ref, last_ref, halves):
    halves[here[CORE]] = total[...]
    halves[1 - here[CORE]] = other[...]
    grad_normed = jnp.concatenate([halves[0], halves[1]], axis=0)
    unit, inv = norm_parts(stream[...])
    grad = grad_middle[...] + norm_back(grad_normed, unit, inv, vec[ATTEND_GAIN : ATTEND_GAIN + 1, :])
    out_ref[...] = grad
    kinds = jnp.broadcast_to(kind[...].astype(f32), (128, 256)).T[:, 0:1]
    last_ref[0:1, :] = jnp.sum(grad_normed * unit, axis=0, keepdims=True)
    last_ref[1:2, :] = jnp.sum(grad_normed, axis=0, keepdims=True)
    for c in range(3):
        last_ref[2 + c : 3 + c, :] = jnp.sum(jnp.where(kinds == c, grad, 0.0), axis=0, keepdims=True)
    last_ref[5:, :] = jnp.zeros((3, D), f32)


def leave(here, *operands):
    return run(
        leave_kernel,
        "leave",
        here,
        operands,
        [((256, D), f32), ((8, D), f32)],
        [pltpu.VMEM((2, 128, D), f32)],
        megabytes=7,
        weight=10,
    )


def ring_sum(values, swap, opposite):
    values = values + lax.ppermute(values, "seq", swap)
    return values + lax.ppermute(values, "seq", opposite)


def last_sum_kernel(here, own, other, table_ref, gain_ref, bias_ref):
    total = own[...] + other[...]
    gain_ref[...] = total[0:1]
    bias_ref[...] = total[1:2]
    table_ref[...] = total[2:5]


def last_sum(here, own, other):
    return run(
        last_sum_kernel,
        "last_sum",
        here,
        (own, other),
        [((3, D), f32), ((1, D), f32), ((1, D), f32)],
        megabytes=1,
    )


ATTEND_GAIN, OUTPUT_BIAS, FEED_GAIN, FEED_BIAS, DOWN_BIAS, UP_BIAS, HIDDEN_GAIN, HIDDEN_BIAS, INNER = range(9)


def tables_of(positions, total_rows):
    pair_index = (jnp.arange(128) % 32).astype(f32)
    frequency = 1.0 / 10000.0 ** (pair_index / 32)
    angles = positions.astype(f32)[:, None] * frequency[None, :]
    ratios = (2.0 * pair_index + 0.4 * HEAD_DIM) / (1.4 * HEAD_DIM)
    exponent = (positions - total_rows // 2).astype(f32)[:, None] / scale_base
    return jnp.cos(angles), jnp.sin(angles), ratios[None, :] ** exponent


def back_tables(positions, total_rows, score_scale):
    lane = jnp.arange(128)
    cosine, sine, growth = tables_of(positions, total_rows)
    cosine = cosine * score_scale
    sine = sine * jnp.where(lane % 64 < 32, score_scale, -score_scale)[None]
    turned = (lane < 64)[None]
    factor = jnp.where(turned, 1.0 / growth, growth)
    return cosine * factor, sine * factor


def per_device(
    tokens,
    segment_kind,
    document,
    type_table,
    attend_gain,
    attend_bias,
    input_weight,
    input_bias,
    inner_gain,
    inner_bias,
    output_weight,
    output_bias,
    feed_gain,
    feed_bias,
    up_weight,
    up_bias,
    hidden_gain,
    hidden_bias,
    down_weight,
    down_bias,
    cotangent,
):
    local_rows = tokens.shape[0]
    total_rows = document.shape[0]
    local_width = input_weight.shape[2]
    score_scale = HEAD_DIM ** (-0.5)
    place = lax.axis_index("seq")
    part = lax.axis_index("ffn")
    y, z, x = place // 8, (place // 4) % 2, place % 4
    here = jnp.stack([x, y, z, part % 2, part, part, part, part]).astype(jnp.int32)
    query_pos = place * local_rows + jnp.arange(local_rows, dtype=jnp.int32)
    kind = segment_kind[None]

    stream, normed_low, *pieces = enter(
        here,
        tokens,
        kind,
        type_table,
        jnp.stack([attend_gain, attend_bias]),
        input_weight,
        input_bias,
        *tables_of(query_pos, total_rows),
    )
    received = shift_x(pieces)

    row_kv, row_q = rows(here, pieces[0], *received)
    kv_received = [lax.ppermute(row_kv, "seq", pairs) for pairs in Y_SHIFTS]
    queries_a = lax.ppermute(row_q, "seq", TO_SAME)
    queries_b = lax.ppermute(row_q, "seq", TO_OTHER)

    normed_row = gather_x(after(normed_low, row_kv))

    document = after(document, queries_a)
    begins = jnp.zeros((total_rows,), jnp.int32)
    for number in range(1, 4):
        begins = begins + jnp.where(
            document >= number, jnp.sum((document == number - 1).astype(jnp.int32)), 0
        )
    row_a = jnp.where(y % 2 == z, y, 7 - y)
    row_b = 7 - row_a
    begin_a = lax.dynamic_slice_in_dim(begins, row_a * ROW, ROW)
    begin_b = lax.dynamic_slice_in_dim(begins, row_b * ROW, ROW)
    begin = jnp.concatenate([begin_a, begin_b])[None]
    info = jnp.stack([z, row_a, row_b, begin_a[0], begin_b[0], begin_a[-1], begin_b[-1], y]).astype(
        jnp.int32
    )
    vec = jnp.concatenate(
        [
            v.astype(f32)
            for v in (
                attend_gain,
                output_bias,
                feed_gain,
                feed_bias,
                down_bias,
                up_bias,
                hidden_gain,
                hidden_bias,
                inner_gain,
                inner_bias,
            )
        ]
        + [jnp.zeros((16 * D - 8 * D - 512,), f32)]
    ).reshape(16, D)
    queries_a, queries_b, plane, vec, begin, info = lax.optimization_barrier(
        (queries_a, queries_b, [row_kv] + kv_received, vec, begin, info)
    )
    out_a, out_b, plane, queries = attend_forward(info, queries_a, queries_b, plane, begin)
    part_a = lax.ppermute(out_a, "seq", FROM_SAME)
    part_b = lax.ppermute(out_b, "seq", FROM_OTHER)
    mixed_row, logs_row, *pieces = combine(here, part_a, part_b)
    mixed, mine, theirs = inner(
        here, pieces[0], *shift_x(pieces), inner_gain[None], inner_bias[None], output_weight
    )
    chip = chip_stats(here, mine, core_swap(theirs))
    row_pos = (2 * y + z) * ROW + jnp.arange(ROW, dtype=jnp.int32)
    tables = back_tables(after(row_pos, chip), total_rows, score_scale)
    grad_hidden = jnp.einsum("td,fd->tf", after(cotangent, chip), down_weight, preferred_element_type=f32)
    total = join_stats(here, chip, far_swap(chip))
    total, tables, grad_hidden = lax.optimization_barrier((total, tables, grad_hidden))
    feed_low, inner_low, middle, before_act, inner_unit, inner_inv, sums, through = feed(
        here, total, core_swap(total), stream, vec, mixed, up_weight, grad_hidden
    )
    sums = sums + core_swap(sums)
    sums = sums + far_swap(sums)
    hidden_low, grad_pre, small_a, mine, theirs = hidden(
        here, sums, before_act, grad_hidden, vec, up_weight
    )
    chip = add_chip(here, mine, core_swap(theirs))
    total = add_far(here, chip, far_swap(chip))
    other = core_swap(total)
    grad_middle, small_b, *head_pieces, branch = middle_back(
        here,
        total,
        other,
        middle,
        stream,
        cotangent,
        vec,
        output_weight,
        inner_unit,
        inner_inv,
        through,
    )
    grad_pre, head_pieces = lax.optimization_barrier((grad_pre, head_pieces))
    head_received = shift_x(head_pieces)
    feed_parts = feed_grads(here, hidden_low, cotangent, grad_pre, feed_low, inner_low, branch, small_a, small_b)
    head_received, feed_parts, normed_row = lax.optimization_barrier((head_received, feed_parts, normed_row))
    feed_sums = lax.psum_scatter(feed_parts, "seq", scatter_dimension=0, axis_index_groups=X_GROUPS)
    message = grad_message(here, head_pieces[0], *head_received, mixed_row, logs_row)
    message_a = lax.ppermute(message, "seq", TO_SAME)
    message_b = lax.ppermute(message, "seq", TO_OTHER)
    weight_heads = head_weights(here, after(input_weight, message))
    message_a, message_b, weight_heads = lax.optimization_barrier((message_a, message_b, weight_heads))
    grad_qa, grad_qb, *kv_pieces = attend_backward(
        info, plane, queries, message_a, message_b, begin
    )
    kv_parts = shift_y(kv_pieces)
    q_parts = [lax.ppermute(grad_qa, "seq", FROM_SAME), lax.ppermute(grad_qb, "seq", FROM_OTHER)]
    feed_mine, feed_theirs = feed_out(here, after(hidden_low, kv_pieces[0]), down_weight)
    feed_chip = add_chip(here, feed_mine, core_swap(feed_theirs))
    feed_far = far_swap(feed_chip)
    kv_parts, q_parts, feed_chip = lax.optimization_barrier((kv_parts, q_parts, feed_chip))
    projected_row, projected_sums, *pieces = row_grads(here, kv_pieces[0], *kv_parts, *q_parts, *tables)
    back_received = shift_x(pieces)
    block_pieces = blocks(here, after(feed_sums, projected_row))
    block_received = shift_y(block_pieces)
    quarter_pieces = attend_quarter(here, normed_row, after(projected_row, block_pieces), projected_sums)
    block_received, back_received, quarter_pieces = lax.optimization_barrier(
        (block_received, back_received, quarter_pieces)
    )
    feed_pair = sum_z(pair(here, block_pieces[0], *block_received))
    quarter_received = shift_y(quarter_pieces)
    mine, theirs = normed_back(here, pieces[0], *back_received, weight_heads)
    mine, theirs, feed_pair = lax.optimization_barrier((mine, theirs, feed_pair))
    feed_shared = lax.all_gather(feed_pair, "seq", axis_index_groups=YX_GROUPS).reshape(4, 4, 592, 256)
    chip = add_chip(here, mine, core_swap(theirs))
    far, quarter_received = lax.optimization_barrier((far_swap(chip), quarter_received))
    total = add_far(here, chip, far)
    other = core_swap(total)
    attend_pair = sum_z(add_four(here, quarter_pieces[0], *quarter_received))
    grad_tokens, last = leave(here, total, other, stream, grad_middle, vec, kind)
    last, attend_pair = lax.optimization_barrier((last, attend_pair))
    attend_near = jnp.stack(ring(attend_pair, Y_SHIFTS))
    last = ring_sum(last, X_SWAP, X_SHIFTS[1])
    attend_near, last = lax.optimization_barrier((attend_near, last))
    attend_parts = ring(attend_near, X_SHIFTS)
    last = ring_sum(last, Y_SWAP, Y_SHIFTS[1])
    feed_chip, feed_far, last = lax.optimization_barrier((feed_chip, feed_far, last))
    last_other = lax.ppermute(last, "seq", Z_SWAP)
    total = add_far(here, feed_chip, feed_far)
    result = result_out(here, total, core_swap(total), middle, vec)
    grad_type_table, grad_attend_gain, grad_attend_bias = last_sum(here, last, last_other)
    grad_down_weight, grad_up_weight, grad_output_weight, *small = feed_weights_out(here, feed_shared)
    attend_parts, result, grad_type_table, grad_down_weight = lax.optimization_barrier(
        (attend_parts, result, grad_type_table, grad_down_weight)
    )
    grad_input_weight, grad_input_bias = attend_weights_out(here, *attend_parts)
    small = [v.reshape(D) for v in small]
    return (
        result,
        grad_tokens,
        grad_type_table,
        grad_attend_gain.reshape(D),
        grad_attend_bias.reshape(D),
        grad_input_weight,
        grad_input_bias,
        small[7][:local_width],
        small[7][local_width : 2 * local_width],
        grad_output_weight,
        small[5],
        small[3],
        small[4],
        grad_up_weight,
        small[2],
        small[0],
        small[1],
        grad_down_weight,
        small[6],
    )


def solution(mesh):
    in_specs = (
        P("seq", None),
        P("seq"),
        P(),
        P(),
        P(),
        P(),
        P(None, None, "ffn"),
        P(None, "ffn"),
        P("ffn"),
        P("ffn"),
        P("ffn", None),
        P(),
        P(),
        P(),
        P(None, "ffn"),
        P("ffn"),
        P("ffn"),
        P("ffn"),
        P("ffn", None),
        P(),
        P("seq", None),
    )
    out_specs = (
        P("seq", None),
        P("seq", None),
        P(),
        P(),
        P(),
        P(None, None, "ffn"),
        P(None, "ffn"),
        P("ffn"),
        P("ffn"),
        P("ffn", None),
        P(),
        P(),
        P(),
        P(None, "ffn"),
        P("ffn"),
        P("ffn"),
        P("ffn"),
        P("ffn", None),
        P(),
    )
    return jax.shard_map(
        per_device, mesh=mesh, in_specs=in_specs, out_specs=out_specs, check_vma=False
    )
```

```python
from functools import partial
import math

import jax
import jax.numpy as jnp
from jax import lax
from jax.experimental import pallas as pl
from jax.experimental.pallas import tpu as pltpu
from jax.sharding import PartitionSpec as P

D = 1024
FF = 4096
HEAD_DIM = 64
ROW = 1024
PACK = ROW // 2
PLANE = 4

epsilon = 1e-05
scale_base = 512.0
masked_score = -1e30
log2_e = 1.4426950408889634
score_factor = HEAD_DIM ** (-0.5) * log2_e
highest = lax.Precision.HIGHEST
f32 = jnp.float32
bf16 = jnp.bfloat16


def seq_index(y, z, x):
    return (y % 4) * 8 + (z % 2) * 4 + x % 4


def seq_pairs(move):
    pairs = []
    for y in range(4):
        for z in range(2):
            for x in range(4):
                pairs.append((seq_index(y, z, x), seq_index(*move(y, z, x))))
    return pairs


def shift_pairs(dy, dz, dx):
    return seq_pairs(lambda y, z, x: (y + dy, z + dz, x + dx))


def group_of(row):
    return min(row, 7 - row)


TO_SAME = seq_pairs(lambda y, z, x: (group_of(2 * y + z), z, x))
TO_OTHER = seq_pairs(lambda y, z, x: (group_of(2 * y + z), 1 - z, x))
FROM_SAME = [(b, a) for a, b in TO_SAME]
FROM_OTHER = [(b, a) for a, b in TO_OTHER]
X_SHIFTS = [shift_pairs(0, 0, d) for d in (1, 2, 3)]
Y_SHIFTS = [shift_pairs(d, 0, 0) for d in (1, 2, 3)]
Z_SWAP = shift_pairs(0, 1, 0)
X_SWAP = seq_pairs(lambda y, z, x: (y, z, x ^ 1))
Y_SWAP = seq_pairs(lambda y, z, x: (y ^ 1, z, x))
CORE_SWAP = [(f, f ^ 1) for f in range(4)]
FAR_SWAP = [(f, f ^ 2) for f in range(4)]
Y_GROUPS = [[seq_index(y, z, x) for y in range(4)] for z in range(2) for x in range(4)]
X_GROUPS = [[seq_index(y, z, x) for x in range(4)] for y in range(4) for z in range(2)]
Z_GROUPS = [[seq_index(y, z, x) for z in range(2)] for y in range(4) for x in range(4)]
YX_GROUPS = [[seq_index(y, z, x) for y in range(4) for x in range(4)] for z in range(2)]


def shift_x(pieces):
    return [lax.ppermute(piece, "seq", pairs) for piece, pairs in zip(pieces[1:], X_SHIFTS)]


def shift_y(pieces):
    return [lax.ppermute(piece, "seq", pairs) for piece, pairs in zip(pieces[1:], Y_SHIFTS)]


def core_swap(values):
    return lax.ppermute(values, "ffn", CORE_SWAP)


def far_swap(values):
    return lax.ppermute(values, "ffn", FAR_SWAP)


def gather_x(values):
    return lax.all_gather(values, "seq", axis_index_groups=X_GROUPS, tiled=True)


def ring(values, shifts):
    return [values] + [lax.ppermute(values, "seq", pairs) for pairs in shifts]


def sum_z(values):
    other = lax.ppermute(values, "seq", Z_SWAP)
    return (values.astype(f32) + other.astype(f32)).astype(bf16)


def after(value, *others):
    return lax.optimization_barrier((value,) + others)[0]


X, Y, Z, CORE, PART = range(5)


def run(kernel, name, here, operands, outs, scratch=(), megabytes=18, weight=0):
    return pl.pallas_call(
        kernel,
        in_specs=[pl.BlockSpec(memory_space=pltpu.SMEM)]
        + [pl.BlockSpec(memory_space=pltpu.VMEM)] * len(operands),
        out_specs=[pl.BlockSpec(memory_space=pltpu.VMEM)] * len(outs),
        out_shape=[jax.ShapeDtypeStruct(shape, kind) for shape, kind in outs],
        scratch_shapes=list(scratch),
        compiler_params=pltpu.CompilerParams(vmem_limit_bytes=megabytes * 2**20),
        cost_estimate=pl.CostEstimate(
            flops=2**20 + weight * 10**9,
            bytes_accessed=sum(v.size * v.dtype.itemsize for v in operands)
            + sum(math.prod(shape) * jnp.dtype(kind).itemsize for shape, kind in outs),
            transcendentals=0,
        ),
        name=name,
    )(here, *operands)


def dot_nn(a, b):
    return lax.dot_general(a, b, (((1,), (0,)), ((), ())), preferred_element_type=f32)


def dot_nt(a, b):
    return lax.dot_general(a, b, (((1,), (1,)), ((), ())), preferred_element_type=f32)


def dot_tn(a, b):
    return lax.dot_general(a, b, (((0,), (0,)), ((), ())), preferred_element_type=f32)


def before(place, d):
    return lax.rem(place + (4 - d), 4)


def store_at(refs, place, index, value):
    for d, ref in enumerate(refs):

        @pl.when(lax.rem(place + d, 4) == index)
        def _(ref=ref):
            ref[...] = value


def store_half(mine, theirs, core, half, value):
    @pl.when(core == half)
    def _():
        mine[...] = value

    @pl.when(core != half)
    def _():
        theirs[...] = value


def row_of(column):
    return jnp.broadcast_to(column, (column.shape[0], 128)).T[0:1]


def split_three(values):
    high = values.astype(bf16).astype(f32)
    middle = (values - high).astype(bf16).astype(f32)
    return high, middle, values - high - middle


def norm_parts(values):
    center = values - jnp.mean(values, axis=-1, keepdims=True)
    inv_std = lax.rsqrt(jnp.mean(center * center, axis=-1, keepdims=True) + epsilon)
    return center * inv_std, inv_std


def norm_back(grad_out, unit, inv_std, gain):
    scaled = grad_out * gain
    return inv_std * (
        scaled
        - jnp.mean(scaled, axis=-1, keepdims=True)
        - unit * jnp.mean(scaled * unit, axis=-1, keepdims=True)
    )


def pair_pack(values, side):
    left = lax.broadcasted_iota(jnp.int32, (128, 128), 1) < 64
    if side == 0:
        return jnp.where(left, values[:128], pltpu.roll(values[128:], 64, 1))
    return jnp.where(left, pltpu.roll(values[:128], 64, 1), values[128:])


def pair_unpack(even, odd):
    left = lax.broadcasted_iota(jnp.int32, (128, 128), 1) < 64
    low = jnp.where(left, even, pltpu.roll(odd, 64, 1))
    high = jnp.where(left, pltpu.roll(even, 64, 1), odd)
    return jnp.concatenate([low, high], axis=0)


def half_swapped(values):
    lane = lax.broadcasted_iota(jnp.int32, values.shape, 1)
    return jnp.where(lane % 64 < 32, pltpu.roll(values, 96, 1), pltpu.roll(values, 32, 1))


def enter_kernel(
    here, tokens, kind, table, norm, weight, shift, cosine, sine, growth, stream_ref, normed_ref, *out
):
    stream = tokens[...].astype(f32)
    kinds = jnp.broadcast_to(kind[...].astype(f32), (128, 256)).T[:, 0:1]
    for c in range(3):
        stream = stream + jnp.where(kinds == c, table[c : c + 1, :].astype(f32), 0.0)
    stream_ref[...] = stream
    unit, _ = norm_parts(stream)
    normed = (unit * norm[0:1, :].astype(f32) + norm[1:2, :].astype(f32)).astype(bf16)
    normed_ref[...] = normed
    projected = [dot_nn(normed, weight[s]) + shift[s : s + 1, :].astype(f32) for s in range(3)]
    lane = lax.broadcasted_iota(jnp.int32, (256, 128), 1)
    left = lane < 64
    signed = jnp.where(lane % 64 < 32, -sine[...], sine[...])
    for group in range(2):
        lanes = slice(128 * group, 128 * group + 128)
        query, key, value = [p[:, lanes] for p in projected]
        query = (query * cosine[...] + half_swapped(query) * signed) * growth[...]
        key = (key * cosine[...] + half_swapped(key) * signed) / growth[...]
        for side in range(2):
            if side == 0:
                both = jnp.where(left, key, pltpu.roll(value, 64, 1))
            else:
                both = jnp.where(left, pltpu.roll(key, 64, 1), value)
            message = jnp.concatenate([both, pair_pack(query, side)], axis=0).astype(bf16)
            store_at(out, here[X], 2 * group + side, message)


def enter(here, *operands):
    return run(
        enter_kernel,
        "enter",
        here,
        operands,
        [((256, D), f32), ((256, D), bf16)] + [((384, 128), bf16)] * 4,
        megabytes=3,
    )


def rows_kernel(here, p0, p1, p2, p3, kv_ref, q_ref):
    for d, ref in enumerate((p0, p1, p2, p3)):
        source = before(here[X], d)
        kv_ref[pl.ds(pl.multiple_of(source * 256, 256), 256), :] = ref[:256, :]
        q_ref[pl.ds(pl.multiple_of(source * 128, 128), 128), :] = ref[256:, :]


def rows(here, *pieces):
    return run(rows_kernel, "rows", here, pieces, [((ROW, 128), bf16), ((PACK, 128), bf16)], megabytes=1)


def lane_rows(row):
    return jnp.concatenate([row[:, 128 * j : 128 * j + 128] for j in range(8)], axis=0)


def unpack_transposed(source, target, offset):
    for b in range(4):
        piece = source[128 * b : 128 * b + 128, :].T
        target[offset : offset + 64, 256 * b : 256 * b + 128] = piece[:64]
        target[offset : offset + 64, 256 * b + 128 : 256 * b + 256] = piece[64:]


def pack_transposed(columns, target):
    for b in range(4):
        piece = jnp.concatenate(
            [columns[:, 256 * b : 256 * b + 128], columns[:, 256 * b + 128 : 256 * b + 256]], axis=0
        )
        target[128 * b : 128 * b + 128, :] = piece.T.astype(target.dtype)


def chunk_bounds(info, tile):
    z = info[0]
    row = info[1 + tile]
    lowest = info[3 + tile]
    first = jnp.int32(0)
    last = jnp.int32(0)
    for c in range(PLANE):
        start = (2 * c + z) * ROW
        first = first + (start + ROW - 1 < lowest).astype(jnp.int32)
        last = last + (2 * c + z <= row).astype(jnp.int32)
    return first, last


def visible(info, tile, c, begin_ref, keys, queries):
    shape = (keys.stop - keys.start, queries.stop - queries.start)
    key = (2 * c + info[0]) * ROW + keys.start + lax.broadcasted_iota(jnp.int32, shape, 0)
    query = info[1 + tile] * ROW + queries.start + lax.broadcasted_iota(jnp.int32, shape, 1)
    return (key <= query) & (key >= begin_ref[:, queries])


def each_block(info, tile, step):
    whole, low, high = slice(0, ROW), slice(0, ROW // 2), slice(ROW // 2, ROW)

    def body(c, carry):
        own = 2 * c + info[0] == info[1 + tile]
        masked = jnp.logical_not(own) & needs_mask(info, tile, c)

        @pl.when(own)
        def _():
            step(c, True, low, whole)
            step(c, True, high, high)

        @pl.when(masked)
        def _():
            step(c, True, whole, whole)

        @pl.when(jnp.logical_not(own | masked))
        def _():
            step(c, False, whole, whole)

        return carry

    first, last = chunk_bounds(info, tile)
    lax.fori_loop(first, last, body, 0)


def needs_mask(info, tile, c):
    key_row = 2 * c + info[0]
    return (key_row == info[1 + tile]) | (key_row * ROW < info[5 + tile])


def plane_copies(info, pieces, kv_ref):
    return [
        (piece, kv_ref.at[pl.ds(pl.multiple_of(before(info[7], d) * ROW, ROW), ROW)])
        for d, piece in enumerate(pieces)
    ]


def forward_kernel(
    info,
    qa,
    qb,
    kv0,
    kv1,
    kv2,
    kv3,
    begin_ref,
    outa_ref,
    outb_ref,
    kv_ref,
    q_in,
    qt_ref,
    vt_ref,
    acc_ref,
    top_ref,
    semaphores,
):
    tile = pl.program_id(0)

    @pl.when(tile == 0)
    def _():
        copies = [
            pltpu.make_async_copy(source, target, semaphores.at[k])
            for k, (source, target) in enumerate(
                [(qa, q_in.at[0]), (qb, q_in.at[1])] + plane_copies(info, (kv0, kv1, kv2, kv3), kv_ref)
            )
        ]
        for copy in copies:
            copy.start()
        for copy in copies:
            copy.wait()
        for c in range(PLANE):
            block = kv_ref[c * ROW : c * ROW + ROW, :].T
            index = lax.broadcasted_iota(jnp.int32, block.shape, 0)
            vt_ref[:, c * ROW : c * ROW + ROW] = jnp.where(index < 64, jnp.ones_like(block), block)
        qt_ref[64:, :] = jnp.zeros((64, ROW), bf16)

    unpack_transposed(q_in.at[tile], qt_ref, 0)

    top_ref[...] = jnp.full(top_ref.shape, masked_score, f32)
    acc_ref[...] = jnp.zeros(acc_ref.shape, f32)

    def step(c, masked, keys, queries):
        start = pl.multiple_of(c * ROW + keys.start, ROW // 2)
        count = keys.stop - keys.start
        scores = dot_nn(kv_ref[pl.ds(start, count), :], qt_ref[:, queries]) * score_factor
        if masked:
            seen = visible(info, tile, c, begin_ref, keys, queries)
            scores = jnp.where(seen, scores, 2 * masked_score)
        old = top_ref[:, queries]
        top = jnp.maximum(old, jnp.max(scores, axis=0, keepdims=True))
        weights = jnp.exp2(scores - top)
        top_ref[:, queries] = top
        acc_ref[:, queries] = acc_ref[:, queries] * jnp.exp2(old - top) + dot_nn(
            vt_ref[:, pl.ds(start, count)], weights.astype(bf16)
        )

    each_block(info, tile, step)
    total = acc_ref[0:1, :]
    some = total > 0
    safe = jnp.where(some, total, 1.0)
    log_total = jnp.where(some, top_ref[...] + jnp.log2(safe), masked_score)
    for index, out_ref in enumerate((outa_ref, outb_ref)):

        @pl.when(tile == index)
        def _(out_ref=out_ref):
            pack_transposed(acc_ref[64:, :] / safe, out_ref)
            parts = [lane_rows(part) for part in split_three(log_total)]
            out_ref[PACK:, :] = jnp.concatenate(parts + [jnp.zeros((8, 128), f32)], axis=0).astype(bf16)


def attend_forward(info, queries_a, queries_b, keys_values, begin):
    hbm = pl.BlockSpec(memory_space=pltpu.HBM)
    return pl.pallas_call(
        forward_kernel,
        grid_spec=pltpu.PrefetchScalarGridSpec(
            num_scalar_prefetch=1,
            grid=(2,),
            in_specs=[hbm] * 6 + [pl.BlockSpec((1, ROW), lambda i, s: (0, i))],
            out_specs=[pl.BlockSpec(memory_space=pltpu.VMEM)] * 4,
            scratch_shapes=[
                pltpu.VMEM((128, ROW), bf16),
                pltpu.VMEM((128, PLANE * ROW), bf16),
                pltpu.VMEM((128, ROW), f32),
                pltpu.VMEM((1, ROW), f32),
                pltpu.SemaphoreType.DMA((6,)),
            ],
        ),
        out_shape=[jax.ShapeDtypeStruct((PACK + 32, 128), bf16)] * 2
        + [jax.ShapeDtypeStruct((PLANE * ROW, 128), bf16), jax.ShapeDtypeStruct((2, PACK, 128), bf16)],
        compiler_params=pltpu.CompilerParams(vmem_limit_bytes=9 * 2**20),
        cost_estimate=pl.CostEstimate(flops=10 * 10**9, bytes_accessed=2**21, transcendentals=0),
        name="attend_forward",
    )(info, queries_a, queries_b, *keys_values, begin)


def combine_kernel(here, a_ref, b_ref, full_ref, log_ref, *out):
    logs = []
    for ref in (a_ref, b_ref):
        rows = ref[PACK:, :].astype(f32)
        logs.append(rows[:8] + rows[8:16] + rows[16:24])
    top = jnp.maximum(logs[0], logs[1])
    shares = [jnp.exp2(part - top) for part in logs]
    total = shares[0] + shares[1]
    log_ref[...] = top + jnp.log2(total)
    columns = [(share / total).T for share in shares]
    left = lax.broadcasted_iota(jnp.int32, (128, 128), 1) < 64
    for b in range(4):
        mixed = jnp.zeros((128, 128), f32)
        for ref, column in zip((a_ref, b_ref), columns):
            weight = jnp.where(left, column[:, 2 * b : 2 * b + 1], column[:, 2 * b + 1 : 2 * b + 2])
            mixed = mixed + weight * ref[128 * b : 128 * b + 128, :].astype(f32)
        full_ref[128 * b : 128 * b + 128, :] = mixed
        store_at(out, here[X], b, mixed.astype(bf16))


def combine(here, part_a, part_b):
    return run(
        combine_kernel,
        "combine",
        here,
        (part_a, part_b),
        [((PACK, 128), f32), ((8, 128), f32)] + [((128, 128), bf16)] * 4,
        megabytes=1,
    )


def grad_message_kernel(here, p0, p1, p2, p3, mixed_ref, log_ref, out_ref):
    for d, ref in enumerate((p0, p1, p2, p3)):
        out_ref[pl.ds(pl.multiple_of(before(here[X], d) * 128, 128), 128), :] = ref[...]
    deltas = []
    for b in range(4):
        rows = slice(128 * b, 128 * b + 128)
        each = (out_ref[rows, :].astype(f32) * mixed_ref[rows, :]).T
        deltas.append(jnp.sum(each[:64], axis=0, keepdims=True))
        deltas.append(jnp.sum(each[64:], axis=0, keepdims=True))
    parts = list(split_three(log_ref[...])) + list(split_three(jnp.concatenate(deltas, axis=0)))
    out_ref[PACK:, :] = jnp.concatenate(parts, axis=0).astype(bf16)


def grad_message(here, *operands):
    return run(grad_message_kernel, "grad_message", here, operands, [((PACK + 48, 128), bf16)], megabytes=1)[0]


def backward_kernel(
    info,
    plane,
    queries,
    ma,
    mb,
    begin_ref,
    dqa_ref,
    dqb_ref,
    own_ref,
    one_ref,
    two_ref,
    three_ref,
    qt_ref,
    gt_ref,
    q_ref,
    g_ref,
    kv_ref,
    kt_ref,
    row_ref,
    acc_ref,
    dq_acc,
    q_in,
    m_in,
    semaphores,
):
    tile = pl.program_id(0)

    def load(query_ref, message_ref):
        unpack_transposed(query_ref, qt_ref, 0)
        unpack_transposed(message_ref, gt_ref, 64)
        q_ref[...] = qt_ref[...].T
        g_ref[...] = gt_ref[...].T
        rows = message_ref[PACK:, :].astype(f32)
        for k in range(2):
            part = rows[24 * k : 24 * k + 8] + rows[24 * k + 8 : 24 * k + 16] + rows[24 * k + 16 : 24 * k + 24]
            for j in range(8):
                row_ref[k : k + 1, 128 * j : 128 * j + 128] = part[j : j + 1, :]

    @pl.when(tile == 0)
    def _():
        copies = [
            pltpu.make_async_copy(source, target, semaphores.at[k])
            for k, (source, target) in enumerate(
                [(queries, q_in), (ma, m_in.at[0]), (mb, m_in.at[1]), (plane, kv_ref)]
            )
        ]
        for copy in copies:
            copy.start()
        acc_ref[...] = jnp.zeros(acc_ref.shape, f32)
        qt_ref[64:, :] = jnp.zeros((64, ROW), bf16)
        gt_ref[:64, :] = jnp.zeros((64, ROW), bf16)
        for copy in copies:
            copy.wait()
        for c in range(PLANE):
            kt_ref[:, c * ROW : c * ROW + ROW] = kv_ref[c * ROW : c * ROW + ROW, :].T

    load(q_in.at[tile], m_in.at[tile])
    dq_acc[...] = jnp.zeros(dq_acc.shape, f32)

    def step(c, masked, keys, queries):
        start = pl.multiple_of(c * ROW + keys.start, ROW // 2)
        count = keys.stop - keys.start
        block = kv_ref[pl.ds(start, count), :]
        scores = dot_nn(block, qt_ref[:, queries]) * score_factor
        if masked:
            seen = visible(info, tile, c, begin_ref, keys, queries)
            scores = jnp.where(seen, scores, 2 * masked_score)
        weights = jnp.exp2(scores - row_ref[0:1, queries])
        grad_weights = dot_nn(block, gt_ref[:, queries])
        grad_scores = (weights * (grad_weights - row_ref[1:2, queries])).astype(bf16)
        acc_ref[pl.ds(start, count), :] += dot_nn(grad_scores, q_ref[queries, :]) + dot_nn(
            weights.astype(bf16), g_ref[queries, :]
        )
        dq_acc[:, queries] += dot_nn(kt_ref[:, pl.ds(start, count)], grad_scores)

    each_block(info, tile, step)

    @pl.when(tile == 0)
    def _():
        pack_transposed(dq_acc[:64, :], dqa_ref)

    @pl.when(tile == 1)
    def _():
        pack_transposed(dq_acc[:64, :], dqb_ref)
        for d, ref in enumerate((own_ref, one_ref, two_ref, three_ref)):
            start = pl.multiple_of(lax.rem(info[7] + d, 4) * ROW, ROW)
            ref[...] = acc_ref[pl.ds(start, ROW), :].astype(bf16)


def attend_backward(info, plane, queries, message_a, message_b, begin):
    packed = pl.BlockSpec((PACK, 128), lambda i, s: (0, 0))
    hbm = pl.BlockSpec(memory_space=pltpu.HBM)
    block = pl.BlockSpec((ROW, 128), lambda i, s: (0, 0))
    return pl.pallas_call(
        backward_kernel,
        grid_spec=pltpu.PrefetchScalarGridSpec(
            num_scalar_prefetch=1,
            grid=(2,),
            in_specs=[hbm] * 4 + [pl.BlockSpec((1, ROW), lambda i, s: (0, i))],
            out_specs=[packed] * 2 + [block] * 4,
            scratch_shapes=[
                pltpu.VMEM((128, ROW), bf16),
                pltpu.VMEM((128, ROW), bf16),
                pltpu.VMEM((ROW, 128), bf16),
                pltpu.VMEM((ROW, 128), bf16),
                pltpu.VMEM((PLANE * ROW, 128), bf16),
                pltpu.VMEM((128, PLANE * ROW), bf16),
                pltpu.VMEM((8, ROW), f32),
                pltpu.VMEM((PLANE * ROW, 128), f32),
                pltpu.VMEM((128, ROW), f32),
                pltpu.VMEM((2, PACK, 128), bf16),
                pltpu.VMEM((2, PACK + 48, 128), bf16),
                pltpu.SemaphoreType.DMA((4,)),
            ],
        ),
        out_shape=[jax.ShapeDtypeStruct((PACK, 128), bf16)] * 2
        + [jax.ShapeDtypeStruct((ROW, 128), bf16)] * 4,
        compiler_params=pltpu.CompilerParams(vmem_limit_bytes=16 * 2**20),
        cost_estimate=pl.CostEstimate(flops=18 * 10**9, bytes_accessed=2**22, transcendentals=0),
        name="attend_backward",
    )(info, plane, queries, message_a, message_b, begin)


def inner_kernel(here, p0, p1, p2, p3, gain, shift, weight, mixed_ref, mine, theirs, heads):
    for d, ref in enumerate((p0, p1, p2, p3)):
        heads[before(here[X], d)] = ref[...].astype(f32)
    mixed = jnp.concatenate([pair_unpack(heads[0], heads[1]), pair_unpack(heads[2], heads[3])], axis=1)
    mixed_ref[...] = mixed
    mean = jnp.mean(mixed, axis=-1, keepdims=True)
    centred = mixed - mean
    spread = jnp.sum(centred * centred, axis=-1, keepdims=True)
    gains = gain[...].astype(f32)
    projected = dot_nn((centred * gains).astype(bf16), weight[...])
    full = weight[...].astype(f32)
    gain_column = jnp.broadcast_to(gains, (128, 256)).T[:, 0:1]
    shift_column = jnp.broadcast_to(shift[...].astype(f32), (128, 256)).T[:, 0:1]
    through = jnp.sum(full * gain_column, axis=0, keepdims=True)
    vectors = [jnp.where(here[PART] == k, through, 0.0) for k in range(4)]
    vectors.append(jnp.sum(full * shift_column, axis=0, keepdims=True))
    for half in range(2):
        tokens = slice(128 * half, 128 * half + 128)
        stats = [row_of(mean[tokens]), row_of(spread[tokens])]
        slots = [jnp.where(here[PART] == j // 2, stats[j % 2], 0.0) for j in range(8)]
        rows = vectors + [jnp.concatenate(slots, axis=1), jnp.zeros((2, D), f32)]
        store_half(mine, theirs, here[CORE], half, jnp.concatenate([projected[tokens]] + rows, axis=0))


def inner(here, *operands):
    return run(
        inner_kernel,
        "inner",
        here,
        operands,
        [((256, 256), f32), ((136, D), f32), ((136, D), f32)],
        [pltpu.VMEM((4, 128, 128), f32)],
        megabytes=4,
    )


def chip_stats_kernel(here, mine, other, out):
    total = mine[...] + other[...]
    parts = list(split_three(total[128:])) + [jnp.zeros((8, D), f32)]
    out[...] = jnp.concatenate([total[:128]] + parts, axis=0).astype(bf16)


def join_stats_kernel(here, chip, far, out):
    total = chip[...].astype(f32) + far[...].astype(f32)
    out[...] = jnp.concatenate([total[:128], total[128:136] + total[136:144] + total[144:152]], axis=0)


def add_chip_kernel(here, mine, other, out):
    out[...] = (mine[...] + other[...]).astype(bf16)


def add_far_kernel(here, chip, far, out):
    out[...] = chip[...].astype(f32) + far[...].astype(f32)


def chip_stats(here, mine, other):
    return run(chip_stats_kernel, "chip_stats", here, (mine, other), [((160, D), bf16)], megabytes=1)[0]


def join_stats(here, chip, far):
    return run(join_stats_kernel, "join_stats", here, (chip, far), [((136, D), f32)], megabytes=1)[0]


def add_chip(here, mine, other):
    return run(add_chip_kernel, "add_chip", here, (mine, other), [((128, D), bf16)], megabytes=1)[0]


def add_far(here, chip, far):
    return run(add_far_kernel, "add_far", here, (chip, far), [((128, D), f32)], megabytes=1)[0]


def sum_ffn(here, mine, theirs):
    chip = add_chip(here, mine, core_swap(theirs))
    total = add_far(here, chip, far_swap(chip))
    return total, core_swap(total)


def gauss_share(values):
    return 0.5 + 0.5 * lax.erf(values * math.sqrt(0.5))


def feed_kernel(
    here,
    total,
    other,
    stream,
    vec,
    mixed_ref,
    weight,
    grad_hidden,
    low_ref,
    inner_ref,
    middle_ref,
    before_ref,
    unit_ref,
    inv_ref,
    sums_ref,
    vectors_ref,
    halves,
):
    halves[here[CORE]] = total[...]
    halves[1 - here[CORE]] = other[...]
    vectors = halves[0, 128:, :]
    vectors_ref[...] = vectors
    ending = vectors[4:5, :] + vec[OUTPUT_BIAS : OUTPUT_BIAS + 1, :]
    inner_gain = vec[INNER : INNER + 1, :256]
    inner_bias = vec[INNER : INNER + 1, 256:512]
    for half in range(2):
        tokens = slice(128 * half, 128 * half + 128)
        stats = jnp.concatenate([halves[half, 133:134, 128 * j : 128 * j + 128] for j in range(8)], axis=0).T
        means = [stats[:, 2 * k : 2 * k + 1] for k in range(4)]
        mean = (means[0] + means[1] + means[2] + means[3]) * 0.25
        spread = stats[:, 1:2] + stats[:, 3:4] + stats[:, 5:6] + stats[:, 7:8]
        projected = halves[half, :128, :]
        for k in range(4):
            move = means[k] - mean
            spread = spread + 256.0 * move * move
            projected = projected + move * vectors[k : k + 1, :]
        inv = lax.rsqrt(spread / D + epsilon)
        middle_ref[tokens, :] = stream[tokens, :] + projected * inv + ending
        unit = (mixed_ref[tokens, :] - mean) * inv
        unit_ref[tokens, :] = unit
        inv_ref[tokens, :] = jnp.broadcast_to(inv, (128, 128))
        inner_ref[tokens, :] = (unit * inner_gain + inner_bias).astype(bf16)
    unit, _ = norm_parts(middle_ref[...])
    low_ref[...] = (
        unit * vec[FEED_GAIN : FEED_GAIN + 1, :] + vec[FEED_BIAS : FEED_BIAS + 1, :]
    ).astype(bf16)
    before_act = dot_nn(low_ref[...], weight[...]) + vec[UP_BIAS : UP_BIAS + 1, :]
    before_ref[...] = before_act
    active = before_act * gauss_share(before_act)
    scaled = grad_hidden[...] * vec[HIDDEN_GAIN : HIDDEN_GAIN + 1, :]
    columns = [
        jnp.sum(part, axis=-1, keepdims=True) for part in (active, active * active, scaled, scaled * active)
    ]
    lane = lax.broadcasted_iota(jnp.int32, (256, 128), 1)
    spread = jnp.zeros((256, 128), f32)
    for k, column in enumerate(columns):
        spread = jnp.where(lane == k, column, spread)
    sums_ref[...] = spread.T[:8]


def feed(here, *operands):
    return run(
        feed_kernel,
        "feed",
        here,
        operands,
        [
            ((256, D), bf16),
            ((256, 256), bf16),
            ((256, D), f32),
            ((256, D), f32),
            ((256, 256), f32),
            ((256, 128), f32),
            ((8, 256), f32),
            ((8, D), f32),
        ],
        [pltpu.VMEM((2, 136, D), f32)],
        megabytes=6,
    )


def hidden_kernel(
    here, sums, before_ref, grad_hidden, vec, weight, low_ref, grad_ref, small_ref, mine, theirs
):
    before_act = before_ref[...]
    share = gauss_share(before_act)
    slope = share + before_act * jnp.exp(-0.5 * before_act * before_act) * (1.0 / math.sqrt(2.0 * math.pi))
    columns = sums[...].T
    mean = columns[:, 0:1] / FF
    inv = lax.rsqrt(columns[:, 1:2] / FF - mean * mean + epsilon)
    first = columns[:, 2:3]
    cross = inv * (columns[:, 3:4] - mean * first)
    gain = vec[HIDDEN_GAIN : HIDDEN_GAIN + 1, :]
    unit = (before_act * share - mean) * inv
    low_ref[...] = (unit * gain + vec[HIDDEN_BIAS : HIDDEN_BIAS + 1, :]).astype(bf16)
    grad_out = grad_hidden[...]
    grad_pre = (inv * (grad_out * gain - first / FF - unit * (cross / FF)) * slope).astype(bf16)
    small_ref[0:1, :] = jnp.sum(grad_out * unit, axis=0, keepdims=True)
    small_ref[1:2, :] = jnp.sum(grad_out, axis=0, keepdims=True)
    small_ref[2:3, :] = jnp.sum(grad_pre.astype(f32), axis=0, keepdims=True)
    small_ref[3:, :] = jnp.zeros((5, D), f32)
    grad_ref[...] = grad_pre
    back = dot_nt(grad_pre, weight[...])
    for half in range(2):
        store_half(mine, theirs, here[CORE], half, back[128 * half : 128 * half + 128])


def hidden(here, *operands):
    return run(
        hidden_kernel,
        "hidden",
        here,
        operands,
        [((256, D), bf16), ((256, D), bf16), ((8, D), f32), ((128, D), f32), ((128, D), f32)],
        megabytes=6,
    )


def feed_out_kernel(here, low_ref, weight, mine, theirs):
    for half in range(2):
        tokens = slice(128 * half, 128 * half + 128)
        store_half(mine, theirs, here[CORE], half, dot_nn(low_ref[tokens, :], weight[...]))


def feed_out(here, low, weight):
    return run(
        feed_out_kernel, "feed_out", here, (low, weight), [((128, D), f32), ((128, D), f32)], megabytes=2
    )


def result_kernel(here, total, other, middle, vec, out, halves):
    halves[here[CORE]] = total[...]
    halves[1 - here[CORE]] = other[...]
    for half in range(2):
        tokens = slice(128 * half, 128 * half + 128)
        out[tokens, :] = (
            middle[tokens, :] + halves[half] + vec[DOWN_BIAS : DOWN_BIAS + 1, :]
        ).astype(bf16)


def result_out(here, *operands):
    return run(
        result_kernel,
        "result",
        here,
        operands,
        [((256, D), bf16)],
        [pltpu.VMEM((2, 128, D), f32)],
        megabytes=4,
    )[0]


def feed_grads_kernel(here, low, cotangent, grad_pre, feed_low, inner_low, branch, small_a, small_b, out):
    grads = dot_tn(inner_low[...], branch[...])
    vectors = [small_a[k : k + 1, :] for k in range(3)] + [small_b[k : k + 1, :] for k in range(5)]
    for k in range(4):
        lanes = slice(256 * k, 256 * k + 256)
        parts = [dot_tn(low[:, lanes], cotangent[...]), dot_tn(grad_pre[:, lanes], feed_low[...])]
        parts += [grads[64 * k : 64 * k + 64], vectors[2 * k], vectors[2 * k + 1], jnp.zeros((14, D), f32)]
        out[k] = jnp.concatenate(parts, axis=0).astype(bf16)


def feed_grads(here, *operands):
    return run(feed_grads_kernel, "feed_grads", here, operands, [((4, 592, D), bf16)], megabytes=8)[0]


def blocks_kernel(here, total, *out):
    for k in range(4):
        store_at(out, here[Y], k, total[:, 256 * k : 256 * k + 256])


def blocks(here, total):
    return run(blocks_kernel, "blocks", here, (total,), [((total.shape[0], 256), bf16)] * 4, megabytes=2)


def pair_kernel(here, p0, p1, p2, p3, out):
    total = p0[...].astype(f32) + p1[...].astype(f32) + p2[...].astype(f32) + p3[...].astype(f32)
    out[...] = jnp.concatenate([total[:256], total[256:512].T, total[512:]], axis=0).astype(bf16)


def pair(here, *pieces):
    return run(pair_kernel, "pair", here, pieces, [((592, 256), bf16)], megabytes=3)[0]


def middle_back_kernel(
    here,
    total,
    other,
    middle,
    stream,
    cotangent,
    vec,
    weight,
    unit_ref,
    inv_ref,
    vectors,
    grad_ref,
    small_ref,
    h0,
    h1,
    h2,
    h3,
    low_ref,
    halves,
):
    halves[here[CORE]] = total[...]
    halves[1 - here[CORE]] = other[...]
    grad_feed = jnp.concatenate([halves[0], halves[1]], axis=0)
    unit, inv = norm_parts(middle[...])
    grad_result = cotangent[...].astype(f32)
    grad_middle = grad_result + norm_back(grad_feed, unit, inv, vec[FEED_GAIN : FEED_GAIN + 1, :])
    grad_ref[...] = grad_middle
    low = grad_middle.astype(bf16)
    branch = low.astype(f32)
    low_ref[...] = low
    grad_inner = dot_nt(low, weight[...])
    through = vectors[0:1, :] + vectors[1:2, :] + vectors[2:3, :] + vectors[3:4, :]
    first = jnp.sum(branch * through, axis=-1, keepdims=True)
    ending = vectors[4:5, :] + vec[OUTPUT_BIAS : OUTPUT_BIAS + 1, :]
    cross = jnp.sum(branch * (middle[...] - stream[...] - ending), axis=-1, keepdims=True)
    inner_unit = unit_ref[...]
    inner_inv = inv_ref[:, 0:1]
    grad_mixed = inner_inv * (
        grad_inner * vec[INNER : INNER + 1, :256] - first / D - inner_unit * (cross / D)
    )
    for group in range(2):
        lanes = grad_mixed[:, 128 * group : 128 * group + 128]
        for side in range(2):
            store_at((h0, h1, h2, h3), here[X], 2 * group + side, pair_pack(lanes, side).astype(bf16))
    small_ref[0:1, :] = jnp.sum(grad_feed * unit, axis=0, keepdims=True)
    small_ref[1:2, :] = jnp.sum(grad_feed, axis=0, keepdims=True)
    small_ref[2:3, :] = jnp.sum(branch, axis=0, keepdims=True)
    small_ref[3:4, :] = jnp.sum(grad_result, axis=0, keepdims=True)
    small_ref[4:5, :256] = jnp.sum(grad_inner * inner_unit, axis=0, keepdims=True)
    small_ref[4:5, 256:512] = jnp.sum(grad_inner, axis=0, keepdims=True)
    small_ref[4:5, 512:] = jnp.zeros((1, 512), f32)
    small_ref[5:, :] = jnp.zeros((3, D), f32)


def middle_back(here, *operands):
    return run(
        middle_back_kernel,
        "middle_back",
        here,
        operands,
        [((256, D), f32), ((8, D), f32)] + [((128, 128), bf16)] * 4 + [((256, D), bf16)],
        [pltpu.VMEM((2, 128, D), f32)],
        megabytes=8,
    )


def row_grads_kernel(
    here, own, one, two, three, qa, qb, cos_in, sin_in, out_ref, sums_ref, p0, p1, p2, p3
):
    left = lax.broadcasted_iota(jnp.int32, (128, 128), 1) < 64

    def turned(values, cos_part, sin_part):
        return (values * cos_part + half_swapped(values) * sin_part).astype(bf16)

    for b in range(8):
        rows = slice(128 * b, 128 * b + 128)
        total = own[rows, :].astype(f32)
        for ref in (one, two, three):
            total = total + ref[rows, :].astype(f32)
        out_ref[rows, :128] = turned(
            total, jnp.where(left, cos_in[rows, :], 1.0), jnp.where(left, sin_in[rows, :], 0.0)
        )
    for b in range(4):
        rows = slice(128 * b, 128 * b + 128)
        total = qa[rows, :].astype(f32) + qb[rows, :].astype(f32)
        for side in range(2):
            tokens = slice(256 * b + 128 * side, 256 * b + 128 * side + 128)
            values = total if side == 0 else pltpu.roll(total, 64, 1)
            values = jnp.where(left, values, 0.0)
            out_ref[tokens, 128:] = turned(
                values, pltpu.roll(cos_in[tokens, :], 64, 1), pltpu.roll(sin_in[tokens, :], 64, 1)
            )
    for b in range(4):
        store_at((p0, p1, p2, p3), here[X], b, out_ref[256 * b : 256 * b + 256, :])
    sums_ref[...] = jnp.broadcast_to(jnp.sum(out_ref[...].astype(f32), axis=0, keepdims=True), (8, 256))


def row_grads(here, *operands):
    return run(
        row_grads_kernel,
        "row_grads",
        here,
        operands,
        [((ROW, 256), bf16), ((8, 256), f32)] + [((256, 256), bf16)] * 4,
        megabytes=3,
    )


def head_weights_kernel(here, weight, out):
    left = lax.broadcasted_iota(jnp.int32, (256, 128), 1) < 64
    for r in range(4):
        rows = slice(256 * r, 256 * r + 256)
        for group in range(2):
            lanes = slice(128 * group, 128 * group + 128)
            query, key, value = [weight[s, rows, lanes].astype(f32) for s in range(3)]
            even = [jnp.where(left, key, pltpu.roll(value, 64, 1)), jnp.where(left, query, 0.0)]
            odd = [
                jnp.where(left, pltpu.roll(key, 64, 1), value),
                jnp.where(left, pltpu.roll(query, 64, 1), 0.0),
            ]
            for side, parts in enumerate((even, odd)):
                out[2 * group + side, rows, :] = jnp.concatenate(parts, axis=1).astype(bf16)


def head_weights(here, weight):
    return run(head_weights_kernel, "head_weights", here, (weight,), [((4, D, 256), bf16)], megabytes=2)[0]


def normed_back_kernel(here, p0, p1, p2, p3, weight, mine, theirs):
    for half in range(2):
        total = jnp.zeros((128, D), f32)
        for d, ref in enumerate((p0, p1, p2, p3)):
            total = total + dot_nt(ref[128 * half : 128 * half + 128, :], weight[before(here[X], d)])
        store_half(mine, theirs, here[CORE], half, total)


def normed_back(here, *operands):
    return run(
        normed_back_kernel, "normed_back", here, operands, [((128, D), f32), ((128, D), f32)], megabytes=2
    )


def attend_quarter_kernel(here, normed, projected, sums, *out):
    grad_input = dot_tn(projected[...], normed[...])
    left = lax.broadcasted_iota(jnp.int32, (64, 128), 1) < 64
    for y in range(4):
        parts = []
        for z in range(2):
            tall = grad_input[:, 256 * y + 128 * z : 256 * y + 128 * z + 128].T
            query = jnp.where(left, tall[:64, 128:], pltpu.roll(tall[64:, 128:], 64, 1))
            last = jnp.zeros((16, 128), f32)
            if y == 0 and z == 0:
                last = jnp.concatenate([sums[0:1, :128], sums[0:1, 128:], last[:14]], axis=0)
            parts.append(jnp.concatenate([tall[:, :128], query, last], axis=0).astype(bf16)[None])
        store_at(out, here[Y], y, jnp.concatenate(parts, axis=0))


def attend_quarter(here, *operands):
    return run(attend_quarter_kernel, "attend_quarter", here, operands, [((2, 208, 128), bf16)] * 4, megabytes=5)


def add_four_kernel(here, p0, p1, p2, p3, out):
    total = p0[...].astype(f32) + p1[...].astype(f32) + p2[...].astype(f32) + p3[...].astype(f32)
    out[...] = total.astype(bf16)


def add_four(here, *pieces):
    return run(add_four_kernel, "add_four", here, pieces, [(pieces[0].shape, bf16)], megabytes=1)[0]


def feed_weights_kernel(here, shared, down, up, output_ref, *rest):
    small_refs, (inputs, blocks, arrived, sent) = rest[:9], rest[9:]
    loads = [pltpu.make_async_copy(shared.at[y], inputs.at[y], arrived.at[y]) for y in range(4)]
    for load in loads:
        load.start()
    copies = []
    for y in range(4):
        loads[y].wait()
        for x in range(4):
            blocks[y, :, 256 * x : 256 * x + 256] = inputs[y, x, 256:512, :].astype(f32)
        copies.append(pltpu.make_async_copy(blocks.at[y], up.at[pl.ds(256 * y, 256)], sent.at[y]))
        copies[-1].start()
    for x in range(4):
        for y in range(4):
            blocks[4 + x, :, 256 * y : 256 * y + 256] = inputs[y, x, :256, :].astype(f32)
        copies.append(pltpu.make_async_copy(blocks.at[4 + x], down.at[pl.ds(256 * x, 256)], sent.at[4 + x]))
        copies[-1].start()
    for x in range(4):
        tail = jnp.concatenate([inputs[y, x, 512:, :].astype(f32) for y in range(4)], axis=1)
        output_ref[64 * x : 64 * x + 64, :] = tail[:64]
        small_refs[2 * x][...] = tail[64:65]
        if x < 3:
            small_refs[2 * x + 1][...] = tail[65:66]
        else:
            small_refs[7][...] = tail[65:66, :256]
            small_refs[8][...] = tail[65:66, 256:512]
    for copy in copies:
        copy.wait()


def feed_weights_out(here, shared):
    return pl.pallas_call(
        feed_weights_kernel,
        in_specs=[pl.BlockSpec(memory_space=pltpu.SMEM), pl.BlockSpec(memory_space=pl.ANY)],
        out_specs=[pl.BlockSpec(memory_space=pl.ANY)] * 2 + [pl.BlockSpec(memory_space=pltpu.VMEM)] * 10,
        out_shape=[jax.ShapeDtypeStruct((D, D), f32)] * 2
        + [jax.ShapeDtypeStruct((256, D), f32)]
        + [jax.ShapeDtypeStruct((1, D), f32)] * 7
        + [jax.ShapeDtypeStruct((1, 256), f32)] * 2,
        scratch_shapes=[
            pltpu.VMEM((4, 4, 592, 256), bf16),
            pltpu.VMEM((8, 256, D), f32),
            pltpu.SemaphoreType.DMA((4,)),
            pltpu.SemaphoreType.DMA((8,)),
        ],
        compiler_params=pltpu.CompilerParams(vmem_limit_bytes=56 * 2**20),
        cost_estimate=pl.CostEstimate(flops=1, bytes_accessed=1, transcendentals=0),
        name="feed_weights",
    )(here, shared)


def attend_weights_kernel(here, *refs):
    parts, (input_ref, bias_ref), shared = refs[:4], refs[4:6], refs[6]
    for dx, ref in enumerate(parts):
        for dy in range(4):
            shared[before(here[Y], dy), before(here[X], dx)] = ref[dy]
    for y in range(4):
        for z in range(2):
            rows = slice(256 * y + 128 * z, 256 * y + 128 * z + 128)
            blocks = [shared[y, x, z].astype(f32) for x in range(4)]
            queries = [jnp.concatenate([b[128:192, :64], b[128:192, 64:]], axis=0) for b in blocks]
            input_ref[0, rows, :] = jnp.concatenate(queries, axis=1)
            input_ref[1, rows, :] = jnp.concatenate([b[:128, :64] for b in blocks], axis=1)
            input_ref[2, rows, :] = jnp.concatenate([b[:128, 64:] for b in blocks], axis=1)
            if y == 0 and z == 0:
                bias_ref[0:1, :] = jnp.concatenate([b[193:194, :64] for b in blocks], axis=1)
                bias_ref[1:2, :] = jnp.concatenate([b[192:193, :64] for b in blocks], axis=1)
                bias_ref[2:3, :] = jnp.concatenate([b[192:193, 64:] for b in blocks], axis=1)


def attend_weights_out(here, *operands):
    return run(
        attend_weights_kernel,
        "attend_weights",
        here,
        operands,
        [((3, D, 256), f32), ((3, 256), f32)],
        [pltpu.VMEM((4, 4, 2, 208, 128), bf16)],
        megabytes=9,
    )


def leave_kernel(here, total, other, stream, grad_middle, vec, kind, out_ref, last_ref, halves):
    halves[here[CORE]] = total[...]
    halves[1 - here[CORE]] = other[...]
    grad_normed = jnp.concatenate([halves[0], halves[1]], axis=0)
    unit, inv = norm_parts(stream[...])
    grad = grad_middle[...] + norm_back(grad_normed, unit, inv, vec[ATTEND_GAIN : ATTEND_GAIN + 1, :])
    out_ref[...] = grad
    kinds = jnp.broadcast_to(kind[...].astype(f32), (128, 256)).T[:, 0:1]
    last_ref[0:1, :] = jnp.sum(grad_normed * unit, axis=0, keepdims=True)
    last_ref[1:2, :] = jnp.sum(grad_normed, axis=0, keepdims=True)
    for c in range(3):
        last_ref[2 + c : 3 + c, :] = jnp.sum(jnp.where(kinds == c, grad, 0.0), axis=0, keepdims=True)
    last_ref[5:, :] = jnp.zeros((3, D), f32)


def leave(here, *operands):
    return run(
        leave_kernel,
        "leave",
        here,
        operands,
        [((256, D), f32), ((8, D), f32)],
        [pltpu.VMEM((2, 128, D), f32)],
        megabytes=7,
        weight=10,
    )


def ring_sum(values, swap, opposite):
    values = values + lax.ppermute(values, "seq", swap)
    return values + lax.ppermute(values, "seq", opposite)


def last_sum_kernel(here, own, other, table_ref, gain_ref, bias_ref):
    total = own[...] + other[...]
    gain_ref[...] = total[0:1]
    bias_ref[...] = total[1:2]
    table_ref[...] = total[2:5]


def last_sum(here, own, other):
    return run(
        last_sum_kernel,
        "last_sum",
        here,
        (own, other),
        [((3, D), f32), ((1, D), f32), ((1, D), f32)],
        megabytes=1,
    )


ATTEND_GAIN, OUTPUT_BIAS, FEED_GAIN, FEED_BIAS, DOWN_BIAS, UP_BIAS, HIDDEN_GAIN, HIDDEN_BIAS, INNER = range(9)


def tables_of(positions, total_rows):
    pair_index = (jnp.arange(128) % 32).astype(f32)
    frequency = 1.0 / 10000.0 ** (pair_index / 32)
    angles = positions.astype(f32)[:, None] * frequency[None, :]
    ratios = (2.0 * pair_index + 0.4 * HEAD_DIM) / (1.4 * HEAD_DIM)
    exponent = (positions - total_rows // 2).astype(f32)[:, None] / scale_base
    return jnp.cos(angles), jnp.sin(angles), ratios[None, :] ** exponent


def back_tables(positions, total_rows, score_scale):
    lane = jnp.arange(128)
    cosine, sine, growth = tables_of(positions, total_rows)
    cosine = cosine * score_scale
    sine = sine * jnp.where(lane % 64 < 32, score_scale, -score_scale)[None]
    turned = (lane < 64)[None]
    factor = jnp.where(turned, 1.0 / growth, growth)
    return cosine * factor, sine * factor


def per_device(
    tokens,
    segment_kind,
    document,
    type_table,
    attend_gain,
    attend_bias,
    input_weight,
    input_bias,
    inner_gain,
    inner_bias,
    output_weight,
    output_bias,
    feed_gain,
    feed_bias,
    up_weight,
    up_bias,
    hidden_gain,
    hidden_bias,
    down_weight,
    down_bias,
    cotangent,
):
    local_rows = tokens.shape[0]
    total_rows = document.shape[0]
    local_width = input_weight.shape[2]
    score_scale = HEAD_DIM ** (-0.5)
    place = lax.axis_index("seq")
    part = lax.axis_index("ffn")
    y, z, x = place // 8, (place // 4) % 2, place % 4
    here = jnp.stack([x, y, z, part % 2, part, part, part, part]).astype(jnp.int32)
    query_pos = place * local_rows + jnp.arange(local_rows, dtype=jnp.int32)
    kind = segment_kind[None]

    stream, normed_low, *pieces = enter(
        here,
        tokens,
        kind,
        type_table,
        jnp.stack([attend_gain, attend_bias]),
        input_weight,
        input_bias,
        *tables_of(query_pos, total_rows),
    )
    received = shift_x(pieces)

    row_kv, row_q = rows(here, pieces[0], *received)
    kv_received = [lax.ppermute(row_kv, "seq", pairs) for pairs in Y_SHIFTS]
    queries_a = lax.ppermute(row_q, "seq", TO_SAME)
    queries_b = lax.ppermute(row_q, "seq", TO_OTHER)

    normed_row = gather_x(after(normed_low, row_kv))

    document = after(document, queries_a)
    begins = jnp.zeros((total_rows,), jnp.int32)
    for number in range(1, 4):
        begins = begins + jnp.where(
            document >= number, jnp.sum((document == number - 1).astype(jnp.int32)), 0
        )
    row_a = jnp.where(y % 2 == z, y, 7 - y)
    row_b = 7 - row_a
    begin_a = lax.dynamic_slice_in_dim(begins, row_a * ROW, ROW)
    begin_b = lax.dynamic_slice_in_dim(begins, row_b * ROW, ROW)
    begin = jnp.concatenate([begin_a, begin_b])[None]
    info = jnp.stack([z, row_a, row_b, begin_a[0], begin_b[0], begin_a[-1], begin_b[-1], y]).astype(
        jnp.int32
    )
    vec = jnp.concatenate(
        [
            v.astype(f32)
            for v in (
                attend_gain,
                output_bias,
                feed_gain,
                feed_bias,
                down_bias,
                up_bias,
                hidden_gain,
                hidden_bias,
                inner_gain,
                inner_bias,
            )
        ]
        + [jnp.zeros((16 * D - 8 * D - 512,), f32)]
    ).reshape(16, D)
    queries_a, queries_b, plane, vec, begin, info = lax.optimization_barrier(
        (queries_a, queries_b, [row_kv] + kv_received, vec, begin, info)
    )
    out_a, out_b, plane, queries = attend_forward(info, queries_a, queries_b, plane, begin)
    part_a = lax.ppermute(out_a, "seq", FROM_SAME)
    part_b = lax.ppermute(out_b, "seq", FROM_OTHER)
    mixed_row, logs_row, *pieces = combine(here, part_a, part_b)
    mixed, mine, theirs = inner(
        here, pieces[0], *shift_x(pieces), inner_gain[None], inner_bias[None], output_weight
    )
    chip = chip_stats(here, mine, core_swap(theirs))
    row_pos = (2 * y + z) * ROW + jnp.arange(ROW, dtype=jnp.int32)
    tables = back_tables(after(row_pos, chip), total_rows, score_scale)
    grad_hidden = jnp.einsum("td,fd->tf", after(cotangent, chip), down_weight, preferred_element_type=f32)
    total = join_stats(here, chip, far_swap(chip))
    total, tables, grad_hidden = lax.optimization_barrier((total, tables, grad_hidden))
    feed_low, inner_low, middle, before_act, inner_unit, inner_inv, sums, through = feed(
        here, total, core_swap(total), stream, vec, mixed, up_weight, grad_hidden
    )
    sums = sums + core_swap(sums)
    sums = sums + far_swap(sums)
    hidden_low, grad_pre, small_a, mine, theirs = hidden(
        here, sums, before_act, grad_hidden, vec, up_weight
    )
    chip = add_chip(here, mine, core_swap(theirs))
    total = add_far(here, chip, far_swap(chip))
    other = core_swap(total)
    grad_middle, small_b, *head_pieces, branch = middle_back(
        here,
        total,
        other,
        middle,
        stream,
        cotangent,
        vec,
        output_weight,
        inner_unit,
        inner_inv,
        through,
    )
    grad_pre, head_pieces = lax.optimization_barrier((grad_pre, head_pieces))
    head_received = shift_x(head_pieces)
    feed_parts = feed_grads(here, hidden_low, cotangent, grad_pre, feed_low, inner_low, branch, small_a, small_b)
    head_received, feed_parts, normed_row = lax.optimization_barrier((head_received, feed_parts, normed_row))
    feed_sums = lax.psum_scatter(feed_parts, "seq", scatter_dimension=0, axis_index_groups=X_GROUPS)
    message = grad_message(here, head_pieces[0], *head_received, mixed_row, logs_row)
    message_a = lax.ppermute(message, "seq", TO_SAME)
    message_b = lax.ppermute(message, "seq", TO_OTHER)
    weight_heads = head_weights(here, after(input_weight, message))
    message_a, message_b, weight_heads = lax.optimization_barrier((message_a, message_b, weight_heads))
    grad_qa, grad_qb, *kv_pieces = attend_backward(
        info, plane, queries, message_a, message_b, begin
    )
    kv_parts = shift_y(kv_pieces)
    q_parts = [lax.ppermute(grad_qa, "seq", FROM_SAME), lax.ppermute(grad_qb, "seq", FROM_OTHER)]
    feed_mine, feed_theirs = feed_out(here, after(hidden_low, kv_pieces[0]), down_weight)
    feed_chip = add_chip(here, feed_mine, core_swap(feed_theirs))
    feed_far = far_swap(feed_chip)
    kv_parts, q_parts, feed_chip = lax.optimization_barrier((kv_parts, q_parts, feed_chip))
    projected_row, projected_sums, *pieces = row_grads(here, kv_pieces[0], *kv_parts, *q_parts, *tables)
    back_received = shift_x(pieces)
    block_pieces = blocks(here, after(feed_sums, projected_row))
    block_received = shift_y(block_pieces)
    quarter_pieces = attend_quarter(here, normed_row, after(projected_row, block_pieces), projected_sums)
    block_received, back_received, quarter_pieces = lax.optimization_barrier(
        (block_received, back_received, quarter_pieces)
    )
    feed_pair = sum_z(pair(here, block_pieces[0], *block_received))
    quarter_received = shift_y(quarter_pieces)
    mine, theirs = normed_back(here, pieces[0], *back_received, weight_heads)
    mine, theirs, feed_pair = lax.optimization_barrier((mine, theirs, feed_pair))
    feed_shared = lax.all_gather(feed_pair, "seq", axis_index_groups=YX_GROUPS).reshape(4, 4, 592, 256)
    chip = add_chip(here, mine, core_swap(theirs))
    far, quarter_received = lax.optimization_barrier((far_swap(chip), quarter_received))
    total = add_far(here, chip, far)
    other = core_swap(total)
    attend_pair = sum_z(add_four(here, quarter_pieces[0], *quarter_received))
    grad_tokens, last = leave(here, total, other, stream, grad_middle, vec, kind)
    last, attend_pair = lax.optimization_barrier((last, attend_pair))
    attend_near = jnp.stack(ring(attend_pair, Y_SHIFTS))
    last = ring_sum(last, X_SWAP, X_SHIFTS[1])
    attend_near, last = lax.optimization_barrier((attend_near, last))
    attend_parts = ring(attend_near, X_SHIFTS)
    last = ring_sum(last, Y_SWAP, Y_SHIFTS[1])
    feed_chip, feed_far, last = lax.optimization_barrier((feed_chip, feed_far, last))
    last_other = lax.ppermute(last, "seq", Z_SWAP)
    total = add_far(here, feed_chip, feed_far)
    result = result_out(here, total, core_swap(total), middle, vec)
    grad_type_table, grad_attend_gain, grad_attend_bias = last_sum(here, last, last_other)
    grad_down_weight, grad_up_weight, grad_output_weight, *small = feed_weights_out(here, feed_shared)
    attend_parts, result, grad_type_table, grad_down_weight = lax.optimization_barrier(
        (attend_parts, result, grad_type_table, grad_down_weight)
    )
    grad_input_weight, grad_input_bias = attend_weights_out(here, *attend_parts)
    small = [v.reshape(v.shape[1]) for v in small]
    return (
        result,
        grad_tokens,
        grad_type_table,
        grad_attend_gain.reshape(D),
        grad_attend_bias.reshape(D),
        grad_input_weight,
        grad_input_bias,
        small[7],
        small[8],
        grad_output_weight,
        small[5],
        small[3],
        small[4],
        grad_up_weight,
        small[2],
        small[0],
        small[1],
        grad_down_weight,
        small[6],
    )


def solution(mesh):
    in_specs = (
        P("seq", None),
        P("seq"),
        P(),
        P(),
        P(),
        P(),
        P(None, None, "ffn"),
        P(None, "ffn"),
        P("ffn"),
        P("ffn"),
        P("ffn", None),
        P(),
        P(),
        P(),
        P(None, "ffn"),
        P("ffn"),
        P("ffn"),
        P("ffn"),
        P("ffn", None),
        P(),
        P("seq", None),
    )
    out_specs = (
        P("seq", None),
        P("seq", None),
        P(),
        P(),
        P(),
        P(None, None, "ffn"),
        P(None, "ffn"),
        P("ffn"),
        P("ffn"),
        P("ffn", None),
        P(),
        P(),
        P(),
        P(None, "ffn"),
        P("ffn"),
        P("ffn"),
        P("ffn"),
        P("ffn", None),
        P(),
    )
    return jax.shard_map(
        per_device, mesh=mesh, in_specs=in_specs, out_specs=out_specs, check_vma=False
    )
```
